128 devices in a mesh: sx: 16 (over z, x), sy: 8 (over y, core).
Axes of the slice: x: 4, y: 4, z: 4, core: 2. Of those that a mesh axis runs over, the one named last changes fastest.
Arguments:
- modes: bfloat16 [160, 80, 64, 3, 128], P('sx', 'sy'), may hold values from -0.44921875 to 0.44921875
- centre: float32 [128, 64, 128], P('sx', 'sy'), may hold values from -6 to 6
- coupling: float32 [128, 64, 128], P('sx', 'sy'), may hold values from 0.5 to 2
- volume: float32 [128, 64, 128], P('sx', 'sy'), may hold values from 0.25 to 1
Outputs:
- coarse_rows: float32 [8, 16, 64, 576], P('sy')
The draws below stay inside these ranges and needn't reach their ends.
All inputs are finite; a program needn't handle non-finite values.
Results may differ from the reference program's by a relative error of at most 0.0003.
Values may be sent and summed in bfloat16 or wider, within the bound.
No kernel may reach another device: no remote copies, remote signals or barrier semaphores. Data moves between devices by JAX's collectives and lax.ppermute only.
A program may use at most 192 MiB of HBM per device.

```python
import math
import jax
import jax.numpy as jnp
from jax import lax

K = 64
C = 8
CZ = 128
W = 1
EX = 10
NX = 128
NY = 64
N_SX = 16
N_SY = 8


def shard_levels(rng, shape, cuts, smallest, top_value):
    def one(dim, blocks):
        heights = jax.random.uniform(jax.random.fold_in(jax.random.fold_in(rng, 6), dim), (blocks,), jnp.float32, smallest / len(cuts), top_value / len(cuts))
        return jnp.repeat(jnp.exp(heights), shape[dim] // blocks).reshape((-1,) + (1,) * (len(shape) - dim - 1))

    level = one(*cuts[0])
    for cut in cuts[1:]:
        level = level * one(*cut)
    return level


def centred(stream_key, extent, deviation, limit, split=(), kind=jnp.bfloat16):
    gain = shard_levels(stream_key, extent, split, -0.22, 0.18) if split else 1.0
    values = jax.random.normal(stream_key, extent, jnp.float32) * deviation * gain
    return jnp.minimum(jnp.maximum(values, -limit), limit).astype(kind)


def setup_inputs(seed: int = 0) -> dict:
    key_of = jax.random.split(jax.random.key(seed), 5)
    modes = centred(key_of[0], (N_SX * EX, N_SY * EX, K, 3, CZ), 0.07, 0.44921875, ((0, 16), (1, 8)))
    centre = centred(key_of[1], (NX, NY, CZ), 1.0, 6.0, ((0, 16), (1, 8)), jnp.float32)
    coupling = jnp.clip(jnp.exp(math.log(2.0) - 1.3862944 * jax.random.uniform(key_of[2], (NX, NY, CZ), jnp.float32) ** shard_levels(key_of[2], (NX, NY, CZ), ((0, 16), (1, 8)), -0.2, 0.2)), 0.5, 2.0)
    volume = jnp.clip(jnp.exp(math.log(1.0) - 1.3862944 * jax.random.uniform(key_of[3], (NX, NY, CZ), jnp.float32) ** shard_levels(key_of[3], (NX, NY, CZ), ((0, 16), (1, 8)), -0.2, 0.2)), 0.25, 1.0)
    return dict(modes=modes, centre=centre, coupling=coupling, volume=volume)


def cover_weights(start_x, start_y, length, cell, count_x, count_y, margin):
    def counts(start, count):
        places = start + jnp.arange(length, dtype=jnp.int32)
        base = jnp.floor_divide(places, cell)
        total = jnp.zeros((length,), jnp.int32)
        for step_off in (-1, 0, 1):
            owner = base + step_off
            inside = (owner >= 0) & (owner < count) & (places >= owner * cell - margin) & (places < owner * cell + cell + margin)
            total = total + inside.astype(jnp.int32)
        in_grid = (places >= 0) & (places < cell * count)
        return jnp.where(in_grid, total, 0)
    both = counts(start_x, count_x)[:, None] * counts(start_y, count_y)[None, :]
    safe = jnp.maximum(both, 1).astype(jnp.float32)
    return jnp.where(both > 0, 1.0 / safe, 0.0).astype(jnp.float32)


def depth_shift(values, offset):
    if offset == 0:
        return values
    zero_slab = jnp.zeros(values.shape[:-1] + (1,), values.dtype)
    if offset > 0:
        return jnp.concatenate([values[..., 1:], zero_slab], axis=-1)
    return jnp.concatenate([zero_slab, values[..., :-1]], axis=-1)


def frame_image(basis_block, coef_frame):
    centre = coef_frame[:, :, 0][:, :, None, None, :]
    coupling = coef_frame[:, :, 1][:, :, None, None, :]
    volume = coef_frame[:, :, 2][:, :, None, None, :]
    values = basis_block.astype(jnp.float32)
    weighted = coupling[1:-1, 1:-1] * values
    padded = jnp.pad(weighted, ((2, 2), (2, 2), (0, 0), (0, 0), (0, 0)))
    framed = jnp.pad(values, ((1, 1), (1, 1), (0, 0), (0, 0), (0, 0)))
    size_x = framed.shape[0]
    size_y = framed.shape[1]
    spread = jnp.zeros(framed.shape, jnp.float32)
    for off_x in (-1, 0, 1):
        for off_y in (-1, 0, 1):
            slab = padded[1 + off_x:1 + off_x + size_x, 1 + off_y:1 + off_y + size_y]
            for off_z in (-1, 0, 1):
                if off_x == 0 and off_y == 0 and off_z == 0:
                    continue
                factor = 0.5 ** (abs(off_x) + abs(off_y) + abs(off_z) + 1)
                spread = spread + factor * depth_shift(slab, off_z)
    total = jnp.sum(framed, axis=3, keepdims=True)
    return centre * framed - coupling * spread + volume * (total - framed)


def pair_block(image, piece):
    return jnp.einsum("xykbz,xylbz->kl", image, piece.astype(jnp.float32), precision=lax.Precision.HIGHEST)


def gram_rows(basis, coef_frame, pieces):
    count_k = basis.shape[2]
    block = 16 if count_k % 16 == 0 else count_k

    def rows_for(start):
        image = frame_image(lax.dynamic_slice_in_dim(basis, start, block, 2), coef_frame)
        parts = [pair_block(image[place_x:place_x + piece.shape[0], place_y:place_y + piece.shape[1]], piece) for place_x, place_y, piece in pieces]
        return jnp.concatenate(parts, axis=1)

    stacked = lax.map(rows_for, jnp.arange(count_k // block, dtype=jnp.int32) * block)
    return stacked.reshape(count_k, stacked.shape[2])


def reference(modes, centre, coupling, volume):
    ext = C + 2 * W
    frame = ext + 2
    band = 2 * W + 1
    coef = jnp.stack([centre, coupling, volume], axis=2)
    coef_pad = jnp.pad(coef, ((W + 1, W + 1), (W + 1, W + 1), (0, 0), (0, 0)))
    modes_pad = jnp.pad(modes, ((ext, ext), (ext, ext), (0, 0), (0, 0), (0, 0)))
    spans = ((0, ext - band, band), (1, 0, ext), (C + 1, 0, band))

    def one(flat):
        index_x = flat // N_SY
        index_y = flat % N_SY
        zero = jnp.zeros((), jnp.int32)
        coef_frame = lax.dynamic_slice(coef_pad, (index_x * C, index_y * C, zero, zero), (frame, frame, 3, CZ))
        weights = cover_weights(index_x * C - W - 1, index_y * C - W - 1, frame, C, N_SX, N_SY, W)
        pieces = []
        for near_x in (-1, 0, 1):
            for near_y in (-1, 0, 1):
                raw = lax.dynamic_slice(modes_pad, ((index_x + near_x + 1) * ext, (index_y + near_y + 1) * ext, zero, zero, zero), (ext, ext, K, 3, CZ))
                place_x, from_x, long_x = spans[near_x + 1]
                place_y, from_y, long_y = spans[near_y + 1]
                piece = raw[from_x:from_x + long_x, from_y:from_y + long_y]
                share = weights[place_x:place_x + long_x, place_y:place_y + long_y]
                pieces.append((place_x, place_y, (share[:, :, None, None, None] * piece.astype(jnp.float32)).astype(jnp.bfloat16)))
        return gram_rows(pieces[4][2], coef_frame, pieces)

    rows = lax.map(one, jnp.arange(N_SX * N_SY, dtype=jnp.int32))
    rows = rows.reshape(N_SX, N_SY, K, 9 * K)
    return jnp.transpose(rows, (1, 0, 2, 3))
```

```python
import functools

import jax
import jax.numpy as jnp
from jax import lax
from jax.experimental import pallas as pl
from jax.experimental.pallas import tpu as pltpu
from jax.sharding import PartitionSpec as P

F32 = jnp.float32
BF16 = jnp.bfloat16
KAP, DIA, VOL, MID, LOW, UPP = range(6)
NT = (((1,), (1,)), ((), ()))
VMEM_LIMIT = 56 * 1024 * 1024


def cover(start, length, cell, count, margin):
    places = start + jnp.arange(length, dtype=jnp.int32)
    base = jnp.floor_divide(places, cell)
    total = jnp.zeros((length,), jnp.int32)
    for step_off in (-1, 0, 1):
        owner = base + step_off
        inside = (
            (owner >= 0)
            & (owner < count)
            & (places >= owner * cell - margin)
            & (places < owner * cell + cell + margin)
        )
        total = total + inside.astype(jnp.int32)
    in_grid = (places >= 0) & (places < cell * count)
    safe = jnp.maximum(total, 1).astype(F32)
    return jnp.where(in_grid & (total > 0), 1.0 / safe, 0.0)


def neighbours(count):
    up = [(i, i + 1) for i in range(count - 1)]
    return up, [(b, a) for a, b in up]


def with_halo(block, sides, width):
    for axis, dim in sides:
        up, down = neighbours(lax.axis_size(axis))
        low = lax.ppermute(
            lax.slice_in_dim(block, block.shape[dim] - width, None, axis=dim), axis, up
        )
        high = lax.ppermute(lax.slice_in_dim(block, 0, width, axis=dim), axis, down)
        block = jnp.concatenate([low, block, high], axis=dim)
    return block


def cell_rows(centre, coupling, volume, share_x, share_y):
    frame = with_halo(jnp.stack([centre, coupling, volume]), (("sx", 1), ("sy", 2)), 2)
    share = (share_x[:, None] * share_y[None, :])[:, :, None]
    kap = frame[1] * share
    vol = frame[2] * share * share
    dia = frame[0] * share * share - vol + 0.5 * kap * kap
    base = kap * (1.0 / 16.0)
    lane = lax.broadcasted_iota(jnp.int32, base.shape, 2)
    low = jnp.where(lane == 0, 0.0, base)
    upp = jnp.where(lane == base.shape[2] - 1, 0.0, base)
    none = jnp.zeros_like(base)
    return jnp.stack([kap, dia, vol, base + base, low, upp, none, none], axis=2)


def spread3(w):
    return [w[0], w[0] + w[0] + w[1], w[0] + w[1] + w[1] + w[2]]


def image_terms(lines, values, rows):
    out = []
    total = None
    if values is not None:
        total = rows[VOL] * (values[0] + values[1] + values[2])
    for a in range(3):
        r = lines[a]
        depth = rows[MID] * r + rows[LOW] * pltpu.roll(r, 1, 1) + rows[UPP] * pltpu.roll(r, 127, 1)
        out.append(-depth if values is None else rows[DIA] * values[a] + total - depth)
    return out


def put_image(img_ref, slot, pos, chunk, image):
    for a in range(3):
        high = image[a].astype(BF16)
        low = (image[a] - high.astype(F32)).astype(BF16)
        lanes = pl.ds((pos * 3 + a) * 128, 128)
        img_ref[slot, pl.ds(chunk * 16, 16), lanes] = high
        img_ref[slot, pl.ds(64 + chunk * 16, 16), lanes] = low


def cell_coefs(coef_ref, x, y, names):
    return {n: coef_ref[x, y, pl.ds(n, 1), :] for n in names}


def side(blocks):
    return jnp.concatenate(blocks, axis=1)


def fold(total):
    return total[:, :64] + total[:, 64:]


def fold_rows(total):
    return total[:64] + total[64:]


def own_kernel(m_hbm, coef_ref, out_ref, m_ref, q_ref, img_ref, acc_ref, sems):
    ext = m_ref.shape[0]
    copies = [pltpu.make_async_copy(m_hbm.at[x], m_ref.at[x], sems.at[x]) for x in range(ext)]
    for copy in copies:
        copy.start()
    zero = jnp.zeros(q_ref.shape[1:], F32)
    q_ref[0] = zero
    q_ref[ext + 1] = zero
    acc_ref[...] = jnp.zeros_like(acc_ref)

    def first(x, _):
        pltpu.make_async_copy(m_hbm.at[x], m_ref.at[x], sems.at[x]).wait()
        kaps = [coef_ref[x + 1, j + 1, pl.ds(KAP, 1), :] for j in range(ext)]
        for a in range(3):
            for chunk in range(4):
                rows = pl.ds(chunk * 16, 16)
                pair = None
                last = None
                for j in range(ext):
                    w = m_ref[x, j, a, rows, :].astype(F32) * kaps[j]
                    if j > 0:
                        now = last + w
                        q_ref[x + 1, j - 1, a, rows, :] = now + (last if pair is None else pair)
                        pair = now
                    last = w
                q_ref[x + 1, ext - 1, a, rows, :] = pair + last
        return 0

    lax.fori_loop(0, ext, first, 0)

    def second(x, _):
        total = acc_ref[...]
        for j in range(ext):
            rows_of = cell_coefs(coef_ref, x + 1, j + 1, (DIA, VOL, MID, LOW, UPP))
            for chunk in range(4):
                rows = pl.ds(chunk * 16, 16)
                values = [m_ref[x, j, a, rows, :].astype(F32) for a in range(3)]
                lines = []
                for a in range(3):
                    mid = q_ref[x + 1, j, a, rows, :]
                    lines.append(
                        (q_ref[x, j, a, rows, :] + mid) + (mid + q_ref[x + 2, j, a, rows, :])
                    )
                put_image(img_ref, j // 2, j % 2, chunk, image_terms(lines, values, rows_of))
            if j % 2 == 1:
                left = side([m_ref[x, i, a] for i in (j - 1, j) for a in range(3)])
                total = total + lax.dot_general(
                    left, img_ref[j // 2], NT, preferred_element_type=F32
                )
        acc_ref[...] = total
        return 0

    lax.fori_loop(0, ext, second, 0)
    out_ref[...] = fold(acc_ref[...])


def rows_kernel(m_hbm, south_hbm, north_hbm, coef_ref, out_ref, d_ref, r_ref, q_ref, img_ref, acc_ref, sems):
    ext = m_hbm.shape[0]
    copies = [
        pltpu.make_async_copy(south_hbm, r_ref.at[0], sems.at[0]),
        pltpu.make_async_copy(north_hbm, r_ref.at[1], sems.at[1]),
        pltpu.make_async_copy(m_hbm.at[:, pl.ds(0, 3)], d_ref.at[0], sems.at[2]),
        pltpu.make_async_copy(m_hbm.at[:, pl.ds(ext - 3, 3)], d_ref.at[1], sems.at[3]),
    ]
    for copy in copies:
        copy.start()
    q_ref[...] = jnp.zeros_like(q_ref)
    acc_ref[...] = jnp.zeros_like(acc_ref)
    for copy in copies:
        copy.wait()
    raw_at = ((2, 1, 0), (0, 1, 2))
    raw_coef = ((2, 1, 0), (9, 10, 11))
    img_coef = ((3, 2, 1), (8, 9, 10))
    own_at = ((2, 1, 0), (0, 1, 2))
    for s in range(2):

        def first(x, _, s=s):
            kaps = [coef_ref[x + 1, raw_coef[s][d], pl.ds(KAP, 1), :] for d in range(3)]
            for a in range(3):
                for chunk in range(4):
                    rows = pl.ds(chunk * 16, 16)
                    w = [r_ref[s, x, raw_at[s][d], a, rows, :].astype(F32) * kaps[d] for d in range(3)]
                    for e, value in enumerate(spread3(w)):
                        q_ref[x + 1, e, a, rows, :] = value
            return 0

        lax.fori_loop(0, ext, first, 0)

        def second(x, _, s=s):
            for e in range(3):
                rows_of = cell_coefs(coef_ref, x + 1, img_coef[s][e], (DIA, VOL, MID, LOW, UPP))
                for chunk in range(4):
                    rows = pl.ds(chunk * 16, 16)
                    values = None
                    if e > 0:
                        values = [r_ref[s, x, raw_at[s][e - 1], a, rows, :].astype(F32) for a in range(3)]
                    lines = []
                    for a in range(3):
                        mid = q_ref[x + 1, e, a, rows, :]
                        lines.append(
                            (q_ref[x, e, a, rows, :] + mid) + (mid + q_ref[x + 2, e, a, rows, :])
                        )
                    put_image(img_ref, 0, e, chunk, image_terms(lines, values, rows_of))
            left = side([d_ref[s, x, own_at[s][e], a] for e in range(3) for a in range(3)])
            acc_ref[s] += lax.dot_general(left, img_ref[0], NT, preferred_element_type=F32)
            return 0

        lax.fori_loop(0, ext, second, 0)
    out_ref[...] = side([fold(acc_ref[0]), fold(acc_ref[1])])


def columns_kernel(
    odd_ref, m_hbm, south_hbm, north_hbm, main_hbm, corner_hbm, coef_ref, own_ref, rows_ref, out_ref,
    d_ref, s_ref, n_ref, x_ref, y_ref, q_ref, img_ref, acc_ref, cor_ref, sems,
):
    ext = m_hbm.shape[0]
    odd = odd_ref[0]
    start = jnp.where(odd == 1, 0, ext - 3)
    copies = [
        pltpu.make_async_copy(m_hbm.at[pl.ds(start, 3)], d_ref.at[:, pl.ds(1, ext)], sems.at[0]),
        pltpu.make_async_copy(south_hbm, s_ref, sems.at[1]),
        pltpu.make_async_copy(north_hbm, n_ref, sems.at[2]),
        pltpu.make_async_copy(main_hbm, x_ref.at[:, pl.ds(1, ext)], sems.at[3]),
        pltpu.make_async_copy(corner_hbm, y_ref, sems.at[4]),
    ]
    for copy in copies:
        copy.start()
    none = jnp.zeros((3, 3, 64, 128), BF16)
    for edge in (0, ext + 1):
        d_ref[:, edge] = none
        x_ref[:, edge] = none
    q_ref[...] = jnp.zeros_like(q_ref)
    acc_ref[...] = jnp.zeros_like(acc_ref)
    cor_ref[...] = jnp.zeros_like(cor_ref)
    for copy in copies:
        copy.wait()

    def pick(high, low):
        return jnp.where(odd == 1, low, high)

    names = (DIA, VOL, MID, LOW, UPP)
    xi = [pick(d, 2 - d) for d in range(3)]
    xc = [pick(9 + d, 2 - d) for d in range(3)]
    xe = [pick(8 + e, 3 - e) for e in range(3)]
    xn = [pick(7 + e, 2 - e) for e in range(3)]
    yn = [pick(2 - e, 7 + e) for e in range(3)]
    yi = [pick(2 - d, d) for d in range(3)]
    yc = [pick(2 - d, 9 + d) for d in range(3)]
    ye = [pick(3 - e, 8 + e) for e in range(3)]

    def main_first(y, _):
        kaps = [coef_ref[xc[d], y + 1, pl.ds(KAP, 1), :] for d in range(3)]
        for a in range(3):
            for chunk in range(4):
                rows = pl.ds(chunk * 16, 16)
                w = [x_ref[xi[d], y + 1, a, rows, :].astype(F32) * kaps[d] for d in range(3)]
                for e, value in enumerate(spread3(w)):
                    q_ref[y + 2, e, a, rows, :] = value
        return 0

    lax.fori_loop(0, ext, main_first, 0)

    def main_second(f, corner, other):
        for e in range(3):
            rows_of = cell_coefs(coef_ref, xe[e], f, names)
            for chunk in range(4):
                rows = pl.ds(chunk * 16, 16)
                values = None
                if e > 0:
                    values = [x_ref[xi[e - 1], f, a, rows, :].astype(F32) for a in range(3)]
                lines = []
                for a in range(3):
                    mid = q_ref[f + 1, e, a, rows, :]
                    lines.append((q_ref[f, e, a, rows, :] + mid) + (mid + q_ref[f + 2, e, a, rows, :]))
                put_image(img_ref, 0, e, chunk, image_terms(lines, values, rows_of))
        left = side([d_ref[xi[e], f, a] for e in range(3) for a in range(3)])
        acc_ref[...] += lax.dot_general(left, img_ref[0], NT, preferred_element_type=F32)
        if corner is not None:
            right = side([other(e)[a] for e in range(3) for a in range(3)])
            cor_ref[corner] += lax.dot_general(img_ref[0], right, NT, preferred_element_type=F32)

    def loop(lo, hi, corner, other):
        def body(f, _):
            main_second(f, corner, None if other is None else lambda e: other(e, f))
            return 0

        lax.fori_loop(lo, hi, body, 0)

    loop(0, 3, 0, lambda e, f: [s_ref[xn[e], f, a] for a in range(3)])
    loop(3, 9, None, None)
    loop(9, 12, 1, lambda e, f: [n_ref[xn[e], f - 9, a] for a in range(3)])

    for s, ref in ((0, s_ref), (1, n_ref)):
        raw_y = (0, 1, 2) if s == 0 else (5, 4, 3)
        raw_f = (1, 2, 3) if s == 0 else (10, 9, 8)
        img_f = (0, 1, 2) if s == 0 else (11, 10, 9)
        img_y = (0, 1, 2) if s == 0 else (2, 1, 0)
        for t in range(3):
            kaps = [coef_ref[yc[d], raw_f[t], pl.ds(KAP, 1), :] for d in range(3)]
            for a in range(3):
                for chunk in range(4):
                    rows = pl.ds(chunk * 16, 16)
                    w = [y_ref[yi[d], raw_y[t], a, rows, :].astype(F32) * kaps[d] for d in range(3)]
                    for e, value in enumerate(spread3(w)):
                        q_ref[t, e, a, rows, :] = value
        for u in range(3):
            for e in range(3):
                rows_of = cell_coefs(coef_ref, ye[e], img_f[u], names)
                for chunk in range(4):
                    rows = pl.ds(chunk * 16, 16)
                    values = None
                    if e > 0 and u > 0:
                        values = [
                            y_ref[yi[e - 1], raw_y[u - 1], a, rows, :].astype(F32) for a in range(3)
                        ]
                    lines = []
                    for a in range(3):
                        q = [q_ref[t, e, a, rows, :] for t in range(u + 1)]
                        if u == 0:
                            lines.append(q[0])
                        elif u == 1:
                            lines.append(q[0] + q[0] + q[1])
                        else:
                            lines.append(q[0] + q[1] + q[1] + q[2])
                    put_image(img_ref, 0, e, chunk, image_terms(lines, values, rows_of))
            right = side([ref[yn[e], img_y[u], a] for e in range(3) for a in range(3)])
            cor_ref[2 + s] += lax.dot_general(img_ref[0], right, NT, preferred_element_type=F32)

    corner = [fold_rows(cor_ref[i]) for i in range(4)]
    east = [jnp.where(odd == 1, corner[2 + s], corner[s]) for s in range(2)]
    west = [jnp.where(odd == 1, corner[s], corner[2 + s]) for s in range(2)]
    around = rows_ref[...]
    out_ref[...] = side(
        [
            east[0], fold(acc_ref[...]), east[1], around[:, :64],
            own_ref[...], around[:, 64:], west[0], west[1],
        ]
    )


def final_kernel(odd_ref, slot_ref, *refs):
    *pieces, out_hbm, g_ref, o_ref, sems, out_sem = refs
    count = len(pieces) // 2
    copies = []
    for h in range(2):
        for i in range(count):
            ref = pieces[h * count + i]
            for j in range(4):
                at = h * 16 + i * 4 + j
                copies.append(
                    pltpu.make_async_copy(
                        ref.at[j], g_ref.at[slot_ref[at] + 1, pl.ds(h * 32, 32)], sems.at[at]
                    )
                )
    for copy in copies:
        copy.start()
    odd = odd_ref[0]
    none = jnp.zeros(g_ref.shape[1:], F32)
    g_ref[0] = none
    g_ref[17] = none
    for copy in copies:
        copy.wait()

    def body(p, _):
        before = g_ref.at[p]
        here = g_ref.at[p + 1]
        after = g_ref.at[p + 2]
        turned_from = jnp.where(odd == 1, p + 2, p)
        turned = jnp.transpose(g_ref[turned_from, :, pl.ds(0, 128)])[64:]
        own = here[:, pl.ds(64, 64)]
        left = jnp.where(odd == 1, own, turned)
        right = jnp.where(odd == 1, turned, own)
        o_ref[p] = jnp.concatenate(
            [
                before[:, pl.ds(0, 64)], left, before[:, pl.ds(128, 64)], here[:, pl.ds(192, 192)],
                after[:, pl.ds(384, 64)], right, after[:, pl.ds(448, 64)],
            ],
            axis=1,
        )
        return 0

    lax.fori_loop(0, 16, body, 0)
    done = pltpu.make_async_copy(o_ref, out_hbm, out_sem)
    done.start()
    done.wait()


def any_spec():
    return pl.BlockSpec(memory_space=pl.ANY)


def vmem_spec():
    return pl.BlockSpec(memory_space=pltpu.VMEM)


def smem_spec():
    return pl.BlockSpec(memory_space=pltpu.SMEM)


def call(kernel, out_shape, in_specs, out_spec, scratch, flops, name):
    return pl.pallas_call(
        kernel,
        out_shape=out_shape,
        in_specs=in_specs,
        out_specs=out_spec,
        scratch_shapes=scratch,
        compiler_params=pltpu.CompilerParams(vmem_limit_bytes=VMEM_LIMIT),
        cost_estimate=pl.CostEstimate(flops=flops, bytes_accessed=5_000_000, transcendentals=0),
        name=name,
    )


def ring(value, pairs):
    return [value] + [lax.ppermute(value, "sx", pairs(k)) for k in (1, 2, 3)]


def gathered(rows, nz, nx):
    def along_z(k):
        return [(z * nx + x, (z + k) % nz * nx + x) for z in range(nz) for x in range(nx)]

    def along_x(k):
        return [(z * nx + x, z * nx + (x + k) % nx) for z in range(nz) for x in range(nx)]

    half = rows.shape[0] // 2
    part = [rows[:half], rows[half:]]
    first = [jnp.stack(ring(part[0], along_z)), jnp.stack(ring(part[1], along_x))]
    return ring(first[0], along_x), ring(first[1], along_z)


def local(modes, centre, coupling, volume):
    ext = modes.shape[0]
    cell = centre.shape[0]
    margin = (ext - cell) // 2
    nx = lax.axis_size("sx")
    ny = lax.axis_size("sy")
    ix = lax.axis_index("sx")
    iy = lax.axis_index("sy")
    odd = lax.rem(iy, 2)
    share_x = cover(ix * cell - margin - 1, ext + 2, cell, nx, margin)
    share_y = cover(iy * cell - margin - 1, ext + 2, cell, ny, margin)
    coef = cell_rows(centre, coupling, volume, share_x, share_y)

    m = jnp.transpose(modes, (0, 1, 3, 2, 4))

    def flat(x, y):
        return x * ny + y

    main_pairs, other_pairs = [], []
    for y in range(ny):
        for x in range(nx - 1):
            lo, hi = flat(x, y), flat(x + 1, y)
            main_pairs.append((hi, lo) if y % 2 == 0 else (lo, hi))
            other_pairs.append((lo, hi) if y % 2 == 0 else (hi, lo))
    main_start = jnp.where(odd == 1, ext - 3, 0)
    corner_start = jnp.where(odd == 1, 0, ext - 3)
    main = lax.ppermute(lax.dynamic_slice_in_dim(m, main_start, 3, 0), ("sx", "sy"), main_pairs)
    edge = lax.dynamic_slice_in_dim(m, corner_start, 3, 0)
    edge = jnp.concatenate([edge[:, :3], edge[:, ext - 3 :]], axis=1)
    corner = lax.ppermute(edge, ("sx", "sy"), other_pairs)
    up, down = neighbours(ny)
    south = lax.ppermute(m[:, ext - 3 :], "sy", up)
    north = lax.ppermute(m[:, :3], "sy", down)

    odd1 = odd.astype(jnp.int32).reshape(1)
    own = call(
        own_kernel,
        jax.ShapeDtypeStruct((64, 64), F32),
        [any_spec(), vmem_spec()],
        vmem_spec(),
        [
            pltpu.VMEM((ext, ext, 3, 64, 128), BF16),
            pltpu.VMEM((ext + 2, ext, 3, 64, 128), F32),
            pltpu.VMEM((ext // 2, 128, 768), BF16),
            pltpu.VMEM((64, 128), F32),
            pltpu.SemaphoreType.DMA((ext,)),
        ],
        4_000_000_000,
        "own_gram",
    )(m, coef)
    around = call(
        rows_kernel,
        jax.ShapeDtypeStruct((64, 128), F32),
        [any_spec(), any_spec(), any_spec(), vmem_spec()],
        vmem_spec(),
        [
            pltpu.VMEM((2, ext, 3, 3, 64, 128), BF16),
            pltpu.VMEM((2, ext, 3, 3, 64, 128), BF16),
            pltpu.VMEM((ext + 2, 3, 3, 64, 128), F32),
            pltpu.VMEM((1, 128, 1152), BF16),
            pltpu.VMEM((2, 64, 128), F32),
            pltpu.SemaphoreType.DMA((4,)),
        ],
        2_000_000_000,
        "row_gram",
    )(m, south, north, coef)
    rows = call(
        columns_kernel,
        jax.ShapeDtypeStruct((64, 512), F32),
        [smem_spec()] + [any_spec()] * 5 + [vmem_spec()] * 3,
        vmem_spec(),
        [
            pltpu.VMEM((3, ext + 2, 3, 64, 128), BF16),
            pltpu.VMEM((ext, 3, 3, 64, 128), BF16),
            pltpu.VMEM((ext, 3, 3, 64, 128), BF16),
            pltpu.VMEM((3, ext + 2, 3, 64, 128), BF16),
            pltpu.VMEM((3, 6, 3, 64, 128), BF16),
            pltpu.VMEM((ext + 4, 3, 3, 64, 128), F32),
            pltpu.VMEM((1, 128, 1152), BF16),
            pltpu.VMEM((64, 128), F32),
            pltpu.VMEM((4, 128, 64), F32),
            pltpu.SemaphoreType.DMA((5,)),
        ],
        2_000_000_000,
        "column_gram",
    )(odd1, m, south, north, main, corner, coef, own, around)

    nz, nw = 4, nx // 4
    first, second = gathered(rows, nz, nw)
    iz, iw = ix // nw, lax.rem(ix, nw)
    slots = []
    for i in range(4):
        for j in range(4):
            slots.append(lax.rem(iz - j + nz, nz) * nw + lax.rem(iw - i + nw, nw))
    for i in range(4):
        for j in range(4):
            slots.append(lax.rem(iz - i + nz, nz) * nw + lax.rem(iw - j + nw, nw))
    slot = jnp.stack(slots).astype(jnp.int32)
    pieces = first + second
    out = call(
        final_kernel,
        jax.ShapeDtypeStruct((nx, 64, 576), F32),
        [smem_spec(), smem_spec()] + [any_spec()] * len(pieces),
        any_spec(),
        [
            pltpu.VMEM((nx + 2, 64, 512), F32),
            pltpu.VMEM((nx, 64, 576), F32),
            pltpu.SemaphoreType.DMA((32,)),
            pltpu.SemaphoreType.DMA,
        ],
        1_000_000,
        "assemble",
    )(odd1, slot, *pieces)
    return out[None]


def solution(mesh):
    in_specs = (
        P("sx", "sy", None, None, None),
        P("sx", "sy", None),
        P("sx", "sy", None),
        P("sx", "sy", None),
    )
    out_specs = P("sy", None, None, None)
    return jax.shard_map(local, mesh=mesh, in_specs=in_specs, out_specs=out_specs, check_vma=False)
```

```python
import functools

import jax
import jax.numpy as jnp
from jax import lax
from jax.experimental import pallas as pl
from jax.experimental.pallas import tpu as pltpu
from jax.sharding import PartitionSpec as P

F32 = jnp.float32
BF16 = jnp.bfloat16
MID, LOW, UPP, DIA, VOL, OUT = range(6)
NT = (((1,), (1,)), ((), ()))
MIB = 1024 * 1024


def cover(start, length, cell, count, margin):
    places = start + jnp.arange(length, dtype=jnp.int32)
    base = jnp.floor_divide(places, cell)
    total = jnp.zeros((length,), jnp.int32)
    for step_off in (-1, 0, 1):
        owner = base + step_off
        inside = (
            (owner >= 0)
            & (owner < count)
            & (places >= owner * cell - margin)
            & (places < owner * cell + cell + margin)
        )
        total = total + inside.astype(jnp.int32)
    in_grid = (places >= 0) & (places < cell * count)
    safe = jnp.maximum(total, 1).astype(F32)
    return jnp.where(in_grid & (total > 0), 1.0 / safe, 0.0)


def neighbours(count):
    up = [(i, i + 1) for i in range(count - 1)]
    return up, [(b, a) for a, b in up]


def spread3(w):
    return [w[0], w[0] + w[0] + w[1], w[0] + w[1] + w[1] + w[2]]


def put_image(img_ref, slot, pos, chunk, image):
    for a in range(3):
        high = image[a].astype(BF16)
        low = (image[a] - high.astype(F32)).astype(BF16)
        lanes = pl.ds((pos * 3 + a) * 128, 128)
        img_ref[slot, pl.ds(chunk * 16, 16), lanes] = high
        img_ref[slot, pl.ds(64 + chunk * 16, 16), lanes] = low


def cell_image(lines, values, rows):
    if values is None:
        return [-(rows[2] * lines[a]) for a in range(3)]
    total = rows[1] * (values[0] + values[1] + values[2])
    return [rows[0] * values[a] + total - rows[2] * lines[a] for a in range(3)]


def coef_rows(coef_ref, x, y, names):
    return [coef_ref[x, n, pl.ds(y, 1), :] for n in names]


def depth_sum(raw, rows):
    return (
        raw.astype(F32) * rows[0]
        + pltpu.roll(raw, 1, 1).astype(F32) * rows[1]
        + pltpu.roll(raw, 127, 1).astype(F32) * rows[2]
    )


def side(blocks):
    return jnp.concatenate(blocks, axis=1)


def fold(total):
    return total[:, :64] + total[:, 64:]


def fold_rows(total):
    return total[:64] + total[64:]


def pack_kernel(odd_ref, m_hbm, main_ref, corner_ref, south_ref, north_ref, sems):
    ext = m_hbm.shape[0]
    odd = odd_ref[0]
    here = jnp.where(odd == 1, ext - 3, 0)
    there = jnp.where(odd == 1, 0, ext - 3)
    copies = [
        pltpu.make_async_copy(m_hbm.at[pl.ds(here, 3)], main_ref, sems.at[0]),
        pltpu.make_async_copy(
            m_hbm.at[pl.ds(there, 3), pl.ds(0, 3)], corner_ref.at[:, pl.ds(0, 3)], sems.at[1]
        ),
        pltpu.make_async_copy(
            m_hbm.at[pl.ds(there, 3), pl.ds(ext - 3, 3)], corner_ref.at[:, pl.ds(3, 3)], sems.at[2]
        ),
        pltpu.make_async_copy(m_hbm.at[:, pl.ds(ext - 3, 3)], south_ref, sems.at[3]),
        pltpu.make_async_copy(m_hbm.at[:, pl.ds(0, 3)], north_ref, sems.at[4]),
    ]
    for copy in copies:
        copy.start()
    for copy in copies:
        copy.wait()


def gate_kernel(*refs):
    pass


def own_kernel(
    odd_ref, sx_ref, sy_ref, m_hbm, mid_ref, lo_ref, hi_ref,
    out_ref, coef_ref, simg_hbm, nimg_hbm, ximg_hbm,
    m_ref, q_ref, img_ref, acc_ref, sems, strip_sems,
):
    ext = m_hbm.shape[0]
    frame = ext + 2
    odd = odd_ref[0]

    def load(x):
        return pltpu.make_async_copy(m_hbm.at[x], m_ref.at[x + 1], sems.at[x])

    for x in range(ext):
        load(x).start()
    none = jnp.zeros(m_ref.shape[1:], BF16)
    for edge in (0, ext + 1, ext + 2):
        m_ref[edge] = none
    zero = jnp.zeros(q_ref.shape[1:], F32)
    q_ref[0] = zero
    q_ref[1] = zero
    acc_ref[...] = jnp.zeros_like(acc_ref)

    lane = lax.broadcasted_iota(jnp.int32, (frame, 128), 1)
    place = lax.broadcasted_iota(jnp.int32, (frame, 128), 0)
    share_y = jnp.zeros((frame, 128), F32)
    for g in range(frame):
        share_y = jnp.where(place == g, sy_ref[g], share_y)

    def coefs(f, _):
        share = share_y * sx_ref[f]
        cen, cpl, vol = [
            jnp.concatenate([lo_ref[f, n], mid_ref[f, n], hi_ref[f, n]], axis=0) for n in range(3)
        ]
        kap = cpl * share
        vol = vol * share * share
        coef_ref[f, MID] = kap + kap
        coef_ref[f, LOW] = jnp.where(lane == 0, 0.0, pltpu.roll(kap, 1, 1))
        coef_ref[f, UPP] = jnp.where(lane == 127, 0.0, pltpu.roll(kap, 127, 1))
        coef_ref[f, DIA] = cen * share * share - vol + 0.5 * kap * kap
        coef_ref[f, VOL] = vol
        coef_ref[f, OUT] = kap * (1.0 / 16.0)
        return 0

    lax.fori_loop(0, frame, coefs, 0)

    def strips(f):
        return [
            pltpu.make_async_copy(
                img_ref.at[f, :, pl.ds(0, 1152)], simg_hbm.at[f - 1], strip_sems.at[0, f - 1]
            ),
            pltpu.make_async_copy(
                img_ref.at[f, :, pl.ds((frame - 3) * 384, 1152)], nimg_hbm.at[f - 1], strip_sems.at[1, f - 1]
            ),
        ]

    first_x = jnp.where(odd == 1, 0, frame - 3)

    def strip_x(f):
        return pltpu.make_async_copy(
            img_ref.at[f, :, pl.ds(384, ext * 384)], ximg_hbm.at[f - first_x], strip_sems.at[2, f - first_x]
        )

    def line(f, last, edge):
        if not last:
            kaps = [coef_rows(coef_ref, f + 1, g, (MID, LOW, UPP)) for g in range(1, ext + 1)]
            for a in range(3):
                for chunk in range(4):
                    rows = pl.ds(chunk * 16, 16)
                    pair = None
                    before = None
                    for j in range(ext):
                        w = depth_sum(m_ref[f + 1, j, a, rows, :], kaps[j])
                        if j == 0:
                            q_ref[f + 2, 0, a, rows, :] = w
                            pair = w
                        else:
                            now = before + w
                            q_ref[f + 2, j, a, rows, :] = now + pair
                            pair = now
                        before = w
                    q_ref[f + 2, ext, a, rows, :] = pair + before
                    q_ref[f + 2, ext + 1, a, rows, :] = before
        total = acc_ref[...]
        for g in range(frame):
            rows_of = coef_rows(coef_ref, f, g, (DIA, VOL, OUT))
            for chunk in range(4):
                rows = pl.ds(chunk * 16, 16)
                values = None
                if 1 <= g <= ext and not edge:
                    values = [m_ref[f, g - 1, a, rows, :].astype(F32) for a in range(3)]
                lines = []
                for a in range(3):
                    mid = q_ref[f + 1, g, a, rows, :]
                    if last:
                        lines.append(q_ref[f, g, a, rows, :])
                    else:
                        lines.append(
                            (q_ref[f, g, a, rows, :] + mid) + (mid + q_ref[f + 2, g, a, rows, :])
                        )
                put_image(img_ref, f, g, chunk, cell_image(lines, values, rows_of))
            if g % 2 == 0 and 1 < g <= ext and not edge:
                left = side([m_ref[f, i, a] for i in (g - 2, g - 1) for a in range(3)])
                total = total + lax.dot_general(
                    left, img_ref[f, :, pl.ds((g - 1) * 384, 768)], NT, preferred_element_type=F32
                )
        acc_ref[...] = total

        @pl.when((f >= first_x) & (f < first_x + 3))
        def _():
            strip_x(f).start()

        if not edge:
            for copy in strips(f):
                copy.start()

    load(0).wait()
    line(0, False, True)

    def body(f, _):
        @pl.when(f < ext)
        def _():
            load(f).wait()

        line(f, False, False)
        return 0

    lax.fori_loop(1, ext + 1, body, 0)
    line(ext + 1, True, True)
    out_ref[...] = fold(acc_ref[...])
    for f in range(1, ext + 1):
        for copy in strips(f):
            copy.wait()
    for i in range(3):
        strip_x(first_x + i).wait()


def rows_kernel(
    south_ref, north_ref, simg_hbm, nimg_hbm, coef_ref, out_ref, cimg_ref,
    img_ref, z_ref, acc_ref, sems,
):
    ext = south_ref.shape[0]
    raw_refs = (south_ref, north_ref)
    images = [
        pltpu.make_async_copy(ref, img_ref.at[s], sems.at[s])
        for s, ref in enumerate((simg_hbm, nimg_hbm))
    ]
    for copy in images:
        copy.start()
    acc_ref[...] = jnp.zeros_like(acc_ref)
    for s in range(2):
        r_ref = raw_refs[s]
        raw_y = (2, 1, 0) if s == 0 else (0, 1, 2)
        raw_g = (2, 1, 0) if s == 0 else (9, 10, 11)
        img_g = (3, 2, 1) if s == 0 else (8, 9, 10)
        img_y = (2, 1, 0) if s == 0 else (0, 1, 2)
        for t in range(2):
            raw_x = (0, 1, 2) if t == 0 else (9, 8, 7)
            raw_f = (1, 2, 3) if t == 0 else (10, 9, 8)
            img_f = (0, 1, 2) if t == 0 else (11, 10, 9)
            img_x = (0, 1, 2) if t == 0 else (2, 1, 0)

            def chunked(chunk, _, s=s, t=t, r_ref=r_ref, raw_x=raw_x, raw_f=raw_f, img_f=img_f, img_x=img_x):
                rows = pl.ds(pl.multiple_of(chunk * 16, 16), 16)
                low_rows = pl.ds(pl.multiple_of(64 + chunk * 16, 16), 16)
                for a in range(3):
                    across = []
                    for c in range(3):
                        w = [
                            depth_sum(
                                r_ref[raw_x[c], raw_y[d], a, rows, :],
                                coef_rows(coef_ref, raw_f[c], raw_g[d], (MID, LOW, UPP)),
                            )
                            for d in range(3)
                        ]
                        across.append(spread3(w))
                    for e in range(3):
                        for c, value in enumerate(spread3([across[i][e] for i in range(3)])):
                            z_ref[c, e, a] = value
                for c in range(3):
                    for e in range(3):
                        values = None
                        if c > 0 and e > 0:
                            values = [
                                r_ref[raw_x[c - 1], raw_y[e - 1], a, rows, :].astype(F32)
                                for a in range(3)
                            ]
                        image = cell_image(
                            [z_ref[c, e, a] for a in range(3)], values,
                            coef_rows(coef_ref, img_f[c], img_g[e], (DIA, VOL, OUT)),
                        )
                        for a in range(3):
                            high = image[a].astype(BF16)
                            low = (image[a] - high.astype(F32)).astype(BF16)
                            lanes = pl.ds(((img_x[c] * 3 + img_y[e]) * 3 + a) * 128, 128)
                            cimg_ref[t, s, rows, lanes] = high
                            cimg_ref[t, s, low_rows, lanes] = low
                return 0

            lax.fori_loop(0, 4, chunked, 0)
    for s in range(2):
        images[s].wait()

        def dots(x, _, s=s):
            right = side([raw_refs[s][x, j, a] for j in range(3) for a in range(3)])
            acc_ref[s] += lax.dot_general(img_ref[s, x], right, NT, preferred_element_type=F32)
            return 0

        lax.fori_loop(0, ext, dots, 0)
    out_ref[...] = side([fold_rows(acc_ref[0]), fold_rows(acc_ref[1])])


def corner_dot(raw, img):
    left = side([raw(i, j, a) for i in range(3) for j in range(3) for a in range(3)])
    return fold(lax.dot_general(left, img, NT, preferred_element_type=F32))


def other_kernel(odd_ref, corner_ref, cimg_ref, own_ref, rows_ref, out_ref, keep_ref):
    t = odd_ref[0]
    south = corner_dot(lambda i, j, a: corner_ref[i, j, a], cimg_ref[t, 0])
    north = corner_dot(lambda i, j, a: corner_ref[i, j + 3, a], cimg_ref[t, 1])
    around = rows_ref[...]
    out_ref[...] = side([own_ref[...], around[:, 64:], south, around[:, :64]])
    keep_ref[...] = north


def main_kernel(odd_ref, main_ref, ximg_ref, cimg_ref, keep_ref, out_ref):
    t = 1 - odd_ref[0]
    ext = main_ref.shape[1]
    total = None
    for i in range(3):
        right = side([main_ref[i, j, a] for j in range(ext) for a in range(3)])
        part = lax.dot_general(ximg_ref[i], right, NT, preferred_element_type=F32)
        total = part if total is None else total + part
    south = corner_dot(lambda i, j, a: main_ref[i, j, a], cimg_ref[t, 0])
    north = corner_dot(lambda i, j, a: main_ref[i, ext - 3 + j, a], cimg_ref[t, 1])
    out_ref[...] = side([south, fold_rows(total), north, keep_ref[...]])


def final_kernel(odd_ref, slot_ref, *refs):
    *pieces, out_hbm, e_ref, l_ref, o_ref, sems, out_sems = refs
    copies = []
    for h, ref in enumerate((e_ref, l_ref)):
        for i in range(4):
            for j in range(4):
                at = h * 16 + i * 4 + j
                copies.append(
                    pltpu.make_async_copy(
                        pieces[h * 4 + i].at[j], ref.at[slot_ref[at] + 1], sems.at[at]
                    )
                )
    for copy in copies:
        copy.start()
    odd = odd_ref[0]
    none = jnp.zeros(e_ref.shape[1:], F32)
    for ref in (e_ref, l_ref):
        ref[0] = none
        ref[17] = none
    for copy in copies:
        copy.wait()

    def put(p):
        return pltpu.make_async_copy(o_ref.at[p], out_hbm.at[p], out_sems.at[p])

    low = lax.broadcasted_iota(jnp.int32, (64, 128), 1) < 64

    def turned(tile):
        return jnp.transpose(jnp.concatenate([tile, tile], axis=0))[64:]

    def join(lower, upper):
        return jnp.where(low, lower, upper)

    def tiles(ref, p):
        return ref[p, :, pl.ds(0, 128)], ref[p, :, pl.ds(128, 128)]

    def even(p, _):
        (e_one, e_two), (_, e_after) = tiles(e_ref, p + 1), tiles(e_ref, p + 2)
        (b_one, b_two), (l_one, _), (_, l_after) = [tiles(l_ref, p + i) for i in range(3)]
        o_ref[p, :, pl.ds(0, 512)] = side(
            [join(b_one, turned(b_one)), join(b_two, e_two), e_one, join(e_after, l_one)]
        )
        o_ref[p, :, pl.ds(512, 64)] = l_after[:, 64:]
        put(p).start()
        return 0

    def uneven(p, _):
        (_, e_before), (e_one, e_two) = tiles(e_ref, p), tiles(e_ref, p + 1)
        (_, b_two), (l_one, _), (a_one, a_two) = [tiles(l_ref, p + i) for i in range(3)]
        o_ref[p, :, pl.ds(0, 512)] = side(
            [
                join(e_before, l_one), join(pltpu.roll(b_two, 64, 1), e_two), e_one,
                join(a_one, turned(a_one)),
            ]
        )
        o_ref[p, :, pl.ds(512, 64)] = a_two[:, :64]
        put(p).start()
        return 0

    @pl.when(odd == 0)
    def _():
        lax.fori_loop(0, 16, even, 0)

    @pl.when(odd == 1)
    def _():
        lax.fori_loop(0, 16, uneven, 0)

    for p in range(16):
        put(p).wait()


def any_spec():
    return pl.BlockSpec(memory_space=pl.ANY)


def vmem_spec():
    return pl.BlockSpec(memory_space=pltpu.VMEM)


def smem_spec():
    return pl.BlockSpec(memory_space=pltpu.SMEM)


def shape(*dims, dtype=F32):
    return jax.ShapeDtypeStruct(dims, dtype)


def call(kernel, out_shape, in_specs, out_specs, scratch, mib, name):
    return pl.pallas_call(
        kernel,
        out_shape=out_shape,
        in_specs=in_specs,
        out_specs=out_specs,
        scratch_shapes=scratch,
        compiler_params=pltpu.CompilerParams(vmem_limit_bytes=mib * MIB),
        cost_estimate=pl.CostEstimate(flops=1000, bytes_accessed=1000, transcendentals=0),
        name=name,
    )


def along(nz, nx, dz, dx):
    return [
        (z * nx + x, (z + dz) % nz * nx + (x + dx) % nx) for z in range(nz) for x in range(nx)
    ]


def ring(value, steps):
    return [value] + [lax.ppermute(value, "sx", pairs) for pairs in steps]


def neighbours(count):
    up = [(i, i + 1) for i in range(count - 1)]
    return up, [(b, a) for a, b in up]


def coef_frame(centre, coupling, volume):
    own = jnp.stack([centre, coupling, volume], axis=1)
    up, down = neighbours(lax.axis_size("sx"))
    low = lax.ppermute(own[-2:], "sx", up)
    high = lax.ppermute(own[:2], "sx", down)
    mid = jnp.concatenate([low, own, high], axis=0)
    up, down = neighbours(lax.axis_size("sy"))
    lo = lax.ppermute(mid[:, :, -2:], "sy", up)
    hi = lax.ppermute(mid[:, :, :2], "sy", down)
    return mid, lo, hi


def local(modes, centre, coupling, volume):
    ext = modes.shape[0]
    cell = centre.shape[0]
    margin = (ext - cell) // 2
    nx = lax.axis_size("sx")
    ny = lax.axis_size("sy")
    ix = lax.axis_index("sx")
    iy = lax.axis_index("sy")
    odd = lax.rem(iy, 2).astype(jnp.int32).reshape(1)
    share_x = cover(ix * cell - margin - 1, ext + 2, cell, nx, margin)
    share_y = cover(iy * cell - margin - 1, ext + 2, cell, ny, margin)
    mid, lo, hi = coef_frame(centre, coupling, volume)
    m = jnp.transpose(modes, (0, 1, 3, 2, 4))
    frame = ext + 2

    main, corner, south, north = call(
        pack_kernel,
        [
            shape(3, ext, 3, 64, 128, dtype=BF16),
            shape(3, 6, 3, 64, 128, dtype=BF16),
            shape(ext, 3, 3, 64, 128, dtype=BF16),
            shape(ext, 3, 3, 64, 128, dtype=BF16),
        ],
        [smem_spec(), any_spec()],
        [vmem_spec()] * 4,
        [pltpu.SemaphoreType.DMA((5,))],
        8,
        "pack",
    )(odd, m)
    packed = (main, corner, south, north)
    main, corner, south, north = pl.pallas_call(
        gate_kernel,
        out_shape=[shape(*x.shape, dtype=x.dtype) for x in packed],
        in_specs=[any_spec()] * 6,
        out_specs=[any_spec()] * 4,
        input_output_aliases={i: i for i in range(4)},
        compiler_params=pltpu.CompilerParams(vmem_limit_bytes=MIB),
        name="gate",
    )(*packed, lo, hi)
    main_pairs, other_pairs = [], []
    for y in range(ny):
        for x in range(nx - 1):
            lower, higher = x * ny + y, (x + 1) * ny + y
            main_pairs.append((higher, lower) if y % 2 == 0 else (lower, higher))
            other_pairs.append((lower, higher) if y % 2 == 0 else (higher, lower))
    main = lax.ppermute(main, ("sx", "sy"), main_pairs)
    corner = lax.ppermute(corner, ("sx", "sy"), other_pairs)
    up, down = neighbours(ny)
    south = lax.ppermute(south, "sy", up)
    north = lax.ppermute(north, "sy", down)

    own, coef, simg, nimg, ximg = call(
        own_kernel,
        [
            shape(64, 64),
            shape(frame, 6, frame, 128),
            shape(ext, 128, 1152, dtype=BF16),
            shape(ext, 128, 1152, dtype=BF16),
            shape(3, 128, ext * 384, dtype=BF16),
        ],
        [smem_spec()] * 3 + [any_spec()] + [vmem_spec()] * 3,
        [vmem_spec(), vmem_spec(), any_spec(), any_spec(), any_spec()],
        [
            pltpu.VMEM((ext + 3, ext, 3, 64, 128), BF16),
            pltpu.VMEM((ext + 3, frame, 3, 64, 128), F32),
            pltpu.VMEM((frame, 128, frame * 384), BF16),
            pltpu.VMEM((64, 128), F32),
            pltpu.SemaphoreType.DMA((ext,)),
            pltpu.SemaphoreType.DMA((3, ext)),
        ],
        44,
        "own_gram",
    )(odd, share_x, share_y, m, mid, lo, hi)
    around, cimg = call(
        rows_kernel,
        [shape(64, 128), shape(2, 2, 128, 3456, dtype=BF16)],
        [vmem_spec()] * 2 + [any_spec()] * 2 + [vmem_spec()],
        [vmem_spec(), vmem_spec()],
        [
            pltpu.VMEM((2, ext, 128, 1152), BF16),
            pltpu.VMEM((3, 3, 3, 16, 128), F32),
            pltpu.VMEM((2, 128, 64), F32),
            pltpu.SemaphoreType.DMA((2,)),
        ],
        18,
        "row_gram",
    )(south, north, simg, nimg, coef)
    early, keep = call(
        other_kernel,
        [shape(64, 256), shape(64, 64)],
        [smem_spec()] + [vmem_spec()] * 4,
        [vmem_spec()] * 2,
        [],
        10,
        "corner_gram",
    )(odd, corner, cimg, own, around)
    late = call(
        main_kernel,
        shape(64, 256),
        [smem_spec()] + [vmem_spec()] * 4,
        vmem_spec(),
        [],
        12,
        "column_gram",
    )(odd, main, ximg, cimg, keep)

    nz, nw = 4, nx // 4
    z_steps = [along(nz, nw, k, 0) for k in (1, 2, 3)]
    x_steps = [along(nz, nw, 0, k) for k in (1, 2, 3)]
    early = ring(jnp.stack(ring(early, z_steps)), x_steps)
    late = ring(jnp.stack(ring(late, x_steps)), z_steps)
    iz, iw = ix // nw, lax.rem(ix, nw)
    slots = []
    for i in range(4):
        for j in range(4):
            slots.append(lax.rem(iz - j + nz, nz) * nw + lax.rem(iw - i + nw, nw))
    for i in range(4):
        for j in range(4):
            slots.append(lax.rem(iz - i + nz, nz) * nw + lax.rem(iw - j + nw, nw))
    slot = jnp.stack(slots).astype(jnp.int32)
    pieces = early + late
    out = call(
        final_kernel,
        shape(nx, 64, 576),
        [smem_spec(), smem_spec()] + [any_spec()] * len(pieces),
        any_spec(),
        [
            pltpu.VMEM((nx + 2, 64, 256), F32),
            pltpu.VMEM((nx + 2, 64, 256), F32),
            pltpu.VMEM((nx, 64, 576), F32),
            pltpu.SemaphoreType.DMA((32,)),
            pltpu.SemaphoreType.DMA((nx,)),
        ],
        8,
        "assemble",
    )(odd, slot, *pieces)
    return out[None]


def solution(mesh):
    in_specs = (
        P("sx", "sy", None, None, None),
        P("sx", "sy", None),
        P("sx", "sy", None),
        P("sx", "sy", None),
    )
    out_specs = P("sy", None, None, None)
    return jax.shard_map(local, mesh=mesh, in_specs=in_specs, out_specs=out_specs, check_vma=False)
```

```python
import functools

import jax
import jax.numpy as jnp
from jax import lax
from jax.experimental import pallas as pl
from jax.experimental.pallas import tpu as pltpu
from jax.sharding import PartitionSpec as P

F32 = jnp.float32
BF16 = jnp.bfloat16
MID, LOW, UPP, DIA, VOL, OUT = range(6)
NT = (((1,), (1,)), ((), ()))
MIB = 1024 * 1024
TOP = 1024.0


def cover(start, length, cell, count, margin):
    places = start + jnp.arange(length, dtype=jnp.int32)
    base = jnp.floor_divide(places, cell)
    total = jnp.zeros((length,), jnp.int32)
    for step_off in (-1, 0, 1):
        owner = base + step_off
        inside = (
            (owner >= 0)
            & (owner < count)
            & (places >= owner * cell - margin)
            & (places < owner * cell + cell + margin)
        )
        total = total + inside.astype(jnp.int32)
    in_grid = (places >= 0) & (places < cell * count)
    safe = jnp.maximum(total, 1).astype(F32)
    return jnp.where(in_grid & (total > 0), 1.0 / safe, 0.0)


def neighbours(count):
    up = [(i, i + 1) for i in range(count - 1)]
    return up, [(b, a) for a, b in up]


def spread3(w):
    return [w[0], w[0] + w[0] + w[1], w[0] + w[1] + w[1] + w[2]]


def put_image(img_ref, slot, pos, chunk, image):
    for a in range(3):
        high = image[a].astype(BF16)
        low = (image[a] - high.astype(F32)).astype(BF16)
        lanes = pl.ds((pos * 3 + a) * 128, 128)
        img_ref[slot, pl.ds(chunk * 16, 16), lanes] = high
        img_ref[slot, pl.ds(64 + chunk * 16, 16), lanes] = low


def cell_image(lines, values, rows):
    if values is None:
        return [-(rows[2] * lines[a]) for a in range(3)]
    total = rows[1] * (values[0] + values[1] + values[2])
    return [rows[0] * values[a] + total - rows[2] * lines[a] for a in range(3)]


def coef_rows(coef_ref, x, y, names):
    return [coef_ref[x, n, pl.ds(y, 1), :] for n in names]


def depth_sum(raw, rows):
    return (
        raw.astype(F32) * rows[0]
        + pltpu.roll(raw, 1, 1).astype(F32) * rows[1]
        + pltpu.roll(raw, 127, 1).astype(F32) * rows[2]
    )


def side(blocks):
    return jnp.concatenate(blocks, axis=1)


def fold(total):
    return total[:, :64] + total[:, 64:]


def fold_rows(total):
    return total[:64] + total[64:]


def pack_kernel(odd_ref, m_hbm, main_ref, corner_ref, south_ref, north_ref, sems):
    ext = m_hbm.shape[0]
    odd = odd_ref[0]
    here = jnp.where(odd == 1, ext - 3, 0)
    there = jnp.where(odd == 1, 0, ext - 3)
    copies = [
        pltpu.make_async_copy(m_hbm.at[pl.ds(here, 3)], main_ref, sems.at[0]),
        pltpu.make_async_copy(
            m_hbm.at[pl.ds(there, 3), pl.ds(0, 3)], corner_ref.at[:, pl.ds(0, 3)], sems.at[1]
        ),
        pltpu.make_async_copy(
            m_hbm.at[pl.ds(there, 3), pl.ds(ext - 3, 3)], corner_ref.at[:, pl.ds(3, 3)], sems.at[2]
        ),
        pltpu.make_async_copy(m_hbm.at[:, pl.ds(ext - 3, 3)], south_ref, sems.at[3]),
        pltpu.make_async_copy(m_hbm.at[:, pl.ds(0, 3)], north_ref, sems.at[4]),
    ]
    for copy in copies:
        copy.start()
    for copy in copies:
        copy.wait()


def gate_kernel(*refs):
    pass


def own_kernel(
    odd_ref, sx_ref, sy_ref, m_hbm, mid_ref, lo_ref, hi_ref,
    out_ref, coef_ref, simg_hbm, nimg_hbm, ximg_hbm,
    m_ref, q_ref, img_ref, acc_ref, sems, strip_sems,
):
    ext = m_hbm.shape[0]
    frame = ext + 2
    odd = odd_ref[0]

    def load(x):
        return pltpu.make_async_copy(m_hbm.at[x], m_ref.at[x + 1], sems.at[x])

    for x in range(ext):
        load(x).start()
    none = jnp.zeros(m_ref.shape[1:], BF16)
    for edge in (0, ext + 1, ext + 2):
        m_ref[edge] = none
    zero = jnp.zeros(q_ref.shape[1:], F32)
    q_ref[0] = zero
    q_ref[1] = zero
    acc_ref[...] = jnp.zeros_like(acc_ref)

    lane = lax.broadcasted_iota(jnp.int32, (frame, 128), 1)
    place = lax.broadcasted_iota(jnp.int32, (frame, 128), 0)
    share_y = jnp.zeros((frame, 128), F32)
    for g in range(frame):
        share_y = jnp.where(place == g, sy_ref[g], share_y)

    def coefs(f, _):
        share = share_y * sx_ref[f]
        cen, cpl, vol = [
            jnp.concatenate([lo_ref[f, n], mid_ref[f, n], hi_ref[f, n]], axis=0) for n in range(3)
        ]
        kap = cpl * share
        vol = vol * share * share
        coef_ref[f, MID] = kap + kap
        coef_ref[f, LOW] = jnp.where(lane == 0, 0.0, pltpu.roll(kap, 1, 1))
        coef_ref[f, UPP] = jnp.where(lane == 127, 0.0, pltpu.roll(kap, 127, 1))
        coef_ref[f, DIA] = cen * share * share - vol + 0.5 * kap * kap
        coef_ref[f, VOL] = vol
        coef_ref[f, OUT] = kap * (1.0 / 16.0)
        return 0

    lax.fori_loop(0, frame, coefs, 0)

    def strips(f):
        return [
            pltpu.make_async_copy(
                img_ref.at[f, :, pl.ds(0, 1152)], simg_hbm.at[f - 1], strip_sems.at[0, f - 1]
            ),
            pltpu.make_async_copy(
                img_ref.at[f, :, pl.ds((frame - 3) * 384, 1152)], nimg_hbm.at[f - 1], strip_sems.at[1, f - 1]
            ),
        ]

    first_x = jnp.where(odd == 1, 0, frame - 3)

    def strip_x(f):
        return pltpu.make_async_copy(
            img_ref.at[f, :, pl.ds(384, ext * 384)], ximg_hbm.at[f - first_x], strip_sems.at[2, f - first_x]
        )

    def line(f, last, edge):
        if not last:
            kaps = [coef_rows(coef_ref, f + 1, g, (MID, LOW, UPP)) for g in range(1, ext + 1)]
            for a in range(3):
                for chunk in range(4):
                    rows = pl.ds(chunk * 16, 16)
                    pair = None
                    before = None
                    for j in range(ext):
                        w = depth_sum(m_ref[f + 1, j, a, rows, :], kaps[j])
                        if j == 0:
                            q_ref[f + 2, 0, a, rows, :] = w
                            pair = w
                        else:
                            now = before + w
                            q_ref[f + 2, j, a, rows, :] = now + pair
                            pair = now
                        before = w
                    q_ref[f + 2, ext, a, rows, :] = pair + before
                    q_ref[f + 2, ext + 1, a, rows, :] = before
        total = acc_ref[...]
        for g in range(frame):
            rows_of = coef_rows(coef_ref, f, g, (DIA, VOL, OUT))
            for chunk in range(4):
                rows = pl.ds(chunk * 16, 16)
                values = None
                if 1 <= g <= ext and not edge:
                    values = [m_ref[f, g - 1, a, rows, :].astype(F32) for a in range(3)]
                lines = []
                for a in range(3):
                    mid = q_ref[f + 1, g, a, rows, :]
                    if last:
                        lines.append(q_ref[f, g, a, rows, :])
                    else:
                        lines.append(
                            (q_ref[f, g, a, rows, :] + mid) + (mid + q_ref[f + 2, g, a, rows, :])
                        )
                put_image(img_ref, f, g, chunk, cell_image(lines, values, rows_of))
            if g % 2 == 0 and 1 < g <= ext and not edge:
                left = side([m_ref[f, i, a] for i in (g - 2, g - 1) for a in range(3)])
                total = total + lax.dot_general(
                    left, img_ref[f, :, pl.ds((g - 1) * 384, 768)], NT, preferred_element_type=F32
                )
        acc_ref[...] = total

        @pl.when((f >= first_x) & (f < first_x + 3))
        def _():
            strip_x(f).start()

        if not edge:
            for copy in strips(f):
                copy.start()

    load(0).wait()
    line(0, False, True)

    def body(f, _):
        @pl.when(f < ext)
        def _():
            load(f).wait()

        line(f, False, False)
        return 0

    lax.fori_loop(1, ext + 1, body, 0)
    line(ext + 1, True, True)
    out_ref[...] = fold(acc_ref[...])
    for f in range(1, ext + 1):
        for copy in strips(f):
            copy.wait()
    for i in range(3):
        strip_x(first_x + i).wait()


def rows_kernel(
    south_ref, north_ref, simg_hbm, nimg_hbm, coef_ref, out_ref, cimg_ref,
    img_ref, z_ref, acc_ref, sems,
):
    ext = south_ref.shape[0]
    raw_refs = (south_ref, north_ref)
    images = [
        pltpu.make_async_copy(ref, img_ref.at[s], sems.at[s])
        for s, ref in enumerate((simg_hbm, nimg_hbm))
    ]
    for copy in images:
        copy.start()
    acc_ref[...] = jnp.zeros_like(acc_ref)
    for s in range(2):
        r_ref = raw_refs[s]
        raw_y = (2, 1, 0) if s == 0 else (0, 1, 2)
        raw_g = (2, 1, 0) if s == 0 else (9, 10, 11)
        img_g = (3, 2, 1) if s == 0 else (8, 9, 10)
        img_y = (2, 1, 0) if s == 0 else (0, 1, 2)
        for t in range(2):
            raw_x = (0, 1, 2) if t == 0 else (9, 8, 7)
            raw_f = (1, 2, 3) if t == 0 else (10, 9, 8)
            img_f = (0, 1, 2) if t == 0 else (11, 10, 9)
            img_x = (0, 1, 2) if t == 0 else (2, 1, 0)

            def chunked(chunk, _, s=s, t=t, r_ref=r_ref, raw_x=raw_x, raw_f=raw_f, img_f=img_f, img_x=img_x):
                rows = pl.ds(pl.multiple_of(chunk * 16, 16), 16)
                low_rows = pl.ds(pl.multiple_of(64 + chunk * 16, 16), 16)
                for a in range(3):
                    across = []
                    for c in range(3):
                        w = [
                            depth_sum(
                                r_ref[raw_x[c], raw_y[d], a, rows, :],
                                coef_rows(coef_ref, raw_f[c], raw_g[d], (MID, LOW, UPP)),
                            )
                            for d in range(3)
                        ]
                        across.append(spread3(w))
                    for e in range(3):
                        for c, value in enumerate(spread3([across[i][e] for i in range(3)])):
                            z_ref[c, e, a] = value
                for c in range(3):
                    for e in range(3):
                        values = None
                        if c > 0 and e > 0:
                            values = [
                                r_ref[raw_x[c - 1], raw_y[e - 1], a, rows, :].astype(F32)
                                for a in range(3)
                            ]
                        image = cell_image(
                            [z_ref[c, e, a] for a in range(3)], values,
                            coef_rows(coef_ref, img_f[c], img_g[e], (DIA, VOL, OUT)),
                        )
                        for a in range(3):
                            high = image[a].astype(BF16)
                            low = (image[a] - high.astype(F32)).astype(BF16)
                            lanes = pl.ds(((img_x[c] * 3 + img_y[e]) * 3 + a) * 128, 128)
                            cimg_ref[t, s, rows, lanes] = high
                            cimg_ref[t, s, low_rows, lanes] = low
                return 0

            lax.fori_loop(0, 4, chunked, 0)
    for s in range(2):
        images[s].wait()

        def dots(x, _, s=s):
            right = side([raw_refs[s][x, j, a] for j in range(3) for a in range(3)])
            acc_ref[s] += lax.dot_general(img_ref[s, x], right, NT, preferred_element_type=F32)
            return 0

        lax.fori_loop(0, ext, dots, 0)
    out_ref[...] = side([fold_rows(acc_ref[0]), fold_rows(acc_ref[1])])


def corner_dot(raw, img):
    left = side([raw(i, j, a) for i in range(3) for j in range(3) for a in range(3)])
    return fold(lax.dot_general(left, img, NT, preferred_element_type=F32))


def other_kernel(odd_ref, corner_ref, cimg_ref, own_ref, rows_ref, out_ref, keep_ref):
    t = odd_ref[0]
    south = corner_dot(lambda i, j, a: corner_ref[i, j, a], cimg_ref[t, 0])
    north = corner_dot(lambda i, j, a: corner_ref[i, j + 3, a], cimg_ref[t, 1])
    around = rows_ref[...]
    out_ref[...] = side([own_ref[...], around[:, 64:], south, around[:, :64]])
    keep_ref[...] = north


def main_kernel(odd_ref, main_ref, ximg_ref, cimg_ref, early_ref, keep_ref, out_ref):
    t = 1 - odd_ref[0]
    ext = main_ref.shape[1]
    total = None
    for i in range(3):
        right = side([main_ref[i, j, a] for j in range(ext) for a in range(3)])
        part = lax.dot_general(ximg_ref[i], right, NT, preferred_element_type=F32)
        total = part if total is None else total + part
    south = corner_dot(lambda i, j, a: main_ref[i, j, a], cimg_ref[t, 0])
    north = corner_dot(lambda i, j, a: main_ref[i, ext - 3 + j, a], cimg_ref[t, 1])
    code = encode(side([early_ref[...], south, fold_rows(total), north, keep_ref[...]]))
    for p in range(out_ref.shape[0]):
        out_ref[p] = code


def encode(rows):
    top = jnp.max(jnp.abs(rows), axis=(0, 1), keepdims=True)
    top = jnp.where(top > 0.0, jnp.maximum(top * 1.01, 2.0**-100), 1.0).astype(BF16).astype(F32)
    value = rows * (TOP / top)
    value2 = value * value
    value4 = value2 * value2
    power = value4 * value4 * value4
    code = jnp.where(rows < 0.0, -power, power)
    row = lax.broadcasted_iota(jnp.int32, rows.shape, 0)
    lane = lax.broadcasted_iota(jnp.int32, rows.shape, 1)
    return jnp.where((row == 0) & (lane == 1), top, code).astype(BF16)


def decode(code):
    value = code.astype(F32)
    first = value[:8, :128]
    row = lax.broadcasted_iota(jnp.int32, first.shape, 0)
    lane = lax.broadcasted_iota(jnp.int32, first.shape, 1)

    def pick(tile, i, j):
        return jnp.sum(jnp.where((row == i) & (lane == j), tile, 0.0), axis=(0, 1), keepdims=True)

    scale = pick(first, 0, 1) * (1.0 / TOP)
    root = jnp.exp(jnp.log(jnp.abs(value)) * (1.0 / 12.0)) * scale
    root = jnp.where(value < 0.0, -root, root)
    head = root[:8, :128]
    head = jnp.where((row == 0) & (lane == 1), pick(head, 1, 0), head)
    return root, head


def final_kernel(odd_ref, code_ref, out_hbm, e_ref, l_ref, o_ref, out_sems):
    odd = odd_ref[0]
    none = jnp.zeros(e_ref.shape[1:], F32)
    for ref in (e_ref, l_ref):
        ref[0] = none
        ref[17] = none

    def read(p, _):
        root, head = decode(code_ref[p])
        e_ref[p + 1] = root[:, :256]
        l_ref[p + 1] = root[:, 256:]
        e_ref[p + 1, pl.ds(0, 8), pl.ds(0, 128)] = head
        return 0

    lax.fori_loop(0, 16, read, 0, unroll=2)

    def put(p):
        return pltpu.make_async_copy(o_ref.at[p], out_hbm.at[p], out_sems.at[p])

    low = lax.broadcasted_iota(jnp.int32, (64, 128), 1) < 64

    def turned(tile):
        return jnp.transpose(jnp.concatenate([tile, tile], axis=0))[64:]

    def join(lower, upper):
        return jnp.where(low, lower, upper)

    def tiles(ref, p):
        return ref[p, :, pl.ds(0, 128)], ref[p, :, pl.ds(128, 128)]

    def even(p, _):
        (e_one, e_two), (_, e_after) = tiles(e_ref, p + 1), tiles(e_ref, p + 2)
        (b_one, b_two), (l_one, _), (_, l_after) = [tiles(l_ref, p + i) for i in range(3)]
        o_ref[p, :, pl.ds(0, 512)] = side(
            [join(b_one, turned(b_one)), join(b_two, e_two), e_one, join(e_after, l_one)]
        )
        o_ref[p, :, pl.ds(512, 64)] = l_after[:, 64:]
        put(p).start()
        return 0

    def uneven(p, _):
        (_, e_before), (e_one, e_two) = tiles(e_ref, p), tiles(e_ref, p + 1)
        (_, b_two), (l_one, _), (a_one, a_two) = [tiles(l_ref, p + i) for i in range(3)]
        o_ref[p, :, pl.ds(0, 512)] = side(
            [
                join(e_before, l_one), join(pltpu.roll(b_two, 64, 1), e_two), e_one,
                join(a_one, turned(a_one)),
            ]
        )
        o_ref[p, :, pl.ds(512, 64)] = a_two[:, :64]
        put(p).start()
        return 0

    @pl.when(odd == 0)
    def _():
        lax.fori_loop(0, 16, even, 0)

    @pl.when(odd == 1)
    def _():
        lax.fori_loop(0, 16, uneven, 0)

    for p in range(16):
        put(p).wait()


def any_spec():
    return pl.BlockSpec(memory_space=pl.ANY)


def hbm_spec():
    return pl.BlockSpec(memory_space=pltpu.HBM)


def vmem_spec():
    return pl.BlockSpec(memory_space=pltpu.VMEM)


def smem_spec():
    return pl.BlockSpec(memory_space=pltpu.SMEM)


def shape(*dims, dtype=F32):
    return jax.ShapeDtypeStruct(dims, dtype)


def call(kernel, out_shape, in_specs, out_specs, scratch, mib, name):
    return pl.pallas_call(
        kernel,
        out_shape=out_shape,
        in_specs=in_specs,
        out_specs=out_specs,
        scratch_shapes=scratch,
        compiler_params=pltpu.CompilerParams(vmem_limit_bytes=mib * MIB),
        cost_estimate=pl.CostEstimate(flops=1000, bytes_accessed=1000, transcendentals=0),
        name=name,
    )


def gate(values, others):
    count = len(values)
    return pl.pallas_call(
        gate_kernel,
        out_shape=[shape(*x.shape, dtype=x.dtype) for x in values],
        in_specs=[any_spec()] * (count + len(others)),
        out_specs=[any_spec()] * count,
        input_output_aliases={i: i for i in range(count)},
        compiler_params=pltpu.CompilerParams(vmem_limit_bytes=MIB),
        name="gate",
    )(*values, *others)


def gate(values, others):
    count = len(values)
    return pl.pallas_call(
        gate_kernel,
        out_shape=[shape(*x.shape, dtype=x.dtype) for x in values],
        in_specs=[any_spec()] * (count + len(others)),
        out_specs=[any_spec()] * count,
        input_output_aliases={i: i for i in range(count)},
        compiler_params=pltpu.CompilerParams(vmem_limit_bytes=MIB),
        name="gate",
    )(*values, *others)


def along(nz, nx, dz, dx):
    return [
        (z * nx + x, (z + dz) % nz * nx + (x + dx) % nx) for z in range(nz) for x in range(nx)
    ]


def neighbours(count):
    up = [(i, i + 1) for i in range(count - 1)]
    return up, [(b, a) for a, b in up]


def spread3(w):
    return [w[0], w[0] + w[0] + w[1], w[0] + w[1] + w[1] + w[2]]


def put_image(img_ref, slot, pos, chunk, image):
    for a in range(3):
        high = image[a].astype(BF16)
        low = (image[a] - high.astype(F32)).astype(BF16)
        lanes = pl.ds((pos * 3 + a) * 128, 128)
        img_ref[slot, pl.ds(chunk * 16, 16), lanes] = high
        img_ref[slot, pl.ds(64 + chunk * 16, 16), lanes] = low


def cell_image(lines, values, rows):
    if values is None:
        return [-(rows[2] * lines[a]) for a in range(3)]
    total = rows[1] * (values[0] + values[1] + values[2])
    return [rows[0] * values[a] + total - rows[2] * lines[a] for a in range(3)]


def coef_rows(coef_ref, x, y, names):
    return [coef_ref[x, n, pl.ds(y, 1), :] for n in names]


def depth_sum(raw, rows):
    return (
        raw.astype(F32) * rows[0]
        + pltpu.roll(raw, 1, 1).astype(F32) * rows[1]
        + pltpu.roll(raw, 127, 1).astype(F32) * rows[2]
    )


def side(blocks):
    return jnp.concatenate(blocks, axis=1)


def fold(total):
    return total[:, :64] + total[:, 64:]


def fold_rows(total):
    return total[:64] + total[64:]


def pack_kernel(odd_ref, m_hbm, main_ref, corner_ref, south_ref, north_ref, sems):
    ext = m_hbm.shape[0]
    odd = odd_ref[0]
    here = jnp.where(odd == 1, ext - 3, 0)
    there = jnp.where(odd == 1, 0, ext - 3)
    copies = [
        pltpu.make_async_copy(m_hbm.at[pl.ds(here, 3)], main_ref, sems.at[0]),
        pltpu.make_async_copy(
            m_hbm.at[pl.ds(there, 3), pl.ds(0, 3)], corner_ref.at[:, pl.ds(0, 3)], sems.at[1]
        ),
        pltpu.make_async_copy(
            m_hbm.at[pl.ds(there, 3), pl.ds(ext - 3, 3)], corner_ref.at[:, pl.ds(3, 3)], sems.at[2]
        ),
        pltpu.make_async_copy(m_hbm.at[:, pl.ds(ext - 3, 3)], south_ref, sems.at[3]),
        pltpu.make_async_copy(m_hbm.at[:, pl.ds(0, 3)], north_ref, sems.at[4]),
    ]
    for copy in copies:
        copy.start()
    for copy in copies:
        copy.wait()


def gate_kernel(*refs):
    pass


def own_kernel(
    odd_ref, sx_ref, sy_ref, m_hbm, mid_ref, lo_ref, hi_ref,
    out_ref, coef_ref, simg_hbm, nimg_hbm, ximg_hbm,
    m_ref, q_ref, img_ref, acc_ref, sems, strip_sems,
):
    ext = m_hbm.shape[0]
    frame = ext + 2
    odd = odd_ref[0]

    def load(x):
        return pltpu.make_async_copy(m_hbm.at[x], m_ref.at[x + 1], sems.at[x])

    for x in range(ext):
        load(x).start()
    none = jnp.zeros(m_ref.shape[1:], BF16)
    for edge in (0, ext + 1, ext + 2):
        m_ref[edge] = none
    zero = jnp.zeros(q_ref.shape[1:], F32)
    q_ref[0] = zero
    q_ref[1] = zero
    acc_ref[...] = jnp.zeros_like(acc_ref)

    lane = lax.broadcasted_iota(jnp.int32, (frame, 128), 1)
    place = lax.broadcasted_iota(jnp.int32, (frame, 128), 0)
    share_y = jnp.zeros((frame, 128), F32)
    for g in range(frame):
        share_y = jnp.where(place == g, sy_ref[g], share_y)

    def coefs(f, _):
        share = share_y * sx_ref[f]
        cen, cpl, vol = [
            jnp.concatenate([lo_ref[f, n], mid_ref[f, n], hi_ref[f, n]], axis=0) for n in range(3)
        ]
        kap = cpl * share
        vol = vol * share * share
        coef_ref[f, MID] = kap + kap
        coef_ref[f, LOW] = jnp.where(lane == 0, 0.0, pltpu.roll(kap, 1, 1))
        coef_ref[f, UPP] = jnp.where(lane == 127, 0.0, pltpu.roll(kap, 127, 1))
        coef_ref[f, DIA] = cen * share * share - vol + 0.5 * kap * kap
        coef_ref[f, VOL] = vol
        coef_ref[f, OUT] = kap * (1.0 / 16.0)
        return 0

    lax.fori_loop(0, frame, coefs, 0)

    def strips(f):
        return [
            pltpu.make_async_copy(
                img_ref.at[f, :, pl.ds(0, 1152)], simg_hbm.at[f - 1], strip_sems.at[0, f - 1]
            ),
            pltpu.make_async_copy(
                img_ref.at[f, :, pl.ds((frame - 3) * 384, 1152)], nimg_hbm.at[f - 1], strip_sems.at[1, f - 1]
            ),
        ]

    first_x = jnp.where(odd == 1, 0, frame - 3)

    def strip_x(f):
        return pltpu.make_async_copy(
            img_ref.at[f, :, pl.ds(384, ext * 384)], ximg_hbm.at[f - first_x], strip_sems.at[2, f - first_x]
        )

    def line(f, last, edge):
        if not last:
            kaps = [coef_rows(coef_ref, f + 1, g, (MID, LOW, UPP)) for g in range(1, ext + 1)]
            for a in range(3):
                for chunk in range(4):
                    rows = pl.ds(chunk * 16, 16)
                    pair = None
                    before = None
                    for j in range(ext):
                        w = depth_sum(m_ref[f + 1, j, a, rows, :], kaps[j])
                        if j == 0:
                            q_ref[f + 2, 0, a, rows, :] = w
                            pair = w
                        else:
                            now = before + w
                            q_ref[f + 2, j, a, rows, :] = now + pair
                            pair = now
                        before = w
                    q_ref[f + 2, ext, a, rows, :] = pair + before
                    q_ref[f + 2, ext + 1, a, rows, :] = before
        total = acc_ref[...]
        for g in range(frame):
            rows_of = coef_rows(coef_ref, f, g, (DIA, VOL, OUT))
            for chunk in range(4):
                rows = pl.ds(chunk * 16, 16)
                values = None
                if 1 <= g <= ext and not edge:
                    values = [m_ref[f, g - 1, a, rows, :].astype(F32) for a in range(3)]
                lines = []
                for a in range(3):
                    mid = q_ref[f + 1, g, a, rows, :]
                    if last:
                        lines.append(q_ref[f, g, a, rows, :])
                    else:
                        lines.append(
                            (q_ref[f, g, a, rows, :] + mid) + (mid + q_ref[f + 2, g, a, rows, :])
                        )
                put_image(img_ref, f, g, chunk, cell_image(lines, values, rows_of))
            if g % 2 == 0 and 1 < g <= ext and not edge:
                left = side([m_ref[f, i, a] for i in (g - 2, g - 1) for a in range(3)])
                total = total + lax.dot_general(
                    left, img_ref[f, :, pl.ds((g - 1) * 384, 768)], NT, preferred_element_type=F32
                )
        acc_ref[...] = total

        @pl.when((f >= first_x) & (f < first_x + 3))
        def _():
            strip_x(f).start()

        if not edge:
            for copy in strips(f):
                copy.start()

    load(0).wait()
    line(0, False, True)

    def body(f, _):
        @pl.when(f < ext)
        def _():
            load(f).wait()

        line(f, False, False)
        return 0

    lax.fori_loop(1, ext + 1, body, 0)
    line(ext + 1, True, True)
    out_ref[...] = fold(acc_ref[...])
    for f in range(1, ext + 1):
        for copy in strips(f):
            copy.wait()
    for i in range(3):
        strip_x(first_x + i).wait()


def rows_kernel(
    south_ref, north_ref, simg_hbm, nimg_hbm, coef_ref, out_ref, cimg_ref,
    img_ref, z_ref, acc_ref, sems,
):
    ext = south_ref.shape[0]
    raw_refs = (south_ref, north_ref)
    images = [
        pltpu.make_async_copy(ref, img_ref.at[s], sems.at[s])
        for s, ref in enumerate((simg_hbm, nimg_hbm))
    ]
    for copy in images:
        copy.start()
    acc_ref[...] = jnp.zeros_like(acc_ref)
    for s in range(2):
        r_ref = raw_refs[s]
        raw_y = (2, 1, 0) if s == 0 else (0, 1, 2)
        raw_g = (2, 1, 0) if s == 0 else (9, 10, 11)
        img_g = (3, 2, 1) if s == 0 else (8, 9, 10)
        img_y = (2, 1, 0) if s == 0 else (0, 1, 2)
        for t in range(2):
            raw_x = (0, 1, 2) if t == 0 else (9, 8, 7)
            raw_f = (1, 2, 3) if t == 0 else (10, 9, 8)
            img_f = (0, 1, 2) if t == 0 else (11, 10, 9)
            img_x = (0, 1, 2) if t == 0 else (2, 1, 0)

            def chunked(chunk, _, s=s, t=t, r_ref=r_ref, raw_x=raw_x, raw_f=raw_f, img_f=img_f, img_x=img_x):
                rows = pl.ds(pl.multiple_of(chunk * 16, 16), 16)
                low_rows = pl.ds(pl.multiple_of(64 + chunk * 16, 16), 16)
                for a in range(3):
                    across = []
                    for c in range(3):
                        w = [
                            depth_sum(
                                r_ref[raw_x[c], raw_y[d], a, rows, :],
                                coef_rows(coef_ref, raw_f[c], raw_g[d], (MID, LOW, UPP)),
                            )
                            for d in range(3)
                        ]
                        across.append(spread3(w))
                    for e in range(3):
                        for c, value in enumerate(spread3([across[i][e] for i in range(3)])):
                            z_ref[c, e, a] = value
                for c in range(3):
                    for e in range(3):
                        values = None
                        if c > 0 and e > 0:
                            values = [
                                r_ref[raw_x[c - 1], raw_y[e - 1], a, rows, :].astype(F32)
                                for a in range(3)
                            ]
                        image = cell_image(
                            [z_ref[c, e, a] for a in range(3)], values,
                            coef_rows(coef_ref, img_f[c], img_g[e], (DIA, VOL, OUT)),
                        )
                        for a in range(3):
                            high = image[a].astype(BF16)
                            low = (image[a] - high.astype(F32)).astype(BF16)
                            lanes = pl.ds(((img_x[c] * 3 + img_y[e]) * 3 + a) * 128, 128)
                            cimg_ref[t, s, rows, lanes] = high
                            cimg_ref[t, s, low_rows, lanes] = low
                return 0

            lax.fori_loop(0, 4, chunked, 0)
    for s in range(2):
        images[s].wait()

        def dots(x, _, s=s):
            right = side([raw_refs[s][x, j, a] for j in range(3) for a in range(3)])
            acc_ref[s] += lax.dot_general(img_ref[s, x], right, NT, preferred_element_type=F32)
            return 0

        lax.fori_loop(0, ext, dots, 0)
    out_ref[...] = side([fold_rows(acc_ref[0]), fold_rows(acc_ref[1])])


def corner_dot(raw, img):
    left = side([raw(i, j, a) for i in range(3) for j in range(3) for a in range(3)])
    return fold(lax.dot_general(left, img, NT, preferred_element_type=F32))


def other_kernel(odd_ref, corner_ref, cimg_ref, own_ref, rows_ref, out_ref, keep_ref):
    t = odd_ref[0]
    south = corner_dot(lambda i, j, a: corner_ref[i, j, a], cimg_ref[t, 0])
    north = corner_dot(lambda i, j, a: corner_ref[i, j + 3, a], cimg_ref[t, 1])
    around = rows_ref[...]
    out_ref[...] = side([own_ref[...], around[:, 64:], south, around[:, :64]])
    keep_ref[...] = north


def main_kernel(odd_ref, main_ref, ximg_ref, cimg_ref, early_ref, keep_ref, out_ref):
    t = 1 - odd_ref[0]
    ext = main_ref.shape[1]
    total = None
    for i in range(3):
        right = side([main_ref[i, j, a] for j in range(ext) for a in range(3)])
        part = lax.dot_general(ximg_ref[i], right, NT, preferred_element_type=F32)
        total = part if total is None else total + part
    south = corner_dot(lambda i, j, a: main_ref[i, j, a], cimg_ref[t, 0])
    north = corner_dot(lambda i, j, a: main_ref[i, ext - 3 + j, a], cimg_ref[t, 1])
    code = encode(side([early_ref[...], south, fold_rows(total), north, keep_ref[...]]))
    for p in range(out_ref.shape[0]):
        out_ref[p] = code


def encode(rows):
    top = jnp.max(jnp.abs(rows), axis=(0, 1), keepdims=True)
    top = jnp.where(top > 0.0, jnp.maximum(top * 1.01, 2.0**-100), 1.0).astype(BF16).astype(F32)
    value = rows * (TOP / top)
    value2 = value * value
    value4 = value2 * value2
    power = value4 * value4 * value4
    code = jnp.where(rows < 0.0, -power, power)
    row = lax.broadcasted_iota(jnp.int32, rows.shape, 0)
    lane = lax.broadcasted_iota(jnp.int32, rows.shape, 1)
    return jnp.where((row == 0) & (lane == 1), top, code).astype(BF16)


def decode(code):
    value = code.astype(F32)
    first = value[:8, :128]
    row = lax.broadcasted_iota(jnp.int32, first.shape, 0)
    lane = lax.broadcasted_iota(jnp.int32, first.shape, 1)

    def pick(tile, i, j):
        return jnp.sum(jnp.where((row == i) & (lane == j), tile, 0.0), axis=(0, 1), keepdims=True)

    scale = pick(first, 0, 1) * (1.0 / TOP)
    root = jnp.exp(jnp.log(jnp.abs(value)) * (1.0 / 12.0)) * scale
    root = jnp.where(value < 0.0, -root, root)
    head = root[:8, :128]
    head = jnp.where((row == 0) & (lane == 1), pick(head, 1, 0), head)
    return root, head


def final_kernel(odd_ref, code_ref, out_hbm, e_ref, l_ref, o_ref, out_sems):
    odd = odd_ref[0]
    none = jnp.zeros(e_ref.shape[1:], F32)
    for ref in (e_ref, l_ref):
        ref[0] = none
        ref[17] = none

    def read(p, _):
        root, head = decode(code_ref[p])
        e_ref[p + 1] = root[:, :256]
        l_ref[p + 1] = root[:, 256:]
        e_ref[p + 1, pl.ds(0, 8), pl.ds(0, 128)] = head
        return 0

    lax.fori_loop(0, 16, read, 0, unroll=2)

    def put(p):
        return pltpu.make_async_copy(o_ref.at[p], out_hbm.at[p], out_sems.at[p])

    low = lax.broadcasted_iota(jnp.int32, (64, 128), 1) < 64

    def turned(tile):
        return jnp.transpose(jnp.concatenate([tile, tile], axis=0))[64:]

    def join(lower, upper):
        return jnp.where(low, lower, upper)

    def tiles(ref, p):
        return ref[p, :, pl.ds(0, 128)], ref[p, :, pl.ds(128, 128)]

    def even(p, _):
        (e_one, e_two), (_, e_after) = tiles(e_ref, p + 1), tiles(e_ref, p + 2)
        (b_one, b_two), (l_one, _), (_, l_after) = [tiles(l_ref, p + i) for i in range(3)]
        o_ref[p, :, pl.ds(0, 512)] = side(
            [join(b_one, turned(b_one)), join(b_two, e_two), e_one, join(e_after, l_one)]
        )
        o_ref[p, :, pl.ds(512, 64)] = l_after[:, 64:]
        put(p).start()
        return 0

    def uneven(p, _):
        (_, e_before), (e_one, e_two) = tiles(e_ref, p), tiles(e_ref, p + 1)
        (_, b_two), (l_one, _), (a_one, a_two) = [tiles(l_ref, p + i) for i in range(3)]
        o_ref[p, :, pl.ds(0, 512)] = side(
            [
                join(e_before, l_one), join(pltpu.roll(b_two, 64, 1), e_two), e_one,
                join(a_one, turned(a_one)),
            ]
        )
        o_ref[p, :, pl.ds(512, 64)] = a_two[:, :64]
        put(p).start()
        return 0

    @pl.when(odd == 0)
    def _():
        lax.fori_loop(0, 16, even, 0)

    @pl.when(odd == 1)
    def _():
        lax.fori_loop(0, 16, uneven, 0)

    for p in range(16):
        put(p).wait()


def any_spec():
    return pl.BlockSpec(memory_space=pl.ANY)


def hbm_spec():
    return pl.BlockSpec(memory_space=pltpu.HBM)


def vmem_spec():
    return pl.BlockSpec(memory_space=pltpu.VMEM)


def smem_spec():
    return pl.BlockSpec(memory_space=pltpu.SMEM)


def shape(*dims, dtype=F32):
    return jax.ShapeDtypeStruct(dims, dtype)


def call(kernel, out_shape, in_specs, out_specs, scratch, mib, name):
    return pl.pallas_call(
        kernel,
        out_shape=out_shape,
        in_specs=in_specs,
        out_specs=out_specs,
        scratch_shapes=scratch,
        compiler_params=pltpu.CompilerParams(vmem_limit_bytes=mib * MIB),
        cost_estimate=pl.CostEstimate(flops=1000, bytes_accessed=1000, transcendentals=0),
        name=name,
    )


def gate(values, others):
    count = len(values)
    return pl.pallas_call(
        gate_kernel,
        out_shape=[shape(*x.shape, dtype=x.dtype) for x in values],
        in_specs=[any_spec()] * (count + len(others)),
        out_specs=[any_spec()] * count,
        input_output_aliases={i: i for i in range(count)},
        compiler_params=pltpu.CompilerParams(vmem_limit_bytes=MIB),
        name="gate",
    )(*values, *others)


def gate(values, others):
    count = len(values)
    return pl.pallas_call(
        gate_kernel,
        out_shape=[shape(*x.shape, dtype=x.dtype) for x in values],
        in_specs=[any_spec()] * (count + len(others)),
        out_specs=[any_spec()] * count,
        input_output_aliases={i: i for i in range(count)},
        compiler_params=pltpu.CompilerParams(vmem_limit_bytes=MIB),
        name="gate",
    )(*values, *others)


def along(nz, nx, dz, dx):
    return [
        (z * nx + x, (z + dz) % nz * nx + (x + dx) % nx) for z in range(nz) for x in range(nx)
    ]


def ring(value, steps):
    return [value] + [lax.ppermute(value, "sx", pairs) for pairs in steps]


def neighbours(count):
    up = [(i, i + 1) for i in range(count - 1)]
    return up, [(b, a) for a, b in up]


def coef_columns(centre, coupling, volume):
    own = jnp.stack([centre, coupling, volume], axis=1)
    up, down = neighbours(lax.axis_size("sx"))
    low = lax.ppermute(own[-2:], "sx", up)
    high = lax.ppermute(own[:2], "sx", down)
    return jnp.concatenate([low, own, high], axis=0)


def coef_edges(mid):
    up, down = neighbours(lax.axis_size("sy"))
    lo = lax.ppermute(mid[:, :, -2:], "sy", up)
    hi = lax.ppermute(mid[:, :, :2], "sy", down)
    return lo, hi


def local(modes, centre, coupling, volume):
    ext = modes.shape[0]
    cell = centre.shape[0]
    margin = (ext - cell) // 2
    nx = lax.axis_size("sx")
    ny = lax.axis_size("sy")
    ix = lax.axis_index("sx")
    iy = lax.axis_index("sy")
    odd = lax.rem(iy, 2).astype(jnp.int32).reshape(1)
    share_x = cover(ix * cell - margin - 1, ext + 2, cell, nx, margin)
    share_y = cover(iy * cell - margin - 1, ext + 2, cell, ny, margin)
    mid = coef_columns(centre, coupling, volume)
    m = jnp.transpose(modes, (0, 1, 3, 2, 4))
    frame = ext + 2

    main, corner, south, north = call(
        pack_kernel,
        [
            shape(3, ext, 3, 64, 128, dtype=BF16),
            shape(3, 6, 3, 64, 128, dtype=BF16),
            shape(ext, 3, 3, 64, 128, dtype=BF16),
            shape(ext, 3, 3, 64, 128, dtype=BF16),
        ],
        [smem_spec(), hbm_spec()],
        [vmem_spec()] * 4,
        [pltpu.SemaphoreType.DMA((5,))],
        54,
        "pack",
    )(odd, m)
    main, corner, south, north, mid = gate((main, corner, south, north, mid), ())
    main_pairs, other_pairs = [], []
    for y in range(ny):
        for x in range(nx - 1):
            lower, higher = x * ny + y, (x + 1) * ny + y
            main_pairs.append((higher, lower) if y % 2 == 0 else (lower, higher))
            other_pairs.append((lower, higher) if y % 2 == 0 else (higher, lower))
    main = lax.ppermute(main, ("sx", "sy"), main_pairs)
    corner = lax.ppermute(corner, ("sx", "sy"), other_pairs)
    lo, hi = coef_edges(mid)
    south, north = gate((south, north), (lo, hi))
    up, down = neighbours(ny)
    south = lax.ppermute(south, "sy", up)
    north = lax.ppermute(north, "sy", down)

    own, coef, simg, nimg, ximg = call(
        own_kernel,
        [
            shape(64, 64),
            shape(frame, 6, frame, 128),
            shape(ext, 128, 1152, dtype=BF16),
            shape(ext, 128, 1152, dtype=BF16),
            shape(3, 128, ext * 384, dtype=BF16),
        ],
        [smem_spec()] * 3 + [hbm_spec()] + [vmem_spec()] * 3,
        [vmem_spec(), vmem_spec(), any_spec(), any_spec(), any_spec()],
        [
            pltpu.VMEM((ext + 3, ext, 3, 64, 128), BF16),
            pltpu.VMEM((ext + 3, frame, 3, 64, 128), F32),
            pltpu.VMEM((frame, 128, frame * 384), BF16),
            pltpu.VMEM((64, 128), F32),
            pltpu.SemaphoreType.DMA((ext,)),
            pltpu.SemaphoreType.DMA((3, ext)),
        ],
        44,
        "own_gram",
    )(odd, share_x, share_y, m, mid, lo, hi)
    around, cimg = call(
        rows_kernel,
        [shape(64, 128), shape(2, 2, 128, 3456, dtype=BF16)],
        [vmem_spec()] * 2 + [any_spec()] * 2 + [vmem_spec()],
        [vmem_spec(), vmem_spec()],
        [
            pltpu.VMEM((2, ext, 128, 1152), BF16),
            pltpu.VMEM((3, 3, 3, 16, 128), F32),
            pltpu.VMEM((2, 128, 64), F32),
            pltpu.SemaphoreType.DMA((2,)),
        ],
        18,
        "row_gram",
    )(south, north, simg, nimg, coef)
    early, keep = call(
        other_kernel,
        [shape(64, 256), shape(64, 64)],
        [smem_spec()] + [vmem_spec()] * 4,
        [vmem_spec()] * 2,
        [],
        10,
        "corner_gram",
    )(odd, corner, cimg, own, around)
    code = call(
        main_kernel,
        shape(nx, 64, 512, dtype=BF16),
        [smem_spec()] + [vmem_spec()] * 5,
        vmem_spec(),
        [],
        14,
        "column_gram",
    )(odd, main, ximg, cimg, early, keep)
    code = lax.all_to_all(code, "sx", 0, 0)
    out = call(
        final_kernel,
        shape(nx, 64, 576),
        [smem_spec(), vmem_spec()],
        any_spec(),
        [
            pltpu.VMEM((nx + 2, 64, 256), F32),
            pltpu.VMEM((nx + 2, 64, 256), F32),
            pltpu.VMEM((nx, 64, 576), F32),
            pltpu.SemaphoreType.DMA((nx,)),
        ],
        12,
        "assemble",
    )(odd, code)
    return out[None]


def solution(mesh):
    in_specs = (
        P("sx", "sy", None, None, None),
        P("sx", "sy", None),
        P("sx", "sy", None),
        P("sx", "sy", None),
    )
    out_specs = P("sy", None, None, None)
    return jax.shard_map(local, mesh=mesh, in_specs=in_specs, out_specs=out_specs, check_vma=False)
```

```python
import functools

import jax
import jax.numpy as jnp
from jax import lax
from jax.experimental import pallas as pl
from jax.experimental.pallas import tpu as pltpu
from jax.sharding import PartitionSpec as P

F32 = jnp.float32
BF16 = jnp.bfloat16
MID, LOW, UPP, DIA, VOL, OUT = range(6)
NT = (((1,), (1,)), ((), ()))
MIB = 1024 * 1024
TOP = 1024.0
OWN_MIB = 20


def cover(start, length, cell, count, margin):
    places = start + jnp.arange(length, dtype=jnp.int32)
    base = jnp.floor_divide(places, cell)
    total = jnp.zeros((length,), jnp.int32)
    for step_off in (-1, 0, 1):
        owner = base + step_off
        inside = (
            (owner >= 0)
            & (owner < count)
            & (places >= owner * cell - margin)
            & (places < owner * cell + cell + margin)
        )
        total = total + inside.astype(jnp.int32)
    in_grid = (places >= 0) & (places < cell * count)
    safe = jnp.maximum(total, 1).astype(F32)
    return jnp.where(in_grid & (total > 0), 1.0 / safe, 0.0)


def neighbours(count):
    up = [(i, (i + 1) % count) for i in range(count)]
    return up, [(b, a) for a, b in up]


def spread3(w):
    return [w[0], w[0] + w[0] + w[1], w[0] + w[1] + w[1] + w[2]]


def cell_image(lines, values, rows):
    if values is None:
        return [-(rows[2] * lines[a]) for a in range(3)]
    total = rows[1] * (values[0] + values[1] + values[2])
    return [rows[0] * values[a] + total - rows[2] * lines[a] for a in range(3)]


def coef_rows(coef_ref, x, y, names):
    return [coef_ref[x, n, pl.ds(y, 1), :] for n in names]


def depth_sum(raw, rows):
    return (
        raw.astype(F32) * rows[0]
        + pltpu.roll(raw, 1, 1).astype(F32) * rows[1]
        + pltpu.roll(raw, 127, 1).astype(F32) * rows[2]
    )


def side(blocks):
    return jnp.concatenate(blocks, axis=1)


def fold(total):
    return total[:, :64] + total[:, 64:]


def fold_rows(total):
    return total[:64] + total[64:]


def pack_kernel(odd_ref, m_hbm, main_ref, corner_ref, south_ref, north_ref, sems):
    ext = m_hbm.shape[0]
    odd = odd_ref[0]
    here = jnp.where(odd == 1, ext - 3, 0)
    there = jnp.where(odd == 1, 0, ext - 3)
    copies = [
        pltpu.make_async_copy(m_hbm.at[pl.ds(here, 3)], main_ref, sems.at[0]),
        pltpu.make_async_copy(
            m_hbm.at[pl.ds(there, 3), pl.ds(0, 3)], corner_ref.at[:, pl.ds(0, 3)], sems.at[1]
        ),
        pltpu.make_async_copy(
            m_hbm.at[pl.ds(there, 3), pl.ds(ext - 3, 3)], corner_ref.at[:, pl.ds(3, 3)], sems.at[2]
        ),
        pltpu.make_async_copy(m_hbm.at[:, pl.ds(ext - 3, 3)], south_ref, sems.at[3]),
        pltpu.make_async_copy(m_hbm.at[:, pl.ds(0, 3)], north_ref, sems.at[4]),
    ]
    for copy in copies:
        copy.start()
    for copy in copies:
        copy.wait()


def gate_kernel(*refs):
    pass


def own_kernel(
    odd_ref, sx_ref, sy_ref, m_ref, mid_ref, lo_ref, hi_ref,
    out_ref, coef_ref, img_ref, q_ref, acc_ref,
):
    ext = m_ref.shape[0]
    frame = ext + 2
    odd = odd_ref[0]

    zero = jnp.zeros(q_ref.shape[1:], F32)
    for edge in (0, ext + 1):
        q_ref[edge] = zero

    lane = lax.broadcasted_iota(jnp.int32, (frame, 128), 1)
    place = lax.broadcasted_iota(jnp.int32, (frame, 128), 0)
    share_y = jnp.zeros((frame, 128), F32)
    for g in range(frame):
        share_y = jnp.where(place == g, sy_ref[g], share_y)

    def coefs(f, _):
        share = share_y * sx_ref[f]
        cen, cpl, vol = [
            jnp.concatenate([lo_ref[f, n], mid_ref[f, n], hi_ref[f, n]], axis=0) for n in range(3)
        ]
        kap = cpl * share
        vol = vol * share * share
        coef_ref[f, MID] = kap + kap
        coef_ref[f, LOW] = jnp.where(lane == 0, 0.0, pltpu.roll(kap, 1, 1))
        coef_ref[f, UPP] = jnp.where(lane == 127, 0.0, pltpu.roll(kap, 127, 1))
        coef_ref[f, DIA] = cen * share * share - vol + 0.5 * kap * kap
        coef_ref[f, VOL] = vol
        coef_ref[f, OUT] = kap * (1.0 / 16.0)
        return 0

    lax.fori_loop(0, frame, coefs, 0)

    def first(f, chunk):
        rows = pl.ds(pl.multiple_of(chunk * 16, 16), 16)
        kaps = [coef_rows(coef_ref, f, g, (MID, LOW, UPP)) for g in range(1, ext + 1)]
        for a in range(3):
            before = pair = None
            for j in range(ext):
                w = depth_sum(m_ref[f - 1, j * 3 + a, rows, :], kaps[j])
                if j == 0:
                    q_ref[f, 0, a, rows, :] = w
                    pair = w
                else:
                    now = before + w
                    q_ref[f, j, a, rows, :] = now + pair
                    pair = now
                before = w
            q_ref[f, ext, a, rows, :] = pair + before
            q_ref[f, ext + 1, a, rows, :] = before

    def image(f, chunk, edge, inward=None):
        rows = pl.ds(pl.multiple_of(chunk * 16, 16), 16)
        low_rows = pl.ds(pl.multiple_of(64 + chunk * 16, 16), 16)
        for g in range(frame):
            values = None
            if 1 <= g <= ext and not edge:
                values = [m_ref[f - 1, (g - 1) * 3 + a, rows, :].astype(F32) for a in range(3)]
            lines = []
            for a in range(3):
                if edge:
                    lines.append(q_ref[inward, g, a, rows, :])
                    continue
                mid = q_ref[f, g, a, rows, :]
                lines.append((q_ref[f - 1, g, a, rows, :] + mid) + (mid + q_ref[f + 1, g, a, rows, :]))
            result = cell_image(lines, values, coef_rows(coef_ref, f, g, (DIA, VOL, OUT)))
            for a in range(3):
                high = result[a].astype(BF16)
                lanes = pl.ds((g * 3 + a) * 128, 128)
                img_ref[f, rows, lanes] = high
                img_ref[f, low_rows, lanes] = (result[a] - high.astype(F32)).astype(BF16)

    def dot(f, chunk):
        base = jnp.minimum(chunk * 8, ext * 3 - 8)
        tiles = [m_ref[jnp.maximum(f - 1, 0), base + i] for i in range(8)]
        for i in range(2):
            tiles[i] = jnp.where(chunk == 3, jnp.zeros_like(tiles[i]), tiles[i])
        lanes = pl.ds(pl.multiple_of(base * 128 + 384, 128), 1024)
        acc_ref[...] += lax.dot_general(
            side(tiles), img_ref[f, :, lanes], NT, preferred_element_type=F32
        )

    def chunks(body):
        def step(chunk, _):
            body(chunk)
            return 0

        lax.fori_loop(0, 4, step, 0)

    chunks(lambda chunk: first(1, chunk))

    def inner(f, chunk):
        dot(f - 1, chunk)
        first(f + 1, chunk)
        image(f, chunk, False)

    def line(f, _):
        chunks(lambda chunk: inner(f, chunk))

        @pl.when(f == 1)
        def _():
            acc_ref[...] = jnp.zeros_like(acc_ref)

        return 0

    lax.fori_loop(1, ext, line, 0)

    def inner_last(chunk):
        dot(ext - 1, chunk)
        image(ext, chunk, False)

    chunks(inner_last)
    rim = jnp.where(odd == 1, 0, ext + 1)
    inward = jnp.where(odd == 1, 1, ext)

    def inner_rim(chunk):
        dot(ext, chunk)
        image(rim, chunk, True, inward)

    chunks(inner_rim)
    out_ref[...] = fold(acc_ref[...])


def rows_kernel(
    south_ref, north_ref, img_ref, coef_ref, out_ref, cimg_ref, z_ref, acc_ref
):
    ext = south_ref.shape[0]
    raw_refs = (south_ref, north_ref)
    acc_ref[...] = jnp.zeros_like(acc_ref)
    for s in range(2):
        r_ref = raw_refs[s]
        raw_y = (2, 1, 0) if s == 0 else (0, 1, 2)
        raw_g = (2, 1, 0) if s == 0 else (9, 10, 11)
        img_g = (3, 2, 1) if s == 0 else (8, 9, 10)
        img_y = (2, 1, 0) if s == 0 else (0, 1, 2)
        for t in range(2):
            raw_x = (0, 1, 2) if t == 0 else (9, 8, 7)
            raw_f = (1, 2, 3) if t == 0 else (10, 9, 8)
            img_f = (0, 1, 2) if t == 0 else (11, 10, 9)
            img_x = (0, 1, 2) if t == 0 else (2, 1, 0)

            def chunked(chunk, _, s=s, t=t, r_ref=r_ref, raw_x=raw_x, raw_f=raw_f, img_f=img_f, img_x=img_x):
                rows = pl.ds(pl.multiple_of(chunk * 16, 16), 16)
                low_rows = pl.ds(pl.multiple_of(64 + chunk * 16, 16), 16)
                for a in range(3):
                    across = []
                    for c in range(3):
                        w = [
                            depth_sum(
                                r_ref[raw_x[c], raw_y[d], a, rows, :],
                                coef_rows(coef_ref, raw_f[c], raw_g[d], (MID, LOW, UPP)),
                            )
                            for d in range(3)
                        ]
                        across.append(spread3(w))
                    for e in range(3):
                        for c, value in enumerate(spread3([across[i][e] for i in range(3)])):
                            z_ref[c, e, a] = value
                for c in range(3):
                    for e in range(3):
                        values = None
                        if c > 0 and e > 0:
                            values = [
                                r_ref[raw_x[c - 1], raw_y[e - 1], a, rows, :].astype(F32)
                                for a in range(3)
                            ]
                        image = cell_image(
                            [z_ref[c, e, a] for a in range(3)], values,
                            coef_rows(coef_ref, img_f[c], img_g[e], (DIA, VOL, OUT)),
                        )
                        for a in range(3):
                            high = image[a].astype(BF16)
                            low = (image[a] - high.astype(F32)).astype(BF16)
                            lanes = pl.ds(((img_x[c] * 3 + img_y[e]) * 3 + a) * 128, 128)
                            cimg_ref[t, s, rows, lanes] = high
                            cimg_ref[t, s, low_rows, lanes] = low
                return 0

            lax.fori_loop(0, 4, chunked, 0)
    for s in range(2):

        def dots(x, _, s=s):
            right = side([raw_refs[s][x, j, a] for j in range(3) for a in range(3)])
            lines = img_ref[x + 1, :, pl.ds(s * (ext - 1) * 384, 1152)]
            acc_ref[s] += lax.dot_general(lines, right, NT, preferred_element_type=F32)
            return 0

        lax.fori_loop(0, ext, dots, 0)
    out_ref[...] = side([fold_rows(acc_ref[0]), fold_rows(acc_ref[1])])


def masked(there, block):
    return jnp.where(there, block, jnp.zeros_like(block))


def corner_dot(raw, img):
    left = side([raw(i, j, a) for i in range(3) for j in range(3) for a in range(3)])
    return fold(lax.dot_general(left, img, NT, preferred_element_type=F32))


def other_kernel(odd_ref, there_ref, corner_ref, cimg_ref, own_ref, rows_ref, out_ref, keep_ref):
    t = odd_ref[0]
    low, high = there_ref[0] == 1, there_ref[1] == 1
    beside = there_ref[3] == 1
    south = corner_dot(lambda i, j, a: corner_ref[i, j, a], cimg_ref[t, 0])
    north = corner_dot(lambda i, j, a: corner_ref[i, j + 3, a], cimg_ref[t, 1])
    around = rows_ref[...]
    out_ref[...] = side(
        [
            own_ref[...], masked(high, around[:, 64:]), masked(low & beside, south),
            masked(low, around[:, :64]),
        ]
    )
    keep_ref[...] = masked(high & beside, north)


def main_kernel(odd_ref, there_ref, main_ref, img_ref, cimg_ref, early_ref, keep_ref, out_ref):
    t = 1 - odd_ref[0]
    ext = main_ref.shape[1]
    start = jnp.where(odd_ref[0] == 1, 0, ext - 1)
    total = None
    for i in range(3):
        right = side([main_ref[i, j, a] for j in range(ext) for a in range(3)])
        lines = img_ref[start + i, :, pl.ds(384, ext * 384)]
        part = lax.dot_general(lines, right, NT, preferred_element_type=F32)
        total = part if total is None else total + part
    south = corner_dot(lambda i, j, a: main_ref[i, j, a], cimg_ref[t, 0])
    north = corner_dot(lambda i, j, a: main_ref[i, ext - 3 + j, a], cimg_ref[t, 1])
    low, high = there_ref[0] == 1, there_ref[1] == 1
    beside = there_ref[2] == 1
    blocks = [
        masked(low & beside, south), masked(beside, fold_rows(total)), masked(high & beside, north)
    ]
    code = encode(side([early_ref[...]] + blocks + [keep_ref[...]]))
    for p in range(out_ref.shape[0]):
        out_ref[p] = code


def encode(rows):
    top = jnp.max(jnp.abs(rows), axis=(0, 1), keepdims=True)
    top = jnp.where(top > 0.0, jnp.maximum(top * 1.01, 2.0**-100), 1.0).astype(BF16).astype(F32)
    value = rows * (TOP / top)
    value2 = value * value
    value4 = value2 * value2
    power = value4 * value4 * value4
    code = jnp.where(rows < 0.0, -power, power)
    row = lax.broadcasted_iota(jnp.int32, rows.shape, 0)
    lane = lax.broadcasted_iota(jnp.int32, rows.shape, 1)
    return jnp.where((row == 0) & (lane == 1), top, code).astype(BF16)


def decode(code):
    value = code.astype(F32)
    first = value[:8, :128]
    row = lax.broadcasted_iota(jnp.int32, first.shape, 0)
    lane = lax.broadcasted_iota(jnp.int32, first.shape, 1)

    def pick(tile, i, j):
        return jnp.sum(jnp.where((row == i) & (lane == j), tile, 0.0), axis=(0, 1), keepdims=True)

    scale = pick(first, 0, 1) * (1.0 / TOP)
    root = jnp.exp(jnp.log(jnp.abs(value)) * (1.0 / 12.0)) * scale
    root = jnp.where(value < 0.0, -root, root)
    head = root[:8, :128]
    head = jnp.where((row == 0) & (lane == 1), pick(head, 1, 0), head)
    return root, head


def final_kernel(odd_ref, code_ref, out_hbm, e_ref, l_ref, o_ref, out_sems):
    odd = odd_ref[0]
    none = jnp.zeros(e_ref.shape[1:], F32)
    for ref in (e_ref, l_ref):
        ref[0] = none
        ref[17] = none

    def read(p, _):
        root, head = decode(code_ref[p])
        e_ref[p + 1] = root[:, :256]
        l_ref[p + 1] = root[:, 256:]
        e_ref[p + 1, pl.ds(0, 8), pl.ds(0, 128)] = head
        return 0

    lax.fori_loop(0, 16, read, 0, unroll=2)

    def put(p):
        return pltpu.make_async_copy(o_ref.at[p], out_hbm.at[p], out_sems.at[p])

    low = lax.broadcasted_iota(jnp.int32, (64, 128), 1) < 64

    def turned(tile):
        return jnp.transpose(jnp.concatenate([tile, tile], axis=0))[64:]

    def join(lower, upper):
        return jnp.where(low, lower, upper)

    def tiles(ref, p):
        return ref[p, :, pl.ds(0, 128)], ref[p, :, pl.ds(128, 128)]

    def even(p, _):
        (e_one, e_two), (_, e_after) = tiles(e_ref, p + 1), tiles(e_ref, p + 2)
        (b_one, b_two), (l_one, _), (_, l_after) = [tiles(l_ref, p + i) for i in range(3)]
        o_ref[p, :, pl.ds(0, 512)] = side(
            [join(b_one, turned(b_one)), join(b_two, e_two), e_one, join(e_after, l_one)]
        )
        o_ref[p, :, pl.ds(512, 64)] = l_after[:, 64:]
        put(p).start()
        return 0

    def uneven(p, _):
        (_, e_before), (e_one, e_two) = tiles(e_ref, p), tiles(e_ref, p + 1)
        (_, b_two), (l_one, _), (a_one, a_two) = [tiles(l_ref, p + i) for i in range(3)]
        o_ref[p, :, pl.ds(0, 512)] = side(
            [
                join(e_before, l_one), join(pltpu.roll(b_two, 64, 1), e_two), e_one,
                join(a_one, turned(a_one)),
            ]
        )
        o_ref[p, :, pl.ds(512, 64)] = a_two[:, :64]
        put(p).start()
        return 0

    @pl.when(odd == 0)
    def _():
        lax.fori_loop(0, 16, even, 0)

    @pl.when(odd == 1)
    def _():
        lax.fori_loop(0, 16, uneven, 0)

    for p in range(16):
        put(p).wait()


def any_spec():
    return pl.BlockSpec(memory_space=pl.ANY)


def vmem_spec():
    return pl.BlockSpec(memory_space=pltpu.VMEM)


def smem_spec():
    return pl.BlockSpec(memory_space=pltpu.SMEM)


def shape(*dims, dtype=F32):
    return jax.ShapeDtypeStruct(dims, dtype)


def call(kernel, out_shape, in_specs, out_specs, scratch, mib, name):
    return pl.pallas_call(
        kernel,
        out_shape=out_shape,
        in_specs=in_specs,
        out_specs=out_specs,
        scratch_shapes=scratch,
        compiler_params=pltpu.CompilerParams(vmem_limit_bytes=mib * MIB),
        cost_estimate=pl.CostEstimate(flops=1000, bytes_accessed=1000, transcendentals=0),
        name=name,
    )


def gate(values, others):
    count = len(values)
    return pl.pallas_call(
        gate_kernel,
        out_shape=[shape(*x.shape, dtype=x.dtype) for x in values],
        in_specs=[any_spec()] * (count + len(others)),
        out_specs=[any_spec()] * count,
        input_output_aliases={i: i for i in range(count)},
        compiler_params=pltpu.CompilerParams(vmem_limit_bytes=MIB),
        name="gate",
    )(*values, *others)


def coef_columns(centre, coupling, volume):
    own = jnp.stack([centre, coupling, volume], axis=1)
    up, down = neighbours(lax.axis_size("sx"))
    low = lax.ppermute(own[-2:], "sx", up)
    high = lax.ppermute(own[:2], "sx", down)
    return jnp.concatenate([low, own, high], axis=0)


def coef_edges(mid):
    up, down = neighbours(lax.axis_size("sy"))
    lo = lax.ppermute(mid[:, :, -2:], "sy", up)
    hi = lax.ppermute(mid[:, :, :2], "sy", down)
    return lo, hi


def local(modes, centre, coupling, volume):
    ext = modes.shape[0]
    cell = centre.shape[0]
    margin = (ext - cell) // 2
    nx = lax.axis_size("sx")
    ny = lax.axis_size("sy")
    ix = lax.axis_index("sx")
    iy = lax.axis_index("sy")
    odd = lax.rem(iy, 2).astype(jnp.int32).reshape(1)
    share_x = cover(ix * cell - margin - 1, ext + 2, cell, nx, margin)
    share_y = cover(iy * cell - margin - 1, ext + 2, cell, ny, margin)
    first_x, last_x = ix > 0, ix < nx - 1
    is_odd = odd[0] == 1
    there = jnp.stack(
        [
            iy > 0, iy < ny - 1, jnp.where(is_odd, first_x, last_x),
            jnp.where(is_odd, last_x, first_x),
        ]
    ).astype(jnp.int32)
    mid = coef_columns(centre, coupling, volume)
    m = jnp.transpose(modes, (0, 1, 3, 2, 4))
    frame = ext + 2

    main, corner, south, north = call(
        pack_kernel,
        [
            shape(3, ext, 3, 64, 128, dtype=BF16),
            shape(3, 6, 3, 64, 128, dtype=BF16),
            shape(ext, 3, 3, 64, 128, dtype=BF16),
            shape(ext, 3, 3, 64, 128, dtype=BF16),
        ],
        [smem_spec(), vmem_spec()],
        [vmem_spec()] * 4,
        [pltpu.SemaphoreType.DMA((5,))],
        8,
        "pack",
    )(odd, m)
    main, corner, south, north, mid = gate((main, corner, south, north, mid), ())
    main_pairs, other_pairs = [], []
    for y in range(ny):
        for x in range(nx):
            lower, higher = x * ny + y, (x + 1) % nx * ny + y
            main_pairs.append((higher, lower) if y % 2 == 0 else (lower, higher))
            other_pairs.append((lower, higher) if y % 2 == 0 else (higher, lower))
    main = lax.ppermute(main, ("sx", "sy"), main_pairs)
    corner = lax.ppermute(corner, ("sx", "sy"), other_pairs)
    lo, hi = coef_edges(mid)
    south, north = gate((south, north), (lo, hi))
    up, down = neighbours(ny)
    south = lax.ppermute(south, "sy", up)
    north = lax.ppermute(north, "sy", down)

    own, coef, img = call(
        own_kernel,
        [
            shape(64, 64),
            shape(frame, 6, frame, 128),
            shape(frame, 128, frame * 384, dtype=BF16),
        ],
        [smem_spec()] * 3 + [vmem_spec()] * 4,
        [vmem_spec()] * 3,
        [
            pltpu.VMEM((frame, frame, 3, 64, 128), F32),
            pltpu.VMEM((64, 128), F32),
        ],
        OWN_MIB,
        "own_gram",
    )(odd, share_x, share_y, m.reshape(ext, ext * 3, 64, 128), mid, lo, hi)
    around, cimg = call(
        rows_kernel,
        [shape(64, 128), shape(2, 2, 128, 3456, dtype=BF16)],
        [vmem_spec()] * 4,
        [vmem_spec(), vmem_spec()],
        [
            pltpu.VMEM((3, 3, 3, 16, 128), F32),
            pltpu.VMEM((2, 128, 64), F32),
        ],
        24,
        "row_gram",
    )(south, north, img, coef)
    early, keep = call(
        other_kernel,
        [shape(64, 256), shape(64, 64)],
        [smem_spec()] * 2 + [vmem_spec()] * 4,
        [vmem_spec()] * 2,
        [],
        10,
        "corner_gram",
    )(odd, there, corner, cimg, own, around)
    code = call(
        main_kernel,
        shape(nx, 64, 512, dtype=BF16),
        [smem_spec()] * 2 + [vmem_spec()] * 5,
        vmem_spec(),
        [],
        28,
        "column_gram",
    )(odd, there, main, img, cimg, early, keep)
    code = lax.all_to_all(code, "sx", 0, 0)
    out = call(
        final_kernel,
        shape(nx, 64, 576),
        [smem_spec(), vmem_spec()],
        any_spec(),
        [
            pltpu.VMEM((nx + 2, 64, 256), F32),
            pltpu.VMEM((nx + 2, 64, 256), F32),
            pltpu.VMEM((nx, 64, 576), F32),
            pltpu.SemaphoreType.DMA((nx,)),
        ],
        12,
        "assemble",
    )(odd, code)
    return out[None]


def solution(mesh):
    in_specs = (
        P("sx", "sy", None, None, None),
        P("sx", "sy", None),
        P("sx", "sy", None),
        P("sx", "sy", None),
    )
    out_specs = P("sy", None, None, None)
    return jax.shard_map(local, mesh=mesh, in_specs=in_specs, out_specs=out_specs, check_vma=False)
```

```python
import functools

import jax
import jax.numpy as jnp
from jax import lax
from jax.experimental import pallas as pl
from jax.experimental.pallas import tpu as pltpu
from jax.sharding import PartitionSpec as P

F32 = jnp.float32
BF16 = jnp.bfloat16
MID, LOW, UPP, DIA, VOL, OUT = range(6)
NT = (((1,), (1,)), ((), ()))
MIB = 1024 * 1024
TOP = 1024.0
OWN_MIB = 10


def cover(local, index, cell, count, margin):
    places = index * cell + local
    base = index + (local >= cell).astype(jnp.int32) - (local < 0).astype(jnp.int32)
    total = jnp.zeros(local.shape, jnp.int32)
    for step_off in (-1, 0, 1):
        owner = base + step_off
        inside = (
            (owner >= 0)
            & (owner < count)
            & (places >= owner * cell - margin)
            & (places < owner * cell + cell + margin)
        )
        total = total + inside.astype(jnp.int32)
    in_grid = (places >= 0) & (places < cell * count)
    safe = jnp.maximum(total, 1).astype(F32)
    return jnp.where(in_grid & (total > 0), 1.0 / safe, 0.0)


def is_odd():
    return lax.rem(lax.axis_index("sy"), 2) == 1


def has_y(step):
    place = lax.axis_index("sy") + step
    return (place >= 0) & (place < lax.axis_size("sy"))


def has_x(main):
    step = jnp.where(is_odd() == main, -1, 1)
    place = lax.axis_index("sx") + step
    return (place >= 0) & (place < lax.axis_size("sx"))


def neighbours(count):
    up = [(i, (i + 1) % count) for i in range(count)]
    return up, [(b, a) for a, b in up]


def spread3(w):
    return [w[0], w[0] + w[0] + w[1], w[0] + w[1] + w[1] + w[2]]


def cell_image(lines, values, rows):
    if values is None:
        return [-(rows[2] * lines[a]) for a in range(3)]
    total = rows[1] * (values[0] + values[1] + values[2])
    return [rows[0] * values[a] + total - rows[2] * lines[a] for a in range(3)]


def coef_rows(coef_ref, x, y, names):
    return [coef_ref[x, n, pl.ds(y, 1), :] for n in names]


def depth_sum(raw, rows):
    return (
        raw.astype(F32) * rows[0]
        + pltpu.roll(raw, 1, 1).astype(F32) * rows[1]
        + pltpu.roll(raw, 127, 1).astype(F32) * rows[2]
    )


def side(blocks):
    return jnp.concatenate(blocks, axis=1)


def fold(total):
    return total[:, :64] + total[:, 64:]


def fold_rows(total):
    return total[:64] + total[64:]


def pack_kernel(m_hbm, main_ref, corner_ref, south_ref, north_ref, sems):
    ext = m_hbm.shape[0]
    here = jnp.where(is_odd(), ext - 3, 0)
    there = jnp.where(is_odd(), 0, ext - 3)
    copies = [
        pltpu.make_async_copy(m_hbm.at[pl.ds(here, 3)], main_ref, sems.at[0]),
        pltpu.make_async_copy(
            m_hbm.at[pl.ds(there, 3), pl.ds(0, 3)], corner_ref.at[:, pl.ds(0, 3)], sems.at[1]
        ),
        pltpu.make_async_copy(
            m_hbm.at[pl.ds(there, 3), pl.ds(ext - 3, 3)], corner_ref.at[:, pl.ds(3, 3)], sems.at[2]
        ),
        pltpu.make_async_copy(m_hbm.at[:, pl.ds(ext - 3, 3)], south_ref, sems.at[3]),
        pltpu.make_async_copy(m_hbm.at[:, pl.ds(0, 3)], north_ref, sems.at[4]),
    ]
    for copy in copies:
        copy.start()
    for copy in copies:
        copy.wait()


def gate_kernel(*refs):
    pass


def own_kernel(
    m_ref, mid_ref, lo_ref, hi_ref,
    out_ref, coef_ref, img_ref, q_ref, acc_ref,
):
    ext = m_ref.shape[0]
    frame = ext + 2
    cell = mid_ref.shape[2]
    margin = (ext - cell) // 2
    odd = is_odd()

    q_ref[0] = jnp.zeros(q_ref.shape[1:], F32)
    lane = lax.broadcasted_iota(jnp.int32, (frame, 128), 1)
    place = lax.broadcasted_iota(jnp.int32, (frame, 128), 0)
    share_y = cover(
        place - margin - 1, lax.axis_index("sy"), cell, lax.axis_size("sy"), margin
    )

    def coefs(f, _):
        at = jnp.zeros((1, 128), jnp.int32) + (f - margin - 1)
        share = share_y * cover(at, lax.axis_index("sx"), cell, lax.axis_size("sx"), margin)
        cen, cpl, vol = [
            jnp.concatenate([lo_ref[f, n], mid_ref[f, n], hi_ref[f, n]], axis=0) for n in range(3)
        ]
        kap = cpl * share
        vol = vol * share * share
        coef_ref[f, MID] = kap + kap
        coef_ref[f, LOW] = jnp.where(lane == 0, 0.0, pltpu.roll(kap, 1, 1))
        coef_ref[f, UPP] = jnp.where(lane == 127, 0.0, pltpu.roll(kap, 127, 1))
        coef_ref[f, DIA] = cen * share * share - vol + 0.5 * kap * kap
        coef_ref[f, VOL] = vol
        coef_ref[f, OUT] = kap * (1.0 / 16.0)
        return 0

    lax.fori_loop(0, frame, coefs, 0)

    def first(f, chunk):
        rows = pl.ds(pl.multiple_of(chunk * 16, 16), 16)
        kaps = [coef_rows(coef_ref, f, g, (MID, LOW, UPP)) for g in range(1, ext + 1)]
        slot = f & 3
        for a in range(3):
            before = pair = None
            for j in range(ext):
                w = depth_sum(m_ref[f - 1, j * 3 + a, rows, :], kaps[j])
                if j == 0:
                    q_ref[slot, 0, a, rows, :] = w
                    pair = w
                else:
                    now = before + w
                    q_ref[slot, j, a, rows, :] = now + pair
                    pair = now
                before = w
            q_ref[slot, ext, a, rows, :] = pair + before
            q_ref[slot, ext + 1, a, rows, :] = before

    def image(f, chunk, edge=None, last=False):
        rows = pl.ds(pl.multiple_of(chunk * 16, 16), 16)
        low_rows = pl.ds(pl.multiple_of(64 + chunk * 16, 16), 16)
        for g in range(frame):
            values = None
            if 1 <= g <= ext and edge is None:
                values = [m_ref[f - 1, (g - 1) * 3 + a, rows, :].astype(F32) for a in range(3)]
            lines = []
            for a in range(3):
                if edge is not None:
                    lines.append(q_ref[edge & 3, g, a, rows, :])
                    continue
                mid = q_ref[f & 3, g, a, rows, :]
                one = q_ref[(f - 1) & 3, g, a, rows, :] + mid
                lines.append(one + (mid if last else mid + q_ref[(f + 1) & 3, g, a, rows, :]))
            result = cell_image(lines, values, coef_rows(coef_ref, f, g, (DIA, VOL, OUT)))
            for a in range(3):
                high = result[a].astype(BF16)
                img_ref[f, g * 3 + a, rows, :] = high
                img_ref[f, g * 3 + a, low_rows, :] = (result[a] - high.astype(F32)).astype(BF16)

    def dot(f, chunk):
        base = jnp.minimum(chunk * 8, ext * 3 - 8)
        tiles = [m_ref[jnp.maximum(f - 1, 0), base + i] for i in range(8)]
        for i in range(2):
            tiles[i] = jnp.where(chunk == 3, jnp.zeros_like(tiles[i]), tiles[i])
        lines = side([img_ref[f, base + 3 + i] for i in range(8)])
        acc_ref[...] += lax.dot_general(side(tiles), lines, NT, preferred_element_type=F32)

    def chunks(body):
        def step(chunk, _):
            body(chunk)
            return 0

        lax.fori_loop(0, 4, step, 0)

    chunks(lambda chunk: first(1, chunk))

    @pl.when(odd)
    def _():
        chunks(lambda chunk: image(0, chunk, 1))

    def inner(f, chunk):
        dot(f - 1, chunk)
        first(f + 1, chunk)
        image(f, chunk)

    def line(f, _):
        chunks(lambda chunk: inner(f, chunk))

        @pl.when(f == 1)
        def _():
            acc_ref[...] = jnp.zeros_like(acc_ref)

        return 0

    lax.fori_loop(1, ext, line, 0)

    def inner_last(chunk):
        dot(ext - 1, chunk)
        image(ext, chunk, None, True)

    chunks(inner_last)
    chunks(lambda chunk: dot(ext, chunk))

    @pl.when(jnp.logical_not(odd))
    def _():
        chunks(lambda chunk: image(ext + 1, chunk, ext))

    out_ref[...] = fold(acc_ref[...])


def rows_kernel(
    south_ref, north_ref, img_ref, coef_ref, out_ref, cimg_ref, z_ref, acc_ref
):
    ext = south_ref.shape[0]
    raw_refs = (south_ref, north_ref)
    acc_ref[...] = jnp.zeros_like(acc_ref)

    def dots(x):
        for s in range(2):
            right = side([raw_refs[s][x, j, a] for j in range(3) for a in range(3)])
            lines = side([img_ref[x + 1, s * (ext - 1) * 3 + i] for i in range(9)])
            acc_ref[s] += lax.dot_general(lines, right, NT, preferred_element_type=F32)

    def corner(s, t, chunk):
        raw_y = (2, 1, 0) if s == 0 else (0, 1, 2)
        raw_g = (2, 1, 0) if s == 0 else (9, 10, 11)
        img_g = (3, 2, 1) if s == 0 else (8, 9, 10)
        img_y = (2, 1, 0) if s == 0 else (0, 1, 2)
        raw_x = (0, 1, 2) if t == 0 else (9, 8, 7)
        raw_f = (1, 2, 3) if t == 0 else (10, 9, 8)
        img_f = (0, 1, 2) if t == 0 else (11, 10, 9)
        img_x = (0, 1, 2) if t == 0 else (2, 1, 0)
        rows = pl.ds(pl.multiple_of(chunk * 16, 16), 16)
        low_rows = pl.ds(pl.multiple_of(64 + chunk * 16, 16), 16)
        for a in range(3):
            across = []
            for c in range(3):
                w = [
                    depth_sum(
                        raw_refs[s][raw_x[c], raw_y[d], a, rows, :],
                        coef_rows(coef_ref, raw_f[c], raw_g[d], (MID, LOW, UPP)),
                    )
                    for d in range(3)
                ]
                across.append(spread3(w))
            for e in range(3):
                for c, value in enumerate(spread3([across[i][e] for i in range(3)])):
                    z_ref[s, c, e, a] = value
        for c in range(3):
            for e in range(3):
                values = None
                if c > 0 and e > 0:
                    values = [
                        raw_refs[s][raw_x[c - 1], raw_y[e - 1], a, rows, :].astype(F32)
                        for a in range(3)
                    ]
                image = cell_image(
                    [z_ref[s, c, e, a] for a in range(3)], values,
                    coef_rows(coef_ref, img_f[c], img_g[e], (DIA, VOL, OUT)),
                )
                for a in range(3):
                    tile = (img_x[c] * 3 + img_y[e]) * 3 + a
                    high = image[a].astype(BF16)
                    cimg_ref[t, s, tile, rows, :] = high
                    cimg_ref[t, s, tile, low_rows, :] = (image[a] - high.astype(F32)).astype(BF16)

    for t in range(2):

        def step(chunk, _, t=t):
            dots(t * 4 + chunk)
            corner(0, t, chunk)
            corner(1, t, chunk)
            return 0

        lax.fori_loop(0, 4, step, 0)
    for x in range(8, ext):
        dots(x)
    out_ref[...] = side([fold_rows(acc_ref[0]), fold_rows(acc_ref[1])])


def masked(there, block):
    return jnp.where(there, block, jnp.zeros_like(block))


def corner_dot(raw, img):
    left = side([raw(i, j, a) for i in range(3) for j in range(3) for a in range(3)])
    lines = side([img(i) for i in range(27)])
    return fold(lax.dot_general(left, lines, NT, preferred_element_type=F32))


def other_kernel(corner_ref, cimg_ref, own_ref, rows_ref, out_ref, keep_ref):
    t = is_odd().astype(jnp.int32)
    low, high, beside = has_y(-1), has_y(1), has_x(False)
    south = corner_dot(lambda i, j, a: corner_ref[i, j, a], lambda i: cimg_ref[t, 0, i])
    north = corner_dot(lambda i, j, a: corner_ref[i, j + 3, a], lambda i: cimg_ref[t, 1, i])
    around = rows_ref[...]
    out_ref[...] = side(
        [
            own_ref[...], masked(high, around[:, 64:]), masked(low & beside, south),
            masked(low, around[:, :64]),
        ]
    )
    keep_ref[...] = masked(high & beside, north)


def main_kernel(main_ref, img_ref, cimg_ref, early_ref, keep_ref, out_ref):
    t = 1 - is_odd().astype(jnp.int32)
    ext = main_ref.shape[1]
    start = jnp.where(is_odd(), 0, ext - 1)
    total = None
    for i in range(3):
        right = side([main_ref[i, j, a] for j in range(ext) for a in range(3)])
        lines = side([img_ref[start + i, 3 + j] for j in range(ext * 3)])
        part = lax.dot_general(lines, right, NT, preferred_element_type=F32)
        total = part if total is None else total + part
    south = corner_dot(lambda i, j, a: main_ref[i, j, a], lambda i: cimg_ref[t, 0, i])
    north = corner_dot(lambda i, j, a: main_ref[i, ext - 3 + j, a], lambda i: cimg_ref[t, 1, i])
    low, high, beside = has_y(-1), has_y(1), has_x(True)
    blocks = [
        masked(low & beside, south), masked(beside, fold_rows(total)), masked(high & beside, north)
    ]
    code = encode(side([early_ref[...]] + blocks + [keep_ref[...]]))
    for p in range(out_ref.shape[0]):
        out_ref[p] = code


def encode(rows):
    top = jnp.max(jnp.abs(rows), axis=(0, 1), keepdims=True)
    top = jnp.where(top > 0.0, jnp.maximum(top * 1.01, 2.0**-100), 1.0).astype(BF16).astype(F32)
    value = rows * (TOP / top)
    value2 = value * value
    value4 = value2 * value2
    power = value4 * value4 * value4
    code = jnp.where(rows < 0.0, -power, power)
    row = lax.broadcasted_iota(jnp.int32, rows.shape, 0)
    lane = lax.broadcasted_iota(jnp.int32, rows.shape, 1)
    return jnp.where((row == 0) & (lane == 1), top, code).astype(BF16)


def decode(code):
    value = code.astype(F32)
    first = value[:8, :128]
    row = lax.broadcasted_iota(jnp.int32, first.shape, 0)
    lane = lax.broadcasted_iota(jnp.int32, first.shape, 1)

    def pick(tile, i, j):
        return jnp.sum(jnp.where((row == i) & (lane == j), tile, 0.0), axis=(0, 1), keepdims=True)

    scale = pick(first, 0, 1) * (1.0 / TOP)
    root = jnp.exp(jnp.log(jnp.abs(value)) * (1.0 / 12.0)) * scale
    root = jnp.where(value < 0.0, -root, root)
    head = root[:8, :128]
    head = jnp.where((row == 0) & (lane == 1), pick(head, 1, 0), head)
    return root, head


def final_kernel(code_ref, out_hbm, e_ref, l_ref, o_ref, out_sems):
    odd = is_odd()
    none = jnp.zeros(e_ref.shape[1:], F32)
    for ref in (e_ref, l_ref):
        ref[0] = none
        ref[17] = none

    def read(p, _):
        root, head = decode(code_ref[p])
        e_ref[p + 1] = root[:, :256]
        l_ref[p + 1] = root[:, 256:]
        e_ref[p + 1, pl.ds(0, 8), pl.ds(0, 128)] = head
        return 0

    read(0, 0)

    def put(p):
        return pltpu.make_async_copy(o_ref.at[p], out_hbm.at[p], out_sems.at[p])

    low = lax.broadcasted_iota(jnp.int32, (64, 128), 1) < 64

    def turned(tile):
        return jnp.transpose(jnp.concatenate([tile, tile], axis=0))[64:]

    def join(lower, upper):
        return jnp.where(low, lower, upper)

    def tiles(ref, p):
        return ref[p, :, pl.ds(0, 128)], ref[p, :, pl.ds(128, 128)]

    def ahead(p):
        read(jnp.minimum(p + 1, 15), 0)

    def even(p, _):
        ahead(p)
        (e_one, e_two), (_, e_after) = tiles(e_ref, p + 1), tiles(e_ref, p + 2)
        (b_one, b_two), (l_one, _), (_, l_after) = [tiles(l_ref, p + i) for i in range(3)]
        o_ref[p, :, pl.ds(0, 512)] = side(
            [join(b_one, turned(b_one)), join(b_two, e_two), e_one, join(e_after, l_one)]
        )
        o_ref[p, :, pl.ds(512, 64)] = l_after[:, 64:]
        put(p).start()
        return 0

    def uneven(p, _):
        ahead(p)
        (_, e_before), (e_one, e_two) = tiles(e_ref, p), tiles(e_ref, p + 1)
        (_, b_two), (l_one, _), (a_one, a_two) = [tiles(l_ref, p + i) for i in range(3)]
        o_ref[p, :, pl.ds(0, 512)] = side(
            [
                join(e_before, l_one), join(pltpu.roll(b_two, 64, 1), e_two), e_one,
                join(a_one, turned(a_one)),
            ]
        )
        o_ref[p, :, pl.ds(512, 64)] = a_two[:, :64]
        put(p).start()
        return 0

    @pl.when(jnp.logical_not(odd))
    def _():
        lax.fori_loop(0, 16, even, 0, unroll=2)

    @pl.when(odd)
    def _():
        lax.fori_loop(0, 16, uneven, 0, unroll=2)

    for p in range(16):
        put(p).wait()


def any_spec():
    return pl.BlockSpec(memory_space=pl.ANY)


def vmem_spec():
    return pl.BlockSpec(memory_space=pltpu.VMEM)


def shape(*dims, dtype=F32):
    return jax.ShapeDtypeStruct(dims, dtype)


def call(kernel, out_shape, in_specs, out_specs, scratch, mib, name):
    return pl.pallas_call(
        kernel,
        out_shape=out_shape,
        in_specs=in_specs,
        out_specs=out_specs,
        scratch_shapes=scratch,
        compiler_params=pltpu.CompilerParams(vmem_limit_bytes=mib * MIB),
        cost_estimate=pl.CostEstimate(flops=1000, bytes_accessed=1000, transcendentals=0),
        name=name,
    )


def gate(values, others):
    count = len(values)
    return pl.pallas_call(
        gate_kernel,
        out_shape=[shape(*x.shape, dtype=x.dtype) for x in values],
        in_specs=[any_spec()] * (count + len(others)),
        out_specs=[any_spec()] * count,
        input_output_aliases={i: i for i in range(count)},
        compiler_params=pltpu.CompilerParams(vmem_limit_bytes=MIB),
        name="gate",
    )(*values, *others)


def coef_columns(centre, coupling, volume):
    own = jnp.stack([centre, coupling, volume], axis=1)
    up, down = neighbours(lax.axis_size("sx"))
    low = lax.ppermute(own[-2:], "sx", up)
    high = lax.ppermute(own[:2], "sx", down)
    return jnp.concatenate([low, own, high], axis=0)


def coef_edges(mid):
    up, down = neighbours(lax.axis_size("sy"))
    lo = lax.ppermute(mid[:, :, -2:], "sy", up)
    hi = lax.ppermute(mid[:, :, :2], "sy", down)
    return lo, hi


def local(modes, centre, coupling, volume):
    ext = modes.shape[0]
    nx = lax.axis_size("sx")
    ny = lax.axis_size("sy")
    mid = coef_columns(centre, coupling, volume)
    m = jnp.transpose(modes, (0, 1, 3, 2, 4))
    frame = ext + 2

    main, corner, south, north = call(
        pack_kernel,
        [
            shape(3, ext, 3, 64, 128, dtype=BF16),
            shape(3, 6, 3, 64, 128, dtype=BF16),
            shape(ext, 3, 3, 64, 128, dtype=BF16),
            shape(ext, 3, 3, 64, 128, dtype=BF16),
        ],
        [vmem_spec()],
        [vmem_spec()] * 4,
        [pltpu.SemaphoreType.DMA((5,))],
        8,
        "pack",
    )(m)
    main, corner, south, north, mid = gate((main, corner, south, north, mid), ())
    main_pairs, other_pairs = [], []
    for y in range(ny):
        for x in range(nx):
            lower, higher = x * ny + y, (x + 1) % nx * ny + y
            main_pairs.append((higher, lower) if y % 2 == 0 else (lower, higher))
            other_pairs.append((lower, higher) if y % 2 == 0 else (higher, lower))
    main = lax.ppermute(main, ("sx", "sy"), main_pairs)
    corner = lax.ppermute(corner, ("sx", "sy"), other_pairs)
    lo, hi = coef_edges(mid)
    south, north = gate((south, north), (lo, hi))
    up, down = neighbours(ny)
    south = lax.ppermute(south, "sy", up)
    north = lax.ppermute(north, "sy", down)

    own, coef, img = call(
        own_kernel,
        [
            shape(64, 64),
            shape(frame, 6, frame, 128),
            shape(frame, frame * 3, 128, 128, dtype=BF16),
        ],
        [vmem_spec()] * 4,
        [vmem_spec()] * 3,
        [
            pltpu.VMEM((4, frame, 3, 64, 128), F32),
            pltpu.VMEM((64, 128), F32),
        ],
        OWN_MIB,
        "own_gram",
    )(m.reshape(ext, ext * 3, 64, 128), mid, lo, hi)
    around, cimg = call(
        rows_kernel,
        [shape(64, 128), shape(2, 2, 27, 128, 128, dtype=BF16)],
        [vmem_spec()] * 4,
        [vmem_spec(), vmem_spec()],
        [
            pltpu.VMEM((2, 3, 3, 3, 16, 128), F32),
            pltpu.VMEM((2, 128, 64), F32),
        ],
        8,
        "row_gram",
    )(south, north, img, coef)
    early, keep = call(
        other_kernel,
        [shape(64, 256), shape(64, 64)],
        [vmem_spec()] * 4,
        [vmem_spec()] * 2,
        [],
        10,
        "corner_gram",
    )(corner, cimg, own, around)
    code = call(
        main_kernel,
        shape(nx, 64, 512, dtype=BF16),
        [vmem_spec()] * 5,
        vmem_spec(),
        [],
        8,
        "column_gram",
    )(main, img, cimg, early, keep)
    code = lax.all_to_all(code, "sx", 0, 0)
    out = call(
        final_kernel,
        shape(nx, 64, 576),
        [vmem_spec()],
        any_spec(),
        [
            pltpu.VMEM((nx + 2, 64, 256), F32),
            pltpu.VMEM((nx + 2, 64, 256), F32),
            pltpu.VMEM((nx, 64, 576), F32),
            pltpu.SemaphoreType.DMA((nx,)),
        ],
        12,
        "assemble",
    )(code)
    return out[None]


def solution(mesh):
    in_specs = (
        P("sx", "sy", None, None, None),
        P("sx", "sy", None),
        P("sx", "sy", None),
        P("sx", "sy", None),
    )
    out_specs = P("sy", None, None, None)
    return jax.shard_map(local, mesh=mesh, in_specs=in_specs, out_specs=out_specs, check_vma=False)
```

```python
import functools

import jax
import jax.numpy as jnp
from jax import lax
from jax.experimental import pallas as pl
from jax.experimental.pallas import tpu as pltpu
from jax.sharding import PartitionSpec as P

F32 = jnp.float32
BF16 = jnp.bfloat16
MID, LOW, UPP, DIA, VOL, OUT = range(6)
NT = (((1,), (1,)), ((), ()))
MIB = 1024 * 1024
TOP = 1024.0
OWN_MIB = 10


def cover(local, index, cell, count, margin):
    places = index * cell + local
    base = index + (local >= cell).astype(jnp.int32) - (local < 0).astype(jnp.int32)
    total = jnp.zeros(local.shape, jnp.int32)
    for step_off in (-1, 0, 1):
        owner = base + step_off
        inside = (
            (owner >= 0)
            & (owner < count)
            & (places >= owner * cell - margin)
            & (places < owner * cell + cell + margin)
        )
        total = total + inside.astype(jnp.int32)
    in_grid = (places >= 0) & (places < cell * count)
    safe = jnp.maximum(total, 1).astype(F32)
    return jnp.where(in_grid & (total > 0), 1.0 / safe, 0.0)


def is_odd():
    return lax.rem(lax.axis_index("sy"), 2) == 1


def has_y(step):
    place = lax.axis_index("sy") + step
    return (place >= 0) & (place < lax.axis_size("sy"))


def has_x(main):
    step = jnp.where(is_odd() == main, -1, 1)
    place = lax.axis_index("sx") + step
    return (place >= 0) & (place < lax.axis_size("sx"))


def neighbours(count):
    up = [(i, (i + 1) % count) for i in range(count)]
    return up, [(b, a) for a, b in up]


def spread3(w):
    return [w[0], w[0] + w[0] + w[1], w[0] + w[1] + w[1] + w[2]]


def cell_image(lines, values, rows):
    if values is None:
        return [-(rows[2] * lines[a]) for a in range(3)]
    total = rows[1] * (values[0] + values[1] + values[2])
    return [rows[0] * values[a] + total - rows[2] * lines[a] for a in range(3)]


def coef_rows(coef_ref, x, y, names):
    return [coef_ref[x, n, pl.ds(y, 1), :] for n in names]


def depth_sum(raw, rows):
    return (
        raw.astype(F32) * rows[0]
        + pltpu.roll(raw, 1, 1).astype(F32) * rows[1]
        + pltpu.roll(raw, 127, 1).astype(F32) * rows[2]
    )


def side(blocks):
    return jnp.concatenate(blocks, axis=1)


def fold(total):
    return total[:, :64] + total[:, 64:]


def fold_rows(total):
    return total[:64] + total[64:]


def pack_kernel(m_hbm, main_ref, corner_ref, south_ref, north_ref, sems):
    ext = m_hbm.shape[0]
    here = jnp.where(is_odd(), ext - 3, 0)
    there = jnp.where(is_odd(), 0, ext - 3)
    copies = [
        pltpu.make_async_copy(m_hbm.at[pl.ds(here, 3)], main_ref, sems.at[0]),
        pltpu.make_async_copy(
            m_hbm.at[pl.ds(there, 3), pl.ds(ext - 3, 3)], corner_ref, sems.at[1]
        ),
        pltpu.make_async_copy(m_hbm.at[:, pl.ds(ext - 3, 3)], south_ref, sems.at[2]),
        pltpu.make_async_copy(m_hbm.at[:, pl.ds(0, 3)], north_ref, sems.at[3]),
    ]
    for copy in copies:
        copy.start()
    for copy in copies:
        copy.wait()


def gate_kernel(*refs):
    pass


def own_kernel(
    m_ref, mid_ref, lo_ref, hi_ref,
    out_ref, coef_ref, img_ref, q_ref, acc_ref,
):
    ext = m_ref.shape[0]
    frame = ext + 2
    cell = mid_ref.shape[2]
    margin = (ext - cell) // 2
    odd = is_odd()

    q_ref[0] = jnp.zeros(q_ref.shape[1:], F32)
    lane = lax.broadcasted_iota(jnp.int32, (frame, 128), 1)
    place = lax.broadcasted_iota(jnp.int32, (frame, 128), 0)
    share_y = cover(
        place - margin - 1, lax.axis_index("sy"), cell, lax.axis_size("sy"), margin
    )

    def coefs(f, _):
        at = jnp.zeros((1, 128), jnp.int32) + (f - margin - 1)
        share = share_y * cover(at, lax.axis_index("sx"), cell, lax.axis_size("sx"), margin)
        cen, cpl, vol = [
            jnp.concatenate([lo_ref[f, n], mid_ref[f, n], hi_ref[f, n]], axis=0) for n in range(3)
        ]
        kap = cpl * share
        vol = vol * share * share
        coef_ref[f, MID] = kap + kap
        coef_ref[f, LOW] = jnp.where(lane == 0, 0.0, pltpu.roll(kap, 1, 1))
        coef_ref[f, UPP] = jnp.where(lane == 127, 0.0, pltpu.roll(kap, 127, 1))
        coef_ref[f, DIA] = cen * share * share - vol + 0.5 * kap * kap
        coef_ref[f, VOL] = vol
        coef_ref[f, OUT] = kap * (1.0 / 16.0)
        return 0

    lax.fori_loop(0, frame, coefs, 0, unroll=4)

    def first(f, chunk):
        rows = pl.ds(pl.multiple_of(chunk * 16, 16), 16)
        kaps = [coef_rows(coef_ref, f, g, (MID, LOW, UPP)) for g in range(1, ext + 1)]
        slot = f & 3
        for a in range(3):
            before = pair = None
            for j in range(ext):
                w = depth_sum(m_ref[f - 1, j * 3 + a, rows, :], kaps[j])
                if j == 0:
                    q_ref[slot, 0, a, rows, :] = w
                    pair = w
                else:
                    now = before + w
                    q_ref[slot, j, a, rows, :] = now + pair
                    pair = now
                before = w
            q_ref[slot, ext, a, rows, :] = pair + before
            q_ref[slot, ext + 1, a, rows, :] = before

    def image(f, chunk, edge=None, last=False):
        rows = pl.ds(pl.multiple_of(chunk * 16, 16), 16)
        low_rows = pl.ds(pl.multiple_of(64 + chunk * 16, 16), 16)
        for g in range(frame):
            values = None
            if 1 <= g <= ext and edge is None:
                values = [m_ref[f - 1, (g - 1) * 3 + a, rows, :].astype(F32) for a in range(3)]
            lines = []
            for a in range(3):
                if edge is not None:
                    lines.append(q_ref[edge & 3, g, a, rows, :])
                    continue
                mid = q_ref[f & 3, g, a, rows, :]
                one = q_ref[(f - 1) & 3, g, a, rows, :] + mid
                lines.append(one + (mid if last else mid + q_ref[(f + 1) & 3, g, a, rows, :]))
            result = cell_image(lines, values, coef_rows(coef_ref, f, g, (DIA, VOL, OUT)))
            for a in range(3):
                high = result[a].astype(BF16)
                img_ref[f, g * 3 + a, rows, :] = high
                img_ref[f, g * 3 + a, low_rows, :] = (result[a] - high.astype(F32)).astype(BF16)

    def dot(f, chunk):
        base = jnp.minimum(chunk * 8, ext * 3 - 8)
        tiles = [m_ref[jnp.maximum(f - 1, 0), base + i] for i in range(8)]
        for i in range(2):
            tiles[i] = jnp.where(chunk == 3, jnp.zeros_like(tiles[i]), tiles[i])
        lines = side([img_ref[f, base + 3 + i] for i in range(8)])
        acc_ref[...] += lax.dot_general(side(tiles), lines, NT, preferred_element_type=F32)

    def chunks(body):
        def step(chunk, _):
            body(chunk)
            return 0

        lax.fori_loop(0, 4, step, 0, unroll=4)

    chunks(lambda chunk: first(1, chunk))

    @pl.when(odd)
    def _():
        chunks(lambda chunk: image(0, chunk, 1))

    def inner(f, chunk):
        dot(f - 1, chunk)
        first(f + 1, chunk)
        image(f, chunk)

    def line(f, _):
        chunks(lambda chunk: inner(f, chunk))

        @pl.when(f == 1)
        def _():
            acc_ref[...] = jnp.zeros_like(acc_ref)

        return 0

    lax.fori_loop(1, ext, line, 0)

    def inner_last(chunk):
        dot(ext - 1, chunk)
        image(ext, chunk, None, True)

    chunks(inner_last)
    chunks(lambda chunk: dot(ext, chunk))

    @pl.when(jnp.logical_not(odd))
    def _():
        chunks(lambda chunk: image(ext + 1, chunk, ext))

    out_ref[...] = fold(acc_ref[...])


def rows_kernel(
    south_ref, north_ref, img_ref, coef_ref, out_ref, cimg_ref, z_ref, acc_ref
):
    ext = south_ref.shape[0]
    raw_refs = (south_ref, north_ref)
    acc_ref[...] = jnp.zeros_like(acc_ref)

    def dots(x):
        for s in range(2):
            right = side([raw_refs[s][x, j, a] for j in range(3) for a in range(3)])
            lines = side([img_ref[x + 1, s * (ext - 1) * 3 + i] for i in range(9)])
            acc_ref[s] += lax.dot_general(lines, right, NT, preferred_element_type=F32)

    def corner(s, t, chunk):
        raw_y = (2, 1, 0) if s == 0 else (0, 1, 2)
        raw_g = (2, 1, 0) if s == 0 else (9, 10, 11)
        img_g = (3, 2, 1) if s == 0 else (8, 9, 10)
        img_y = (2, 1, 0) if s == 0 else (0, 1, 2)
        raw_x = (0, 1, 2) if t == 0 else (9, 8, 7)
        raw_f = (1, 2, 3) if t == 0 else (10, 9, 8)
        img_f = (0, 1, 2) if t == 0 else (11, 10, 9)
        img_x = (0, 1, 2) if t == 0 else (2, 1, 0)
        rows = pl.ds(pl.multiple_of(chunk * 16, 16), 16)
        low_rows = pl.ds(pl.multiple_of(64 + chunk * 16, 16), 16)
        for a in range(3):
            across = []
            for c in range(3):
                w = [
                    depth_sum(
                        raw_refs[s][raw_x[c], raw_y[d], a, rows, :],
                        coef_rows(coef_ref, raw_f[c], raw_g[d], (MID, LOW, UPP)),
                    )
                    for d in range(3)
                ]
                across.append(spread3(w))
            for e in range(3):
                for c, value in enumerate(spread3([across[i][e] for i in range(3)])):
                    z_ref[s, c, e, a] = value
        for c in range(3):
            for e in range(3):
                values = None
                if c > 0 and e > 0:
                    values = [
                        raw_refs[s][raw_x[c - 1], raw_y[e - 1], a, rows, :].astype(F32)
                        for a in range(3)
                    ]
                image = cell_image(
                    [z_ref[s, c, e, a] for a in range(3)], values,
                    coef_rows(coef_ref, img_f[c], img_g[e], (DIA, VOL, OUT)),
                )
                for a in range(3):
                    tile = (img_x[c] * 3 + img_y[e]) * 3 + a
                    high = image[a].astype(BF16)
                    cimg_ref[t, s, tile, rows, :] = high
                    cimg_ref[t, s, tile, low_rows, :] = (image[a] - high.astype(F32)).astype(BF16)

    for t in range(2):

        def step(chunk, _, t=t):
            dots(t * 4 + chunk)
            corner(0, t, chunk)
            corner(1, t, chunk)
            return 0

        lax.fori_loop(0, 4, step, 0, unroll=2)
    for x in range(8, ext):
        dots(x)
    out_ref[...] = side([fold_rows(acc_ref[0]), fold_rows(acc_ref[1])])


def masked(there, block):
    return jnp.where(there, block, jnp.zeros_like(block))


def corner_dot(raw, img):
    left = side([raw(i, j, a) for i in range(3) for j in range(3) for a in range(3)])
    lines = side([img(i) for i in range(27)])
    return fold(lax.dot_general(left, lines, NT, preferred_element_type=F32))


def other_kernel(corner_ref, cimg_ref, keep_ref, turned_ref):
    t = is_odd().astype(jnp.int32)
    there = has_y(1) & has_x(False)
    cells = [(i, j, a) for i in range(3) for j in range(3) for a in range(3)]
    raw = side([corner_ref[c] for c in cells])
    lines = side([cimg_ref[t, 1, i] for i in range(27)])
    keep_ref[...] = masked(there, fold(lax.dot_general(raw, lines, NT, preferred_element_type=F32)))
    turned_ref[...] = masked(
        there, fold_rows(lax.dot_general(lines, raw, NT, preferred_element_type=F32))
    )


def main_kernel(main_ref, img_ref, cimg_ref, own_ref, rows_ref, below_ref, keep_ref, out_ref):
    t = 1 - is_odd().astype(jnp.int32)
    ext = main_ref.shape[1]
    start = jnp.where(is_odd(), 0, ext - 1)
    total = None
    for i in range(3):
        right = side([main_ref[i, j, a] for j in range(ext) for a in range(3)])
        lines = side([img_ref[start + i, 3 + j] for j in range(ext * 3)])
        part = lax.dot_general(lines, right, NT, preferred_element_type=F32)
        total = part if total is None else total + part
    south = corner_dot(lambda i, j, a: main_ref[i, j, a], lambda i: cimg_ref[t, 0, i])
    north = corner_dot(lambda i, j, a: main_ref[i, ext - 3 + j, a], lambda i: cimg_ref[t, 1, i])
    low, high, beside = has_y(-1), has_y(1), has_x(True)
    around = rows_ref[...]
    blocks = [
        own_ref[...], masked(high, around[:, 64:]), below_ref[...], masked(low, around[:, :64]),
        masked(low & beside, south), masked(beside, fold_rows(total)),
        masked(high & beside, north), keep_ref[...],
    ]
    code = encode(side(blocks))
    for p in range(out_ref.shape[0]):
        out_ref[p] = code


def encode(rows):
    top = jnp.max(jnp.abs(rows), axis=(0, 1), keepdims=True)
    top = jnp.where(top > 0.0, jnp.maximum(top * 1.01, 2.0**-100), 1.0).astype(BF16).astype(F32)
    value = rows * (TOP / top)
    value2 = value * value
    value4 = value2 * value2
    power = value4 * value4 * value4
    code = jnp.where(rows < 0.0, -power, power)
    row = lax.broadcasted_iota(jnp.int32, rows.shape, 0)
    lane = lax.broadcasted_iota(jnp.int32, rows.shape, 1)
    return jnp.where((row == 0) & (lane == 1), top, code).astype(BF16)


def decode(code):
    value = code.astype(F32)
    first = value[:8, :128]
    row = lax.broadcasted_iota(jnp.int32, first.shape, 0)
    lane = lax.broadcasted_iota(jnp.int32, first.shape, 1)

    def pick(tile, i, j):
        return jnp.sum(jnp.where((row == i) & (lane == j), tile, 0.0), axis=(0, 1), keepdims=True)

    scale = pick(first, 0, 1) * (1.0 / TOP)
    root = jnp.exp(jnp.log(jnp.abs(value)) * (1.0 / 12.0)) * scale
    root = jnp.where(value < 0.0, -root, root)
    head = root[:8, :128]
    head = jnp.where((row == 0) & (lane == 1), pick(head, 1, 0), head)
    return root, head


def final_kernel(code_ref, out_hbm, e_ref, l_ref, o_ref, out_sems):
    odd = is_odd()
    none = jnp.zeros(e_ref.shape[1:], F32)
    for ref in (e_ref, l_ref):
        ref[0] = none
        ref[17] = none

    def read(p, _):
        root, head = decode(code_ref[p])
        e_ref[p + 1] = root[:, :256]
        l_ref[p + 1] = root[:, 256:]
        e_ref[p + 1, pl.ds(0, 8), pl.ds(0, 128)] = head
        return 0

    read(0, 0)

    def put(p):
        return pltpu.make_async_copy(o_ref.at[p], out_hbm.at[p], out_sems.at[p])

    low = lax.broadcasted_iota(jnp.int32, (64, 128), 1) < 64

    def turned(tile):
        return jnp.transpose(jnp.concatenate([tile, tile], axis=0))[64:]

    def join(lower, upper):
        return jnp.where(low, lower, upper)

    def tiles(ref, p):
        return ref[p, :, pl.ds(0, 128)], ref[p, :, pl.ds(128, 128)]

    def ahead(p):
        read(jnp.minimum(p + 1, 15), 0)

    def even(p, _):
        ahead(p)
        e_one, e_two = tiles(e_ref, p + 1)
        (b_one, b_two), (l_one, _), (_, l_after) = [tiles(l_ref, p + i) for i in range(3)]
        o_ref[p, :, pl.ds(0, 512)] = side(
            [join(b_one, turned(b_one)), join(b_two, e_two), e_one, join(e_two, l_one)]
        )
        o_ref[p, :, pl.ds(512, 64)] = l_after[:, 64:]
        put(p).start()
        return 0

    def uneven(p, _):
        ahead(p)
        e_one, e_two = tiles(e_ref, p + 1)
        (_, b_two), (l_one, _), (a_one, a_two) = [tiles(l_ref, p + i) for i in range(3)]
        o_ref[p, :, pl.ds(0, 512)] = side(
            [
                join(e_two, l_one), join(pltpu.roll(b_two, 64, 1), e_two), e_one,
                join(a_one, turned(a_one)),
            ]
        )
        o_ref[p, :, pl.ds(512, 64)] = a_two[:, :64]
        put(p).start()
        return 0

    @pl.when(jnp.logical_not(odd))
    def _():
        lax.fori_loop(0, 16, even, 0, unroll=2)

    @pl.when(odd)
    def _():
        lax.fori_loop(0, 16, uneven, 0, unroll=2)

    for p in range(16):
        put(p).wait()


def any_spec():
    return pl.BlockSpec(memory_space=pl.ANY)


def vmem_spec():
    return pl.BlockSpec(memory_space=pltpu.VMEM)


def shape(*dims, dtype=F32):
    return jax.ShapeDtypeStruct(dims, dtype)


def call(kernel, out_shape, in_specs, out_specs, scratch, mib, name):
    return pl.pallas_call(
        kernel,
        out_shape=out_shape,
        in_specs=in_specs,
        out_specs=out_specs,
        scratch_shapes=scratch,
        compiler_params=pltpu.CompilerParams(vmem_limit_bytes=mib * MIB),
        cost_estimate=pl.CostEstimate(flops=1000, bytes_accessed=1000, transcendentals=0),
        name=name,
    )


def gate(values, others):
    count = len(values)
    return pl.pallas_call(
        gate_kernel,
        out_shape=[shape(*x.shape, dtype=x.dtype) for x in values],
        in_specs=[any_spec()] * (count + len(others)),
        out_specs=[any_spec()] * count,
        input_output_aliases={i: i for i in range(count)},
        compiler_params=pltpu.CompilerParams(vmem_limit_bytes=MIB),
        name="gate",
    )(*values, *others)


def coef_columns(centre, coupling, volume):
    own = jnp.stack([centre, coupling, volume], axis=1)
    up, down = neighbours(lax.axis_size("sx"))
    low = lax.ppermute(own[-2:], "sx", up)
    high = lax.ppermute(own[:2], "sx", down)
    return jnp.concatenate([low, own, high], axis=0)


def coef_edges(mid):
    up, down = neighbours(lax.axis_size("sy"))
    lo = lax.ppermute(mid[:, :, -2:], "sy", up)
    hi = lax.ppermute(mid[:, :, :2], "sy", down)
    return lo, hi


def local(modes, centre, coupling, volume):
    ext = modes.shape[0]
    nx = lax.axis_size("sx")
    ny = lax.axis_size("sy")
    mid = coef_columns(centre, coupling, volume)
    m = jnp.transpose(modes, (0, 1, 3, 2, 4))
    frame = ext + 2

    main, corner, south, north = call(
        pack_kernel,
        [
            shape(3, ext, 3, 64, 128, dtype=BF16),
            shape(3, 3, 3, 64, 128, dtype=BF16),
            shape(ext, 3, 3, 64, 128, dtype=BF16),
            shape(ext, 3, 3, 64, 128, dtype=BF16),
        ],
        [vmem_spec()],
        [vmem_spec()] * 4,
        [pltpu.SemaphoreType.DMA((4,))],
        8,
        "pack",
    )(m)
    main, corner, south, north, mid = gate((main, corner, south, north, mid), ())
    main_pairs, other_pairs = [], []
    for y in range(ny):
        for x in range(nx):
            lower, higher = x * ny + y, (x + 1) % nx * ny + y
            main_pairs.append((higher, lower) if y % 2 == 0 else (lower, higher))
            other_pairs.append((lower, higher) if y % 2 == 0 else (higher, lower))
    main = lax.ppermute(main, ("sx", "sy"), main_pairs)
    corner = lax.ppermute(corner, ("sx", "sy"), other_pairs)
    lo, hi = coef_edges(mid)
    south, north = gate((south, north), (lo, hi))
    up, down = neighbours(ny)
    south = lax.ppermute(south, "sy", up)
    north = lax.ppermute(north, "sy", down)

    own, coef, img = call(
        own_kernel,
        [
            shape(64, 64),
            shape(frame, 6, frame, 128),
            shape(frame, frame * 3, 128, 128, dtype=BF16),
        ],
        [vmem_spec()] * 4,
        [vmem_spec()] * 3,
        [
            pltpu.VMEM((4, frame, 3, 64, 128), F32),
            pltpu.VMEM((64, 128), F32),
        ],
        OWN_MIB,
        "own_gram",
    )(m.reshape(ext, ext * 3, 64, 128), mid, lo, hi)
    around, cimg = call(
        rows_kernel,
        [shape(64, 128), shape(2, 2, 27, 128, 128, dtype=BF16)],
        [vmem_spec()] * 4,
        [vmem_spec(), vmem_spec()],
        [
            pltpu.VMEM((2, 3, 3, 3, 16, 128), F32),
            pltpu.VMEM((2, 128, 64), F32),
        ],
        8,
        "row_gram",
    )(south, north, img, coef)
    keep, turned = call(
        other_kernel,
        [shape(64, 64), shape(64, 64)],
        [vmem_spec()] * 2,
        [vmem_spec()] * 2,
        [],
        8,
        "corner_gram",
    )(corner, cimg)
    below = lax.ppermute(turned, "sy", up)
    code = call(
        main_kernel,
        shape(nx, 64, 512, dtype=BF16),
        [vmem_spec()] * 7,
        vmem_spec(),
        [],
        8,
        "column_gram",
    )(main, img, cimg, own, around, below, keep)
    code = lax.all_to_all(code, "sx", 0, 0)
    out = call(
        final_kernel,
        shape(nx, 64, 576),
        [vmem_spec()],
        any_spec(),
        [
            pltpu.VMEM((nx + 2, 64, 256), F32),
            pltpu.VMEM((nx + 2, 64, 256), F32),
            pltpu.VMEM((nx, 64, 576), F32),
            pltpu.SemaphoreType.DMA((nx,)),
        ],
        12,
        "assemble",
    )(code)
    return out[None]


def solution(mesh):
    in_specs = (
        P("sx", "sy", None, None, None),
        P("sx", "sy", None),
        P("sx", "sy", None),
        P("sx", "sy", None),
    )
    out_specs = P("sy", None, None, None)
    return jax.shard_map(local, mesh=mesh, in_specs=in_specs, out_specs=out_specs, check_vma=False)
```

```python
import functools

import jax
import jax.numpy as jnp
from jax import lax
from jax.experimental import pallas as pl
from jax.experimental.pallas import tpu as pltpu
from jax.sharding import PartitionSpec as P

F32 = jnp.float32
BF16 = jnp.bfloat16
MID, LOW, UPP, DIA, VOL, OUT = range(6)
NT = (((1,), (1,)), ((), ()))
MIB = 1024 * 1024
TOP = 1024.0
OWN_MIB = 10


def cover(local, index, cell, count, margin):
    places = index * cell + local
    base = index + (local >= cell).astype(jnp.int32) - (local < 0).astype(jnp.int32)
    total = jnp.zeros(local.shape, jnp.int32)
    for step_off in (-1, 0, 1):
        owner = base + step_off
        inside = (
            (owner >= 0)
            & (owner < count)
            & (places >= owner * cell - margin)
            & (places < owner * cell + cell + margin)
        )
        total = total + inside.astype(jnp.int32)
    in_grid = (places >= 0) & (places < cell * count)
    safe = jnp.maximum(total, 1).astype(F32)
    return jnp.where(in_grid & (total > 0), 1.0 / safe, 0.0)


def is_odd():
    return lax.rem(lax.axis_index("sy"), 2) == 1


def has_y(step):
    place = lax.axis_index("sy") + step
    return (place >= 0) & (place < lax.axis_size("sy"))


def has_x(main):
    step = jnp.where(is_odd() == main, -1, 1)
    place = lax.axis_index("sx") + step
    return (place >= 0) & (place < lax.axis_size("sx"))


def neighbours(count):
    up = [(i, (i + 1) % count) for i in range(count)]
    return up, [(b, a) for a, b in up]


def spread3(w):
    return [w[0], w[0] + w[0] + w[1], w[0] + w[1] + w[1] + w[2]]


def cell_image(lines, values, rows):
    if values is None:
        return [-(rows[2] * lines[a]) for a in range(3)]
    total = rows[1] * (values[0] + values[1] + values[2])
    return [rows[0] * values[a] + total - rows[2] * lines[a] for a in range(3)]


def coef_rows(coef_ref, x, y, names):
    return [coef_ref[x, n, pl.ds(y, 1), :] for n in names]


def depth_sum(raw, rows):
    return (
        raw.astype(F32) * rows[0]
        + pltpu.roll(raw, 1, 1).astype(F32) * rows[1]
        + pltpu.roll(raw, 127, 1).astype(F32) * rows[2]
    )


def side(blocks):
    return jnp.concatenate(blocks, axis=1)


def fold(total):
    return total[:, :64] + total[:, 64:]


def fold_rows(total):
    return total[:64] + total[64:]


def pack_kernel(m_hbm, main_ref, corner_ref, south_ref, north_ref, sems):
    ext = m_hbm.shape[0]
    here = jnp.where(is_odd(), ext - 3, 0)
    there = jnp.where(is_odd(), 0, ext - 3)
    copies = [
        pltpu.make_async_copy(m_hbm.at[here + i], main_ref.at[pl.ds(i * ext, ext)], sems.at[4 + i])
        for i in range(3)
    ]
    main_ref[3 * ext] = jnp.zeros(main_ref.shape[1:], BF16)
    copies += [
        pltpu.make_async_copy(
            m_hbm.at[pl.ds(there, 3), pl.ds(ext - 3, 3)], corner_ref, sems.at[1]
        ),
        pltpu.make_async_copy(m_hbm.at[:, pl.ds(ext - 3, 3)], south_ref, sems.at[2]),
        pltpu.make_async_copy(m_hbm.at[:, pl.ds(0, 3)], north_ref, sems.at[3]),
    ]
    for copy in copies:
        copy.start()
    for copy in copies:
        copy.wait()


def gate_kernel(*refs):
    pass


def own_kernel(
    m_ref, mid_ref, lo_ref, hi_ref,
    out_ref, coef_ref, img_ref, q_ref, acc_ref,
):
    ext = m_ref.shape[0]
    frame = ext + 2
    cell = mid_ref.shape[2]
    margin = (ext - cell) // 2
    odd = is_odd()

    q_ref[0] = jnp.zeros(q_ref.shape[1:], F32)
    lane = lax.broadcasted_iota(jnp.int32, (frame, 128), 1)
    place = lax.broadcasted_iota(jnp.int32, (frame, 128), 0)
    share_y = cover(
        place - margin - 1, lax.axis_index("sy"), cell, lax.axis_size("sy"), margin
    )

    def coefs(f, _):
        at = jnp.zeros((1, 128), jnp.int32) + (f - margin - 1)
        share = share_y * cover(at, lax.axis_index("sx"), cell, lax.axis_size("sx"), margin)
        cen, cpl, vol = [
            jnp.concatenate([lo_ref[f, n], mid_ref[f, n], hi_ref[f, n]], axis=0) for n in range(3)
        ]
        kap = cpl * share
        vol = vol * share * share
        coef_ref[f, MID] = kap + kap
        coef_ref[f, LOW] = jnp.where(lane == 0, 0.0, pltpu.roll(kap, 1, 1))
        coef_ref[f, UPP] = jnp.where(lane == 127, 0.0, pltpu.roll(kap, 127, 1))
        coef_ref[f, DIA] = cen * share * share - vol + 0.5 * kap * kap
        coef_ref[f, VOL] = vol
        coef_ref[f, OUT] = kap * (1.0 / 16.0)
        return 0

    lax.fori_loop(0, frame, coefs, 0, unroll=4)

    def first(f, chunk):
        rows = pl.ds(pl.multiple_of(chunk * 16, 16), 16)
        kaps = [coef_rows(coef_ref, f, g, (MID, LOW, UPP)) for g in range(1, ext + 1)]
        slot = f & 3
        for a in range(3):
            before = pair = None
            for j in range(ext):
                w = depth_sum(m_ref[f - 1, j * 3 + a, rows, :], kaps[j])
                if j == 0:
                    q_ref[slot, 0, a, rows, :] = w
                    pair = w
                else:
                    now = before + w
                    q_ref[slot, j, a, rows, :] = now + pair
                    pair = now
                before = w
            q_ref[slot, ext, a, rows, :] = pair + before
            q_ref[slot, ext + 1, a, rows, :] = before

    def image(f, chunk, edge=None, last=False):
        rows = pl.ds(pl.multiple_of(chunk * 16, 16), 16)
        low_rows = pl.ds(pl.multiple_of(64 + chunk * 16, 16), 16)
        for g in range(frame) if edge is None else range(1, ext + 1):
            values = None
            if 1 <= g <= ext and edge is None:
                values = [m_ref[f - 1, (g - 1) * 3 + a, rows, :].astype(F32) for a in range(3)]
            lines = []
            for a in range(3):
                if edge is not None:
                    lines.append(q_ref[edge & 3, g, a, rows, :])
                    continue
                mid = q_ref[f & 3, g, a, rows, :]
                one = q_ref[(f - 1) & 3, g, a, rows, :] + mid
                lines.append(one + (mid if last else mid + q_ref[(f + 1) & 3, g, a, rows, :]))
            result = cell_image(lines, values, coef_rows(coef_ref, f, g, (DIA, VOL, OUT)))
            for a in range(3):
                high = result[a].astype(BF16)
                img_ref[f, g * 3 + a, rows, :] = high
                img_ref[f, g * 3 + a, low_rows, :] = (result[a] - high.astype(F32)).astype(BF16)

    def dot(f, chunk):
        base = jnp.minimum(chunk * 8, ext * 3 - 8)
        tiles = [m_ref[jnp.maximum(f - 1, 0), base + i] for i in range(8)]
        for i in range(2):
            tiles[i] = jnp.where(chunk == 3, jnp.zeros_like(tiles[i]), tiles[i])
        lines = side([img_ref[f, base + 3 + i] for i in range(8)])
        acc_ref[...] += lax.dot_general(side(tiles), lines, NT, preferred_element_type=F32)

    def chunks(body):
        def step(chunk, _):
            body(chunk)
            return 0

        lax.fori_loop(0, 4, step, 0, unroll=4)

    chunks(lambda chunk: first(1, chunk))

    @pl.when(odd)
    def _():
        chunks(lambda chunk: image(0, chunk, 1))

    def inner(f, chunk):
        dot(f - 1, chunk)
        first(f + 1, chunk)
        image(f, chunk)

    def line(f, _):
        chunks(lambda chunk: inner(f, chunk))

        @pl.when(f == 1)
        def _():
            acc_ref[...] = jnp.zeros_like(acc_ref)

        return 0

    lax.fori_loop(1, ext, line, 0)

    def inner_last(chunk):
        dot(ext - 1, chunk)
        image(ext, chunk, None, True)

    chunks(inner_last)
    @pl.when(odd)
    def _():
        chunks(lambda chunk: dot(ext, chunk))

    @pl.when(jnp.logical_not(odd))
    def _():
        def inner_rim(chunk):
            dot(ext, chunk)
            image(ext + 1, chunk, ext)

        chunks(inner_rim)

    out_ref[...] = fold(acc_ref[...])


def rows_kernel(
    south_ref, north_ref, img_ref, coef_ref, out_ref, cimg_ref, z_ref, acc_ref
):
    ext = south_ref.shape[0]
    raw_refs = (south_ref, north_ref)
    acc_ref[...] = jnp.zeros_like(acc_ref)

    def dots(x):
        for s in range(2):
            right = side([raw_refs[s][x, j, a] for j in range(3) for a in range(3)])
            lines = side([img_ref[x + 1, s * (ext - 1) * 3 + i] for i in range(9)])
            acc_ref[s] += lax.dot_general(lines, right, NT, preferred_element_type=F32)

    def corner(s, t, chunk, use):
        raw_y = (2, 1, 0) if s == 0 else (0, 1, 2)
        raw_g = (2, 1, 0) if s == 0 else (9, 10, 11)
        img_g = (3, 2, 1) if s == 0 else (8, 9, 10)
        img_y = (2, 1, 0) if s == 0 else (0, 1, 2)
        raw_x = [c + t * (ext - 1 - 2 * c) for c in range(3)]
        raw_f = [1 + c + t * (ext - 1 - 2 * c) for c in range(3)]
        img_f = [c + t * (ext + 1 - 2 * c) for c in range(3)]
        img_x = [c + t * (2 - 2 * c) for c in range(3)]
        rows = pl.ds(pl.multiple_of(chunk * 16, 16), 16)
        low_rows = pl.ds(pl.multiple_of(64 + chunk * 16, 16), 16)
        for a in range(3):
            across = []
            for c in range(3):
                w = [
                    depth_sum(
                        raw_refs[s][raw_x[c], raw_y[d], a, rows, :],
                        coef_rows(coef_ref, raw_f[c], raw_g[d], (MID, LOW, UPP)),
                    )
                    for d in range(3)
                ]
                across.append(spread3(w))
            for e in range(3):
                for c, value in enumerate(spread3([across[i][e] for i in range(3)])):
                    z_ref[use, c, e, a] = value
        for c in range(3):
            for e in range(3):
                values = None
                if c > 0 and e > 0:
                    values = [
                        raw_refs[s][raw_x[c - 1], raw_y[e - 1], a, rows, :].astype(F32)
                        for a in range(3)
                    ]
                image = cell_image(
                    [z_ref[use, c, e, a] for a in range(3)], values,
                    coef_rows(coef_ref, img_f[c], img_g[e], (DIA, VOL, OUT)),
                )
                for a in range(3):
                    tile = (img_x[c] * 3 + img_y[e]) * 3 + a
                    high = image[a].astype(BF16)
                    cimg_ref[t, s, tile, rows, :] = high
                    cimg_ref[t, s, tile, low_rows, :] = (image[a] - high.astype(F32)).astype(BF16)

    main_side = 1 - is_odd().astype(jnp.int32)

    def step(chunk, _):
        dots(2 * chunk)
        dots(2 * chunk + 1)
        corner(0, main_side, chunk, 0)
        corner(1, 0, chunk, 1)
        corner(1, 1, chunk, 2)
        return 0

    lax.fori_loop(0, 4, step, 0, unroll=2)
    for x in range(8, ext):
        dots(x)
    out_ref[...] = side([fold_rows(acc_ref[0]), fold_rows(acc_ref[1])])


def masked(there, block):
    return jnp.where(there, block, jnp.zeros_like(block))


def corner_dot(raw, img):
    left = side([raw(i, j, a) for i in range(3) for j in range(3) for a in range(3)])
    lines = side([img(i) for i in range(27)])
    return fold(lax.dot_general(left, lines, NT, preferred_element_type=F32))


def other_kernel(corner_ref, cimg_ref, keep_ref, turned_ref):
    t = is_odd().astype(jnp.int32)
    there = has_y(1) & has_x(False)
    cells = [(i, j, a) for i in range(3) for j in range(3) for a in range(3)]
    raw = side([corner_ref[c] for c in cells])
    lines = side([cimg_ref[t, 1, i] for i in range(27)])
    keep_ref[...] = masked(there, fold(lax.dot_general(raw, lines, NT, preferred_element_type=F32)))
    turned_ref[...] = masked(
        there, fold_rows(lax.dot_general(lines, raw, NT, preferred_element_type=F32))
    )


def main_kernel(main_ref, img_ref, cimg_ref, own_ref, rows_ref, below_ref, keep_ref, out_ref):
    t = 1 - is_odd().astype(jnp.int32)
    ext = main_ref.shape[0] // 3
    start = jnp.where(is_odd(), 0, ext - 1)
    total = None
    for i in range(3):
        right = side([main_ref[i * ext + j, a] for j in range(ext) for a in range(3)])
        lines = side([img_ref[start + i, 3 + j] for j in range(ext * 3)])
        part = lax.dot_general(lines, right, NT, preferred_element_type=F32)
        total = part if total is None else total + part
    south = corner_dot(lambda i, j, a: main_ref[i * ext + j, a], lambda i: cimg_ref[t, 0, i])
    north = corner_dot(lambda i, j, a: main_ref[i * ext + ext - 3 + j, a], lambda i: cimg_ref[t, 1, i])
    low, high, beside = has_y(-1), has_y(1), has_x(True)
    around = rows_ref[...]
    blocks = [
        own_ref[...], masked(high, around[:, 64:]), below_ref[...], masked(low, around[:, :64]),
        masked(low & beside, south), masked(beside, fold_rows(total)),
        masked(high & beside, north), keep_ref[...],
    ]
    code = encode(side(blocks))
    for p in range(out_ref.shape[0]):
        out_ref[p] = code


def encode(rows):
    top = jnp.max(jnp.abs(rows), axis=(0, 1), keepdims=True)
    top = jnp.where(top > 0.0, jnp.maximum(top * 1.01, 2.0**-100), 1.0).astype(BF16).astype(F32)
    value = rows * (TOP / top)
    value2 = value * value
    value4 = value2 * value2
    power = value4 * value4 * value4
    code = jnp.where(rows < 0.0, -power, power)
    row = lax.broadcasted_iota(jnp.int32, rows.shape, 0)
    lane = lax.broadcasted_iota(jnp.int32, rows.shape, 1)
    return jnp.where((row == 0) & (lane == 1), top, code).astype(BF16)


def decode(code):
    value = code.astype(F32)
    first = value[:8, :128]
    row = lax.broadcasted_iota(jnp.int32, first.shape, 0)
    lane = lax.broadcasted_iota(jnp.int32, first.shape, 1)

    def pick(tile, i, j):
        return jnp.sum(jnp.where((row == i) & (lane == j), tile, 0.0), axis=(0, 1), keepdims=True)

    scale = pick(first, 0, 1) * (1.0 / TOP)
    root = jnp.exp(jnp.log(jnp.abs(value)) * (1.0 / 12.0)) * scale
    root = jnp.where(value < 0.0, -root, root)
    head = root[:8, :128]
    head = jnp.where((row == 0) & (lane == 1), pick(head, 1, 0), head)
    return root, head


def final_kernel(code_ref, out_hbm, e_ref, l_ref, o_ref, out_sems):
    odd = is_odd()
    none = jnp.zeros(e_ref.shape[1:], F32)
    for ref in (e_ref, l_ref):
        ref[0] = none
        ref[17] = none

    def read(p, _):
        root, head = decode(code_ref[p])
        e_ref[p + 1] = root[:, :256]
        l_ref[p + 1] = root[:, 256:]
        e_ref[p + 1, pl.ds(0, 8), pl.ds(0, 128)] = head
        return 0

    read(0, 0)

    def put(p):
        return pltpu.make_async_copy(o_ref.at[p], out_hbm.at[p], out_sems.at[p])

    low = lax.broadcasted_iota(jnp.int32, (64, 128), 1) < 64

    def turned(tile):
        return jnp.transpose(jnp.concatenate([tile, tile], axis=0))[64:]

    def join(lower, upper):
        return jnp.where(low, lower, upper)

    def tiles(ref, p):
        return ref[p, :, pl.ds(0, 128)], ref[p, :, pl.ds(128, 128)]

    def ahead(p):
        read(jnp.minimum(p + 1, 15), 0)

    def even(p, _):
        ahead(p)
        e_one, e_two = tiles(e_ref, p + 1)
        (b_one, b_two), (l_one, _), (_, l_after) = [tiles(l_ref, p + i) for i in range(3)]
        o_ref[p, :, pl.ds(0, 512)] = side(
            [join(b_one, turned(b_one)), join(b_two, e_two), e_one, join(e_two, l_one)]
        )
        o_ref[p, :, pl.ds(512, 64)] = l_after[:, 64:]
        put(p).start()
        return 0

    def uneven(p, _):
        ahead(p)
        e_one, e_two = tiles(e_ref, p + 1)
        (_, b_two), (l_one, _), (a_one, a_two) = [tiles(l_ref, p + i) for i in range(3)]
        o_ref[p, :, pl.ds(0, 512)] = side(
            [
                join(e_two, l_one), join(pltpu.roll(b_two, 64, 1), e_two), e_one,
                join(a_one, turned(a_one)),
            ]
        )
        o_ref[p, :, pl.ds(512, 64)] = a_two[:, :64]
        put(p).start()
        return 0

    @pl.when(jnp.logical_not(odd))
    def _():
        lax.fori_loop(0, 16, even, 0, unroll=2)

    @pl.when(odd)
    def _():
        lax.fori_loop(0, 16, uneven, 0, unroll=2)

    for p in range(16):
        put(p).wait()


def any_spec():
    return pl.BlockSpec(memory_space=pl.ANY)


def vmem_spec():
    return pl.BlockSpec(memory_space=pltpu.VMEM)


def shape(*dims, dtype=F32):
    return jax.ShapeDtypeStruct(dims, dtype)


def call(kernel, out_shape, in_specs, out_specs, scratch, mib, name):
    return pl.pallas_call(
        kernel,
        out_shape=out_shape,
        in_specs=in_specs,
        out_specs=out_specs,
        scratch_shapes=scratch,
        compiler_params=pltpu.CompilerParams(vmem_limit_bytes=mib * MIB),
        cost_estimate=pl.CostEstimate(flops=1000, bytes_accessed=1000, transcendentals=0),
        name=name,
    )


def gate(values, others):
    count = len(values)
    return pl.pallas_call(
        gate_kernel,
        out_shape=[shape(*x.shape, dtype=x.dtype) for x in values],
        in_specs=[any_spec()] * (count + len(others)),
        out_specs=[any_spec()] * count,
        input_output_aliases={i: i for i in range(count)},
        compiler_params=pltpu.CompilerParams(vmem_limit_bytes=MIB),
        name="gate",
    )(*values, *others)


def coef_columns(centre, coupling, volume):
    own = jnp.stack([centre, coupling, volume], axis=1)
    up, down = neighbours(lax.axis_size("sx"))
    low = lax.ppermute(own[-2:], "sx", up)
    high = lax.ppermute(own[:2], "sx", down)
    return jnp.concatenate([low, own, high], axis=0)


def coef_edges(mid):
    up, down = neighbours(lax.axis_size("sy"))
    lo = lax.ppermute(mid[:, :, -2:], "sy", up)
    hi = lax.ppermute(mid[:, :, :2], "sy", down)
    return lo, hi


def local(modes, centre, coupling, volume):
    ext = modes.shape[0]
    nx = lax.axis_size("sx")
    ny = lax.axis_size("sy")
    mid = coef_columns(centre, coupling, volume)
    m = jnp.transpose(modes, (0, 1, 3, 2, 4))
    frame = ext + 2

    main, corner, south, north = call(
        pack_kernel,
        [
            shape(3 * ext + 1, 3, 64, 128, dtype=BF16),
            shape(3, 3, 3, 64, 128, dtype=BF16),
            shape(ext, 3, 3, 64, 128, dtype=BF16),
            shape(ext, 3, 3, 64, 128, dtype=BF16),
        ],
        [vmem_spec()],
        [vmem_spec()] * 4,
        [pltpu.SemaphoreType.DMA((7,))],
        8,
        "pack",
    )(m)
    main, corner, south, north, mid = gate((main, corner, south, north, mid), ())
    main_pairs, other_pairs = [], []
    for y in range(ny):
        for x in range(nx):
            lower, higher = x * ny + y, (x + 1) % nx * ny + y
            main_pairs.append((higher, lower) if y % 2 == 0 else (lower, higher))
            other_pairs.append((lower, higher) if y % 2 == 0 else (higher, lower))
    main = lax.ppermute(main, ("sx", "sy"), main_pairs)
    corner = lax.ppermute(corner, ("sx", "sy"), other_pairs)
    lo, hi = coef_edges(mid)
    south, north = gate((south, north), (lo, hi))
    up, down = neighbours(ny)
    south = lax.ppermute(south, "sy", up)
    north = lax.ppermute(north, "sy", down)

    own, coef, img = call(
        own_kernel,
        [
            shape(64, 64),
            shape(frame, 6, frame, 128),
            shape(frame, frame * 3, 128, 128, dtype=BF16),
        ],
        [vmem_spec()] * 4,
        [vmem_spec()] * 3,
        [
            pltpu.VMEM((4, frame, 3, 64, 128), F32),
            pltpu.VMEM((64, 128), F32),
        ],
        OWN_MIB,
        "own_gram",
    )(m.reshape(ext, ext * 3, 64, 128), mid, lo, hi)
    around, cimg = call(
        rows_kernel,
        [shape(64, 128), shape(2, 2, 27, 128, 128, dtype=BF16)],
        [vmem_spec()] * 4,
        [vmem_spec(), vmem_spec()],
        [
            pltpu.VMEM((3, 3, 3, 3, 16, 128), F32),
            pltpu.VMEM((2, 128, 64), F32),
        ],
        8,
        "row_gram",
    )(south, north, img, coef)
    keep, turned = call(
        other_kernel,
        [shape(64, 64), shape(64, 64)],
        [vmem_spec()] * 2,
        [vmem_spec()] * 2,
        [],
        8,
        "corner_gram",
    )(corner, cimg)
    below = lax.ppermute(turned, "sy", up)
    code = call(
        main_kernel,
        shape(nx, 64, 512, dtype=BF16),
        [vmem_spec()] * 7,
        vmem_spec(),
        [],
        8,
        "column_gram",
    )(main, img, cimg, own, around, below, keep)
    code = lax.all_to_all(code, "sx", 0, 0)
    out = call(
        final_kernel,
        shape(nx, 64, 576),
        [vmem_spec()],
        any_spec(),
        [
            pltpu.VMEM((nx + 2, 64, 256), F32),
            pltpu.VMEM((nx + 2, 64, 256), F32),
            pltpu.VMEM((nx, 64, 576), F32),
            pltpu.SemaphoreType.DMA((nx,)),
        ],
        12,
        "assemble",
    )(code)
    return out[None]


def solution(mesh):
    in_specs = (
        P("sx", "sy", None, None, None),
        P("sx", "sy", None),
        P("sx", "sy", None),
        P("sx", "sy", None),
    )
    out_specs = P("sy", None, None, None)
    return jax.shard_map(local, mesh=mesh, in_specs=in_specs, out_specs=out_specs, check_vma=False)
```

```python
import functools

import jax
import jax.numpy as jnp
from jax import lax
from jax.experimental import pallas as pl
from jax.experimental.pallas import tpu as pltpu
from jax.sharding import PartitionSpec as P

F32 = jnp.float32
BF16 = jnp.bfloat16
MID, LOW, UPP, DIA, VOL, OUT = range(6)
NT = (((1,), (1,)), ((), ()))
MIB = 1024 * 1024
TOP = 1024.0
OWN_MIB = 10


def cover(local, index, cell, count, margin):
    places = index * cell + local
    base = index + (local >= cell).astype(jnp.int32) - (local < 0).astype(jnp.int32)
    total = jnp.zeros(local.shape, jnp.int32)
    for step_off in (-1, 0, 1):
        owner = base + step_off
        inside = (
            (owner >= 0)
            & (owner < count)
            & (places >= owner * cell - margin)
            & (places < owner * cell + cell + margin)
        )
        total = total + inside.astype(jnp.int32)
    in_grid = (places >= 0) & (places < cell * count)
    safe = jnp.maximum(total, 1).astype(F32)
    return jnp.where(in_grid & (total > 0), 1.0 / safe, 0.0)


def is_odd():
    return lax.rem(lax.axis_index("sy"), 2) == 1


def has_y(step):
    place = lax.axis_index("sy") + step
    return (place >= 0) & (place < lax.axis_size("sy"))


def has_x(main):
    step = jnp.where(is_odd() == main, -1, 1)
    place = lax.axis_index("sx") + step
    return (place >= 0) & (place < lax.axis_size("sx"))


def neighbours(count):
    up = [(i, (i + 1) % count) for i in range(count)]
    return up, [(b, a) for a, b in up]


def spread3(w):
    return [w[0], w[0] + w[0] + w[1], w[0] + w[1] + w[1] + w[2]]


def cell_image(lines, values, rows):
    if values is None:
        return [-(rows[2] * lines[a]) for a in range(3)]
    total = rows[1] * (values[0] + values[1] + values[2])
    return [rows[0] * values[a] + total - rows[2] * lines[a] for a in range(3)]


def coef_rows(coef_ref, x, y, names):
    return [coef_ref[x, n, pl.ds(y, 1), :] for n in names]


def depth_sum(raw, rows):
    return (
        raw.astype(F32) * rows[0]
        + pltpu.roll(raw, 1, 1).astype(F32) * rows[1]
        + pltpu.roll(raw, 127, 1).astype(F32) * rows[2]
    )


def side(blocks):
    return jnp.concatenate(blocks, axis=1)


def fold(total):
    return total[:, :64] + total[:, 64:]


def fold_rows(total):
    return total[:64] + total[64:]


def pack_kernel(m_hbm, flat_hbm, main_ref, corner_ref, south_ref, north_ref, sems):
    ext = m_hbm.shape[0]
    here = jnp.where(is_odd(), ext - 3, 0)
    there = jnp.where(is_odd(), 0, ext - 3)
    copies = [
        pltpu.make_async_copy(
            flat_hbm.at[pl.ds(here * ext, 3 * ext)], main_ref.at[pl.ds(0, 3 * ext)], sems.at[0]
        )
    ]
    main_ref[3 * ext] = jnp.zeros(main_ref.shape[1:], BF16)
    copies += [
        pltpu.make_async_copy(
            m_hbm.at[pl.ds(there, 3), pl.ds(ext - 3, 3)], corner_ref, sems.at[1]
        ),
        pltpu.make_async_copy(m_hbm.at[:, pl.ds(ext - 3, 3)], south_ref, sems.at[2]),
        pltpu.make_async_copy(m_hbm.at[:, pl.ds(0, 3)], north_ref, sems.at[3]),
    ]
    for copy in copies:
        copy.start()
    for copy in copies:
        copy.wait()


def gate_kernel(*refs):
    pass


def own_kernel(
    m_ref, mid_ref, lo_ref, hi_ref,
    out_ref, coef_ref, img_ref, q_ref, acc_ref,
):
    ext = m_ref.shape[0]
    frame = ext + 2
    cell = mid_ref.shape[2]
    margin = (ext - cell) // 2
    odd = is_odd()

    q_ref[0] = jnp.zeros(q_ref.shape[1:], F32)
    lane = lax.broadcasted_iota(jnp.int32, (frame, 128), 1)
    place = lax.broadcasted_iota(jnp.int32, (frame, 128), 0)
    share_y = cover(
        place - margin - 1, lax.axis_index("sy"), cell, lax.axis_size("sy"), margin
    )

    def coefs(f, _):
        at = jnp.zeros((1, 128), jnp.int32) + (f - margin - 1)
        share = share_y * cover(at, lax.axis_index("sx"), cell, lax.axis_size("sx"), margin)
        cen, cpl, vol = [
            jnp.concatenate([lo_ref[f, n], mid_ref[f, n], hi_ref[f, n]], axis=0) for n in range(3)
        ]
        kap = cpl * share
        vol = vol * share * share
        coef_ref[f, MID] = kap + kap
        coef_ref[f, LOW] = jnp.where(lane == 0, 0.0, pltpu.roll(kap, 1, 1))
        coef_ref[f, UPP] = jnp.where(lane == 127, 0.0, pltpu.roll(kap, 127, 1))
        coef_ref[f, DIA] = cen * share * share - vol + 0.5 * kap * kap
        coef_ref[f, VOL] = vol
        coef_ref[f, OUT] = kap * (1.0 / 16.0)
        return 0

    lax.fori_loop(0, frame, coefs, 0, unroll=4)

    def first(f, chunk):
        rows = pl.ds(pl.multiple_of(chunk * 16, 16), 16)
        kaps = [coef_rows(coef_ref, f, g, (MID, LOW, UPP)) for g in range(1, ext + 1)]
        slot = f & 3
        for a in range(3):
            before = pair = None
            for j in range(ext):
                w = depth_sum(m_ref[f - 1, j * 3 + a, rows, :], kaps[j])
                if j == 0:
                    q_ref[slot, 0, a, rows, :] = w
                    pair = w
                else:
                    now = before + w
                    q_ref[slot, j, a, rows, :] = now + pair
                    pair = now
                before = w
            q_ref[slot, ext, a, rows, :] = pair + before
            q_ref[slot, ext + 1, a, rows, :] = before

    def image(f, chunk, edge=None, last=False):
        rows = pl.ds(pl.multiple_of(chunk * 16, 16), 16)
        low_rows = pl.ds(pl.multiple_of(64 + chunk * 16, 16), 16)
        for g in range(frame) if edge is None else range(1, ext + 1):
            values = None
            if 1 <= g <= ext and edge is None:
                values = [m_ref[f - 1, (g - 1) * 3 + a, rows, :].astype(F32) for a in range(3)]
            lines = []
            for a in range(3):
                if edge is not None:
                    lines.append(q_ref[edge & 3, g, a, rows, :])
                    continue
                mid = q_ref[f & 3, g, a, rows, :]
                one = q_ref[(f - 1) & 3, g, a, rows, :] + mid
                lines.append(one + (mid if last else mid + q_ref[(f + 1) & 3, g, a, rows, :]))
            result = cell_image(lines, values, coef_rows(coef_ref, f, g, (DIA, VOL, OUT)))
            for a in range(3):
                high = result[a].astype(BF16)
                img_ref[f, g * 3 + a, rows, :] = high
                img_ref[f, g * 3 + a, low_rows, :] = (result[a] - high.astype(F32)).astype(BF16)

    def dot(f, chunk):
        base = jnp.minimum(chunk * 8, ext * 3 - 8)
        tiles = [m_ref[jnp.maximum(f - 1, 0), base + i] for i in range(8)]
        for i in range(2):
            tiles[i] = jnp.where(chunk == 3, jnp.zeros_like(tiles[i]), tiles[i])
        lines = side([img_ref[f, base + 3 + i] for i in range(8)])
        acc_ref[...] += lax.dot_general(side(tiles), lines, NT, preferred_element_type=F32)

    def chunks(body):
        def step(chunk, _):
            body(chunk)
            return 0

        lax.fori_loop(0, 4, step, 0, unroll=4)

    chunks(lambda chunk: first(1, chunk))

    @pl.when(odd)
    def _():
        chunks(lambda chunk: image(0, chunk, 1))

    def inner(f, chunk):
        dot(f - 1, chunk)
        first(f + 1, chunk)
        image(f, chunk)

    def line(f, _):
        chunks(lambda chunk: inner(f, chunk))

        @pl.when(f == 1)
        def _():
            acc_ref[...] = jnp.zeros_like(acc_ref)

        return 0

    lax.fori_loop(1, ext, line, 0)

    def inner_last(chunk):
        dot(ext - 1, chunk)
        image(ext, chunk, None, True)

    chunks(inner_last)
    @pl.when(odd)
    def _():
        chunks(lambda chunk: dot(ext, chunk))

    @pl.when(jnp.logical_not(odd))
    def _():
        def inner_rim(chunk):
            dot(ext, chunk)
            image(ext + 1, chunk, ext)

        chunks(inner_rim)

    out_ref[...] = fold(acc_ref[...])


def rows_kernel(
    south_ref, north_ref, img_ref, coef_ref, out_ref, cimg_ref, z_ref, acc_ref
):
    ext = south_ref.shape[0]
    raw_refs = (south_ref, north_ref)
    acc_ref[...] = jnp.zeros_like(acc_ref)

    def dots(x):
        for s in range(2):
            right = side([raw_refs[s][x, j, a] for j in range(3) for a in range(3)])
            lines = side([img_ref[x + 1, s * (ext - 1) * 3 + i] for i in range(9)])
            acc_ref[s] += lax.dot_general(lines, right, NT, preferred_element_type=F32)

    def corner(s, t, chunk, use):
        raw_y = (2, 1, 0) if s == 0 else (0, 1, 2)
        raw_g = (2, 1, 0) if s == 0 else (9, 10, 11)
        img_g = (3, 2, 1) if s == 0 else (8, 9, 10)
        img_y = (2, 1, 0) if s == 0 else (0, 1, 2)
        raw_x = [c + t * (ext - 1 - 2 * c) for c in range(3)]
        raw_f = [1 + c + t * (ext - 1 - 2 * c) for c in range(3)]
        img_f = [c + t * (ext + 1 - 2 * c) for c in range(3)]
        img_x = [c + t * (2 - 2 * c) for c in range(3)]
        rows = pl.ds(pl.multiple_of(chunk * 16, 16), 16)
        low_rows = pl.ds(pl.multiple_of(64 + chunk * 16, 16), 16)
        for a in range(3):
            across = []
            for c in range(3):
                w = [
                    depth_sum(
                        raw_refs[s][raw_x[c], raw_y[d], a, rows, :],
                        coef_rows(coef_ref, raw_f[c], raw_g[d], (MID, LOW, UPP)),
                    )
                    for d in range(3)
                ]
                across.append(spread3(w))
            for e in range(3):
                for c, value in enumerate(spread3([across[i][e] for i in range(3)])):
                    z_ref[use, c, e, a] = value
        for c in range(3):
            for e in range(3):
                values = None
                if c > 0 and e > 0:
                    values = [
                        raw_refs[s][raw_x[c - 1], raw_y[e - 1], a, rows, :].astype(F32)
                        for a in range(3)
                    ]
                image = cell_image(
                    [z_ref[use, c, e, a] for a in range(3)], values,
                    coef_rows(coef_ref, img_f[c], img_g[e], (DIA, VOL, OUT)),
                )
                for a in range(3):
                    tile = (img_x[c] * 3 + img_y[e]) * 3 + a
                    high = image[a].astype(BF16)
                    cimg_ref[t, s, tile, rows, :] = high
                    cimg_ref[t, s, tile, low_rows, :] = (image[a] - high.astype(F32)).astype(BF16)

    main_side = 1 - is_odd().astype(jnp.int32)

    def step(chunk, _):
        dots(2 * chunk)
        dots(2 * chunk + 1)
        corner(0, main_side, chunk, 0)
        corner(1, 0, chunk, 1)
        corner(1, 1, chunk, 2)
        return 0

    lax.fori_loop(0, 4, step, 0, unroll=2)
    for x in range(8, ext):
        dots(x)
    out_ref[...] = side([fold_rows(acc_ref[0]), fold_rows(acc_ref[1])])


def masked(there, block):
    return jnp.where(there, block, jnp.zeros_like(block))


def corner_dot(raw, img):
    left = side([raw(i, j, a) for i in range(3) for j in range(3) for a in range(3)])
    lines = side([img(i) for i in range(27)])
    return fold(lax.dot_general(left, lines, NT, preferred_element_type=F32))


def other_kernel(corner_ref, cimg_ref, keep_ref, turned_ref):
    t = is_odd().astype(jnp.int32)
    there = has_y(1) & has_x(False)
    cells = [(i, j, a) for i in range(3) for j in range(3) for a in range(3)]
    raw = side([corner_ref[c] for c in cells])
    lines = side([cimg_ref[t, 1, i] for i in range(27)])
    keep_ref[...] = masked(there, fold(lax.dot_general(raw, lines, NT, preferred_element_type=F32)))
    turned_ref[...] = masked(
        there, fold_rows(lax.dot_general(lines, raw, NT, preferred_element_type=F32))
    )


def main_kernel(main_ref, img_ref, cimg_ref, own_ref, rows_ref, below_ref, keep_ref, out_ref):
    t = 1 - is_odd().astype(jnp.int32)
    ext = main_ref.shape[0] // 3
    start = jnp.where(is_odd(), 0, ext - 1)
    total = None
    for i in range(3):
        right = side([main_ref[i * ext + j, a] for j in range(ext) for a in range(3)])
        lines = side([img_ref[start + i, 3 + j] for j in range(ext * 3)])
        part = lax.dot_general(lines, right, NT, preferred_element_type=F32)
        total = part if total is None else total + part
    south = corner_dot(lambda i, j, a: main_ref[i * ext + j, a], lambda i: cimg_ref[t, 0, i])
    north = corner_dot(lambda i, j, a: main_ref[i * ext + ext - 3 + j, a], lambda i: cimg_ref[t, 1, i])
    low, high, beside = has_y(-1), has_y(1), has_x(True)
    around = rows_ref[...]
    blocks = [
        own_ref[...], masked(high, around[:, 64:]), below_ref[...], masked(low, around[:, :64]),
        masked(low & beside, south), masked(beside, fold_rows(total)),
        masked(high & beside, north), keep_ref[...],
    ]
    code = encode(side(blocks))
    for p in range(out_ref.shape[0]):
        out_ref[p] = code


def encode(rows):
    top = jnp.max(jnp.abs(rows), axis=(0, 1), keepdims=True)
    top = jnp.where(top > 0.0, jnp.maximum(top * 1.01, 2.0**-100), 1.0).astype(BF16).astype(F32)
    value = rows * (TOP / top)
    value2 = value * value
    value4 = value2 * value2
    power = value4 * value4 * value4
    code = jnp.where(rows < 0.0, -power, power)
    row = lax.broadcasted_iota(jnp.int32, rows.shape, 0)
    lane = lax.broadcasted_iota(jnp.int32, rows.shape, 1)
    return jnp.where((row == 0) & (lane == 1), top, code).astype(BF16)


def decode(code):
    value = code.astype(F32)
    first = value[:8, :128]
    row = lax.broadcasted_iota(jnp.int32, first.shape, 0)
    lane = lax.broadcasted_iota(jnp.int32, first.shape, 1)

    def pick(tile, i, j):
        return jnp.sum(jnp.where((row == i) & (lane == j), tile, 0.0), axis=(0, 1), keepdims=True)

    scale = pick(first, 0, 1) * (1.0 / TOP)
    root = jnp.exp(jnp.log(jnp.abs(value)) * (1.0 / 12.0)) * scale
    root = jnp.where(value < 0.0, -root, root)
    head = root[:8, :128]
    head = jnp.where((row == 0) & (lane == 1), pick(head, 1, 0), head)
    return root, head


def final_kernel(code_ref, out_hbm, e_ref, l_ref, o_ref, out_sems):
    odd = is_odd()
    none = jnp.zeros(e_ref.shape[1:], F32)
    for ref in (e_ref, l_ref):
        ref[0] = none
        ref[17] = none

    def read(p, _):
        root, head = decode(code_ref[p])
        e_ref[p + 1] = root[:, :256]
        l_ref[p + 1] = root[:, 256:]
        e_ref[p + 1, pl.ds(0, 8), pl.ds(0, 128)] = head
        return 0

    read(0, 0)

    def put(p):
        return pltpu.make_async_copy(o_ref.at[p], out_hbm.at[p], out_sems.at[p])

    low = lax.broadcasted_iota(jnp.int32, (64, 128), 1) < 64

    def turned(tile):
        return jnp.transpose(jnp.concatenate([tile, tile], axis=0))[64:]

    def join(lower, upper):
        return jnp.where(low, lower, upper)

    def tiles(ref, p):
        return ref[p, :, pl.ds(0, 128)], ref[p, :, pl.ds(128, 128)]

    def ahead(p):
        read(jnp.minimum(p + 1, 15), 0)

    def even(p, _):
        ahead(p)
        e_one, e_two = tiles(e_ref, p + 1)
        (b_one, b_two), (l_one, _), (_, l_after) = [tiles(l_ref, p + i) for i in range(3)]
        o_ref[p, :, pl.ds(0, 512)] = side(
            [join(b_one, turned(b_one)), join(b_two, e_two), e_one, join(e_two, l_one)]
        )
        o_ref[p, :, pl.ds(512, 64)] = l_after[:, 64:]
        put(p).start()
        return 0

    def uneven(p, _):
        ahead(p)
        e_one, e_two = tiles(e_ref, p + 1)
        (_, b_two), (l_one, _), (a_one, a_two) = [tiles(l_ref, p + i) for i in range(3)]
        o_ref[p, :, pl.ds(0, 512)] = side(
            [
                join(e_two, l_one), join(pltpu.roll(b_two, 64, 1), e_two), e_one,
                join(a_one, turned(a_one)),
            ]
        )
        o_ref[p, :, pl.ds(512, 64)] = a_two[:, :64]
        put(p).start()
        return 0

    @pl.when(jnp.logical_not(odd))
    def _():
        lax.fori_loop(0, 16, even, 0, unroll=2)

    @pl.when(odd)
    def _():
        lax.fori_loop(0, 16, uneven, 0, unroll=2)

    for p in range(16):
        put(p).wait()


def any_spec():
    return pl.BlockSpec(memory_space=pl.ANY)


def vmem_spec():
    return pl.BlockSpec(memory_space=pltpu.VMEM)


def shape(*dims, dtype=F32):
    return jax.ShapeDtypeStruct(dims, dtype)


def call(kernel, out_shape, in_specs, out_specs, scratch, mib, name):
    return pl.pallas_call(
        kernel,
        out_shape=out_shape,
        in_specs=in_specs,
        out_specs=out_specs,
        scratch_shapes=scratch,
        compiler_params=pltpu.CompilerParams(vmem_limit_bytes=mib * MIB),
        cost_estimate=pl.CostEstimate(flops=1000, bytes_accessed=1000, transcendentals=0),
        name=name,
    )


def gate(values, others):
    count = len(values)
    return pl.pallas_call(
        gate_kernel,
        out_shape=[shape(*x.shape, dtype=x.dtype) for x in values],
        in_specs=[any_spec()] * (count + len(others)),
        out_specs=[any_spec()] * count,
        input_output_aliases={i: i for i in range(count)},
        compiler_params=pltpu.CompilerParams(vmem_limit_bytes=MIB),
        name="gate",
    )(*values, *others)


def coef_columns(centre, coupling, volume):
    own = jnp.stack([centre, coupling, volume], axis=1)
    up, down = neighbours(lax.axis_size("sx"))
    low = lax.ppermute(own[-2:], "sx", up)
    high = lax.ppermute(own[:2], "sx", down)
    return jnp.concatenate([low, own, high], axis=0)


def coef_edges(mid):
    up, down = neighbours(lax.axis_size("sy"))
    lo = lax.ppermute(mid[:, :, -2:], "sy", up)
    hi = lax.ppermute(mid[:, :, :2], "sy", down)
    return lo, hi


def local(modes, centre, coupling, volume):
    ext = modes.shape[0]
    nx = lax.axis_size("sx")
    ny = lax.axis_size("sy")
    mid = coef_columns(centre, coupling, volume)
    m = jnp.transpose(modes, (0, 1, 3, 2, 4))
    frame = ext + 2

    main, corner, south, north = call(
        pack_kernel,
        [
            shape(3 * ext + 1, 3, 64, 128, dtype=BF16),
            shape(3, 3, 3, 64, 128, dtype=BF16),
            shape(ext, 3, 3, 64, 128, dtype=BF16),
            shape(ext, 3, 3, 64, 128, dtype=BF16),
        ],
        [vmem_spec()] * 2,
        [vmem_spec()] * 4,
        [pltpu.SemaphoreType.DMA((4,))],
        8,
        "pack",
    )(m, m.reshape(ext * ext, 3, 64, 128))
    main, corner, south, north, mid = gate((main, corner, south, north, mid), ())
    main_pairs, other_pairs = [], []
    for y in range(ny):
        for x in range(nx):
            lower, higher = x * ny + y, (x + 1) % nx * ny + y
            main_pairs.append((higher, lower) if y % 2 == 0 else (lower, higher))
            other_pairs.append((lower, higher) if y % 2 == 0 else (higher, lower))
    main = lax.ppermute(main, ("sx", "sy"), main_pairs)
    corner = lax.ppermute(corner, ("sx", "sy"), other_pairs)
    lo, hi = coef_edges(mid)
    south, north = gate((south, north), (lo, hi))
    up, down = neighbours(ny)
    south = lax.ppermute(south, "sy", up)
    north = lax.ppermute(north, "sy", down)

    own, coef, img = call(
        own_kernel,
        [
            shape(64, 64),
            shape(frame, 6, frame, 128),
            shape(frame, frame * 3, 128, 128, dtype=BF16),
        ],
        [vmem_spec()] * 4,
        [vmem_spec()] * 3,
        [
            pltpu.VMEM((4, frame, 3, 64, 128), F32),
            pltpu.VMEM((64, 128), F32),
        ],
        OWN_MIB,
        "own_gram",
    )(m.reshape(ext, ext * 3, 64, 128), mid, lo, hi)
    around, cimg = call(
        rows_kernel,
        [shape(64, 128), shape(2, 2, 27, 128, 128, dtype=BF16)],
        [vmem_spec()] * 4,
        [vmem_spec(), vmem_spec()],
        [
            pltpu.VMEM((3, 3, 3, 3, 16, 128), F32),
            pltpu.VMEM((2, 128, 64), F32),
        ],
        8,
        "row_gram",
    )(south, north, img, coef)
    keep, turned = call(
        other_kernel,
        [shape(64, 64), shape(64, 64)],
        [vmem_spec()] * 2,
        [vmem_spec()] * 2,
        [],
        8,
        "corner_gram",
    )(corner, cimg)
    below = lax.ppermute(turned, "sy", up)
    code = call(
        main_kernel,
        shape(nx, 64, 512, dtype=BF16),
        [vmem_spec()] * 7,
        vmem_spec(),
        [],
        8,
        "column_gram",
    )(main, img, cimg, own, around, below, keep)
    code = lax.all_to_all(code, "sx", 0, 0)
    out = call(
        final_kernel,
        shape(nx, 64, 576),
        [vmem_spec()],
        any_spec(),
        [
            pltpu.VMEM((nx + 2, 64, 256), F32),
            pltpu.VMEM((nx + 2, 64, 256), F32),
            pltpu.VMEM((nx, 64, 576), F32),
            pltpu.SemaphoreType.DMA((nx,)),
        ],
        12,
        "assemble",
    )(code)
    return out[None]


def solution(mesh):
    in_specs = (
        P("sx", "sy", None, None, None),
        P("sx", "sy", None),
        P("sx", "sy", None),
        P("sx", "sy", None),
    )
    out_specs = P("sy", None, None, None)
    return jax.shard_map(local, mesh=mesh, in_specs=in_specs, out_specs=out_specs, check_vma=False)
```
